512 devices in a mesh: grp: 4 (over x), gx: 32 (over z, y_hi), gy: 4 (over y_lo, core).
Axes of the slice: x: 4, y: 8 (y_hi: 4, y_lo: 2; y = y_hi * 2 + y_lo), z: 8, core: 2. Of those that a mesh axis runs over, the one named last changes fastest.
Arguments:
- forcing: float32 [512, 64, 512], P('gx', 'gy', 'grp'), may hold values from -8 to 8
- kappa: float32 [512, 64, 512], P('gx', 'gy', 'grp'), may hold values from 0.5 to 8
Outputs:
- solution: float32 [512, 64, 512], P('gx', 'gy', 'grp')
- residual: float32 [512, 64, 512], P('gx', 'gy', 'grp')
The draws below stay inside these ranges and needn't reach their ends.
All inputs are finite; a program needn't handle non-finite values.
Results may differ from the reference program's by a relative error of at most 0.0001.
Values sent between devices are 32-bit elements; how exact they have to be, the bound alone decides.
No kernel may reach another device: no remote copies, remote signals or barrier semaphores. Data moves between devices by JAX's collectives and lax.ppermute only.
A program may use at most 64 MiB of HBM per device.

```python
import math
import jax
import jax.numpy as jnp

ITERS = 2
NX = 512
NY = 64
NZ = 512


def level_of(own_key, shape, cuts, smallest, largest):
    factor_of, own = 1.0, jax.random.fold_in(own_key, 6)
    for position, shards_of in cuts:
        draws = jnp.exp(jax.random.uniform(jax.random.fold_in(own, position), (shards_of,), jnp.float32, smallest / len(cuts), largest / len(cuts)))
        factor_of = factor_of * jnp.repeat(draws, shape[position] // shards_of).reshape([-1 if axis == position else 1 for axis in range(len(shape))])
    return factor_of


def normal_values(stream_key, dims, width, reach, cuts=(), kind=jnp.bfloat16):
    values = jax.random.normal(stream_key, dims, jnp.float32) * width
    if len(cuts) > 0:
        values = level_of(stream_key, dims, cuts, -0.22, 0.18) * values
    return jnp.clip(values, min=-reach, max=reach).astype(kind)


def setup_inputs(seed: int = 0) -> dict:
    keys = jax.random.split(jax.random.key(seed), 3)
    return {
        "forcing": normal_values(keys[0], (NX, NY, NZ), 1.0, 8.0, ((0, 32), (1, 4), (2, 4)), jnp.float32),
        "kappa": jnp.clip(jnp.exp(math.log(8.0) - 2.7725887 * jax.random.uniform(keys[1], (NX, NY, NZ), jnp.float32) ** level_of(keys[1], (NX, NY, NZ), ((0, 32), (1, 4), (2, 4)), -0.2, 0.2)), 0.5, 8.0),
    }


def smooth_sum(padded):
    first = 0.5 * padded[:-2] + padded[1:-1] + 0.5 * padded[2:]
    second = 0.5 * first[:, :-2] + first[:, 1:-1] + 0.5 * first[:, 2:]
    return 0.5 * second[:, :, :-2] + second[:, :, 1:-1] + 0.5 * second[:, :, 2:]


def stencil(padded, coef):
    inner = padded[1:-1, 1:-1, 1:-1]
    return coef * (16.0 * inner - 2.0 * smooth_sum(padded)) + inner


def sweeps(rhs, coef):
    diag = 14.0 * coef + 1.0
    error = 0.8 * rhs / diag
    for sweep in range(2):
        error = error + 0.8 * (rhs - stencil(jnp.pad(error, 1), coef)) / diag
    return error


def restrict(field):
    sx, sy, sz = field.shape
    return field.reshape(sx // 2, 2, sy // 2, 2, sz // 2, 2).mean(axis=(1, 3, 5))


def prolong(field):
    return jnp.repeat(jnp.repeat(jnp.repeat(field, 2, axis=0), 2, axis=1), 2, axis=2)


def reference(forcing, kappa):
    kappa2 = restrict(kappa)
    kappa3 = restrict(kappa2)
    coef2 = kappa2 * 0.25
    coef3 = kappa3 * 0.0625
    solution = jnp.zeros_like(forcing)
    for step in range(ITERS):
        resid = forcing - stencil(jnp.pad(solution, 1), kappa)
        second = restrict(resid)
        third = restrict(second)
        error1 = sweeps(resid, kappa)
        error2 = sweeps(second, coef2)
        error3 = sweeps(third, coef3)
        solution = solution + error1 + prolong(error2 + prolong(error3))
    residual = forcing - stencil(jnp.pad(solution, 1), kappa)
    return solution, residual
```

```python
import jax
import jax.numpy as jnp
from jax import lax
from jax.experimental import pallas as pl
from jax.experimental.pallas import tpu as pltpu
from jax.sharding import PartitionSpec as P

F32 = jnp.float32
LANES = 128
HALO = 3
N = (16, 8, 4)
X = tuple(n + 2 * HALO for n in N)
RING = (24, 16, 16)
STEP = (1, 2, 4)
OWN = tuple(2 * n for n in N)
WIDE = tuple(2 * r for r in RING)
OBASE = (0, 512, 640)
OROWS = 672
XBASE = (0, 96, 144)
XROWS = 168
YBASE = (0, 132, 216)
YROWS = 280
WBASE = (0, 1056, 1504)
WROWS = 1824
SOLROWS = 18 * 48
VMEM_LIMIT = 48 * 1024 * 1024


def lanes_of(rows):
    return lax.broadcasted_iota(jnp.int32, (rows, LANES), 1)


def call(kernel, outs, scratch, *args):
    return pl.pallas_call(
        kernel,
        out_shape=[jax.ShapeDtypeStruct((rows, LANES), F32) for rows in outs],
        in_specs=[pl.BlockSpec(memory_space=pltpu.VMEM)] * len(args),
        out_specs=[pl.BlockSpec(memory_space=pltpu.VMEM)] * len(outs),
        scratch_shapes=[pltpu.VMEM((rows, LANES), F32) for rows in scratch],
        compiler_params=pltpu.CompilerParams(vmem_limit_bytes=VMEM_LIMIT),
    )(*args)


def z_faces(f_ref, k_ref, up_ref, down_ref):
    quarter = lanes_of(16) // 32
    for field, ref in enumerate((f_ref, k_ref)):
        for g in range(4):
            slabs = [ref[pl.ds(16 * (4 * g + m), 16), :] for m in range(4)]
            up = pltpu.roll(slabs[0], 32, 1)
            down = slabs[0]
            for m in range(1, 4):
                shift = 32 * (m + 1) % LANES
                moved = pltpu.roll(slabs[m], shift, 1) if shift else slabs[m]
                up = jnp.where(quarter == m, moved, up)
                down = jnp.where(quarter == m, pltpu.roll(slabs[m], 32 * m, 1), down)
            at = pl.ds(64 * field + 16 * g, 16)
            up_ref[at, :] = up
            down_ref[at, :] = down


def coarsen(ref, level, base, tmp, scale):
    rows = OWN[level]
    half = rows // 2
    bit = STEP[level]
    even = (lanes_of(half) // bit) % 2 == 0
    for a in range(N[level] // 2):
        at = base + OBASE[level] + 2 * a * rows
        tmp[pl.ds(a * rows, rows), :] = ref[pl.ds(at, rows), :] + ref[pl.ds(at + rows, rows), :]
    for a in range(N[level] // 2):
        pair = tmp[pl.ds(a * rows, half, 2), :] + tmp[pl.ds(a * rows + 1, half, 2), :]
        other = jnp.where(even, pltpu.roll(pair, LANES - bit, 1), pltpu.roll(pair, bit, 1))
        ref[pl.ds(base + OBASE[level + 1] + a * half, half), :] = (pair + other) * scale


def x_faces(own_ref, base, up_ref, down_ref, xbase):
    for level in range(3):
        rows = HALO * OWN[level]
        first = base + OBASE[level]
        last = first + (N[level] - HALO) * OWN[level]
        up_ref[pl.ds(xbase + XBASE[level], rows), :] = own_ref[pl.ds(last, rows), :]
        down_ref[pl.ds(xbase + XBASE[level], rows), :] = own_ref[pl.ds(first, rows), :]


def begin(f_ref, k_ref, zl_ref, zr_ref, own_ref, up_ref, down_ref, tmp):
    low = lanes_of(16) < 64
    for field, ref in enumerate((f_ref, k_ref)):
        base = field * OROWS
        for g in range(4):
            at = pl.ds(64 * field + 16 * g, 16)
            left, right = zl_ref[at, :], zr_ref[at, :]
            for m in range(4):
                slab = 4 * g + m
                shift_l, shift_r = (96 - 32 * m) % LANES, (-32 * m) % LANES
                from_l = pltpu.roll(left, shift_l, 1) if shift_l else left
                from_r = pltpu.roll(right, shift_r, 1) if shift_r else right
                own_ref[pl.ds(base + 32 * slab, 16), :] = ref[pl.ds(16 * slab, 16), :]
                own_ref[pl.ds(base + 32 * slab + 16, 16), :] = jnp.where(low, from_r, from_l)
        scale = 0.125 if field == 0 else 0.125 * 0.25
        coarsen(own_ref, 0, base, tmp, scale)
        coarsen(own_ref, 1, base, tmp, scale)
        x_faces(own_ref, base, up_ref, down_ref, field * XROWS)


def y_faces(fields, own_ref, xl_ref, xr_ref, up_ref, down_ref):
    for field in range(fields):
        ob, xb, yb = field * OROWS, field * XROWS, field * YROWS
        for dst, first in ((up_ref, False), (down_ref, True)):
            for level in range(3):
                n, rows = N[level], OWN[level]
                for h in range(2):
                    for j in range(HALO):
                        row = h * n + (j if first else n - HALO + j)
                        off = yb + YBASE[level] + (h * HALO + j) * X[level]
                        dst[pl.ds(off, HALO), :] = xl_ref[pl.ds(xb + XBASE[level] + row, HALO, rows), :]
                        dst[pl.ds(off + HALO, n), :] = own_ref[pl.ds(ob + OBASE[level] + row, n, rows), :]
                        dst[pl.ds(off + HALO + n, HALO), :] = xr_ref[pl.ds(xb + XBASE[level] + row, HALO, rows), :]
            dst[pl.ds(yb + 276, 4), :] = jnp.zeros((4, LANES), F32)


def widen(field, own_ref, xl_ref, xr_ref, yl_ref, yr_ref, wide_ref):
    ob, xb, yb = field * OROWS, field * XROWS, field * YROWS
    for level in range(3):
        n, ring, rows = N[level], RING[level], OWN[level]
        for i in range(X[level]):
            if i < HALO:
                ref, at = xl_ref, xb + XBASE[level] + i * rows
            elif i < HALO + n:
                ref, at = own_ref, ob + OBASE[level] + (i - HALO) * rows
            else:
                ref, at = xr_ref, xb + XBASE[level] + (i - HALO - n) * rows
            for h in range(2):
                to = WBASE[level] + i * WIDE[level] + h * ring
                wide_ref[pl.ds(to, n), :] = ref[pl.ds(at + h * n, n), :]
                wide_ref[pl.ds(to + n, ring - n), :] = jnp.zeros((ring - n, LANES), F32)
        for h in range(2):
            for j in range(HALO):
                off = yb + YBASE[level] + (h * HALO + j) * X[level]
                to = WBASE[level] + h * ring
                wide_ref[pl.ds(to + n + j, X[level], WIDE[level]), :] = yr_ref[pl.ds(off, X[level]), :]
                wide_ref[pl.ds(to + ring - HALO + j, X[level], WIDE[level]), :] = yl_ref[pl.ds(off, X[level]), :]


def slab(ref, base, i, rows):
    return ref[pl.ds(pl.multiple_of(base + i * rows, 8), rows), :]


def put(ref, base, i, rows, value):
    ref[pl.ds(pl.multiple_of(base + i * rows, 8), rows), :] = value


def loop(low, high, body, unroll):
    for lead in range(low, low + (high - low) % unroll):
        body(lead)
    low += (high - low) % unroll

    def step(k, carry):
        for u in range(unroll):
            body(low + k * unroll + u)
        return carry

    if high > low:
        lax.fori_loop(0, (high - low) // unroll, step, 0)


def ring_sum(ref, base, i, ring, step):
    rows = 2 * ring
    mid = slab(ref, base, i, rows)
    total = slab(ref, base, i - 1, rows) + slab(ref, base, i + 1, rows) + (mid + mid)
    halves = []
    for h in range(2):
        t = total[h * ring : (h + 1) * ring]
        t = t + pltpu.roll(t, 1, 0)
        halves.append(t + pltpu.roll(t, ring - 1, 0))
    lane = lanes_of(ring)
    a, b = halves
    ra, rb = pltpu.roll(a, step, 1), pltpu.roll(b, step, 1)
    edge = lane < step
    a, b = a + jnp.where(edge, rb, ra), b + jnp.where(edge, ra, rb)
    ra, rb = pltpu.roll(a, LANES - step, 1), pltpu.roll(b, LANES - step, 1)
    edge = lane >= LANES - step
    a, b = a + jnp.where(edge, rb, ra), b + jnp.where(edge, ra, rb)
    return mid, a, b


def join(a, b):
    return jnp.concatenate([a, b], axis=0)


def coefficients(wide_k, cw, ca, cg):
    for level in range(3):
        rows, base = WIDE[level], WBASE[level]

        def body(i):
            c = slab(wide_k, base, i, rows)
            w = 0.8 / (14.0 * c + 1.0)
            put(cw, base, i, rows, w)
            put(ca, base, i, rows, 1.0 - w * (16.0 * c + 1.0))
            put(cg, base, i, rows, 0.25 * (w * c))

        loop(0, X[level], body, 2)


def sweeps(wide_b, cw, ca, cg, first, second):
    for level in range(3):
        rows, base, ring, step = WIDE[level], WBASE[level], RING[level], STEP[level]

        def start(i):
            put(wide_b, base, i, rows, slab(cw, base, i, rows) * slab(wide_b, base, i, rows))

        loop(0, X[level], start, 2)

        def sweep(src, dst):
            def body(i):
                mid, a, b = ring_sum(src, base, i, ring, step)
                new = slab(ca, base, i, rows) * mid + slab(wide_b, base, i, rows) + slab(cg, base, i, rows) * join(a, b)
                put(dst, base, i, rows, new)

            return body

        loop(1, X[level] - 1, sweep(wide_b, first), 2)
        loop(2, X[level] - 2, sweep(first, second), 2)


def prolong(err, up3, up2):
    for q in range(6):
        for h in range(2):
            e3 = err[pl.ds(WBASE[2] + (q + 2) * 32 + h * 16, 16), :]
            to = q * 32 + h * 16
            up3[pl.ds(to, 5, 2), :] = e3[0:5]
            up3[pl.ds(to + 1, 5, 2), :] = e3[0:5]
            up3[pl.ds(to + 10, 4), :] = jnp.zeros((4, LANES), F32)
            up3[pl.ds(to + 14, 2), :] = jnp.broadcast_to(e3[15:16], (2, LANES))
    for a in range(10):
        for h in range(2):
            e2 = err[pl.ds(WBASE[1] + (a + 2) * 32 + h * 16, 16), :]
            e2 = e2 + up3[pl.ds(((a - 1) // 2 + 1) * 32 + h * 16, 16), :]
            to = a * 48 + h * 24
            up2[pl.ds(to, 9, 2), :] = e2[0:9]
            up2[pl.ds(to + 1, 9, 2), :] = e2[0:9]
            up2[pl.ds(to + 18, 4), :] = jnp.zeros((4, LANES), F32)
            up2[pl.ds(to + 22, 2), :] = jnp.broadcast_to(e2[15:16], (2, LANES))


def correct(err, up2, old_ref, sol_ref):
    for i in range(18):
        value = err[pl.ds((i + 2) * 48, 48), :] + up2[pl.ds(((i - 1) // 2 + 1) * 48, 48), :]
        if old_ref is not None:
            value = value + old_ref[pl.ds(i * 48, 48), :]
        sol_ref[pl.ds(i * 48, 48), :] = value


def first_round(
    own_ref, xl_ref, xr_ref, yl_ref, yr_ref,
    r_ref, up_ref, down_ref, sol_ref, cw, ca, cg,
    wide_b, wide_k, first, second, up3, up2, tmp,
):
    widen(0, own_ref, xl_ref, xr_ref, yl_ref, yr_ref, wide_b)
    widen(1, own_ref, xl_ref, xr_ref, yl_ref, yr_ref, wide_k)
    coefficients(wide_k, cw, ca, cg)
    sweeps(wide_b, cw, ca, cg, first, second)
    prolong(second, up3, up2)
    correct(second, up2, None, sol_ref)

    def resid(i):
        mid, a, b = ring_sum(sol_ref, 0, i + 1, 24, 1)
        for h, t in enumerate((a, b)):
            s = mid[h * 24 : h * 24 + 16]
            at = pl.ds(pl.multiple_of(i * 32 + h * 16, 16), 16)
            f = own_ref[at, :]
            k = own_ref[pl.ds(pl.multiple_of(OROWS + i * 32 + h * 16, 16), 16), :]
            r_ref[at, :] = f - (k * (16.0 * s - 0.25 * t[:16]) + s)

    loop(0, 16, resid, 2)
    coarsen(r_ref, 0, 0, tmp, 0.125)
    coarsen(r_ref, 1, 0, tmp, 0.125)
    x_faces(r_ref, 0, up_ref, down_ref, 0)


def second_round(
    f_ref, k_ref, own_ref, xl_ref, xr_ref, yl_ref, yr_ref, old_ref, cw, ca, cg,
    out_ref, resid_ref,
    wide_b, first, second, sol_ref, up3, up2,
):
    widen(0, own_ref, xl_ref, xr_ref, yl_ref, yr_ref, wide_b)
    sweeps(wide_b, cw, ca, cg, first, second)
    prolong(second, up3, up2)
    correct(second, up2, old_ref, sol_ref)

    def resid(i):
        mid, a, _ = ring_sum(sol_ref, 0, i + 1, 24, 1)
        s = mid[:16]
        at = pl.ds(pl.multiple_of(i * 16, 16), 16)
        out_ref[at, :] = s
        resid_ref[at, :] = f_ref[at, :] - (k_ref[at, :] * (16.0 * s - 0.25 * a[:16]) + s)

    loop(0, 16, resid, 2)


def swap(up, down, axis):
    size = lax.axis_size(axis)
    rising = [(i, i + 1) for i in range(size - 1)]
    falling = [(j, i) for i, j in rising]
    return lax.ppermute(up, axis, rising), lax.ppermute(down, axis, falling)


def shards(forcing, kappa):
    shape = forcing.shape
    f = forcing.reshape(256, LANES)
    k = kappa.reshape(256, LANES)
    zl, zr = swap(*call(z_faces, [128, 128], [], f, k), "grp")
    own, up, down = call(begin, [2 * OROWS, 2 * XROWS, 2 * XROWS], [256], f, k, zl, zr)
    xl, xr = swap(up, down, "gx")

    def faces(fields, own, xl, xr):
        def kernel(*refs):
            y_faces(fields, *refs)

        return call(kernel, [fields * YROWS] * 2, [], own, xl, xr)

    yl, yr = swap(*faces(2, own, xl, xr), "gy")
    r, up, down, sol, cw, ca, cg = call(
        first_round,
        [OROWS, XROWS, XROWS, SOLROWS, WROWS, WROWS, WROWS],
        [WROWS, WROWS, WROWS, WROWS, 192, 480, 256],
        own, xl, xr, yl, yr,
    )
    xl, xr = swap(up, down, "gx")
    yl, yr = swap(*faces(1, r, xl, xr), "gy")
    out, resid = call(
        second_round,
        [256, 256],
        [WROWS, WROWS, WROWS, SOLROWS, 192, 480],
        f, k, r, xl, xr, yl, yr, sol, cw, ca, cg,
    )
    return out.reshape(shape), resid.reshape(shape)


def solution(mesh):
    placed = (P("gx", "gy", "grp"), P("gx", "gy", "grp"))
    return jax.shard_map(shards, mesh=mesh, in_specs=placed, out_specs=placed, check_vma=False)
```

```python
import jax
import jax.numpy as jnp
from jax import lax
from jax.experimental import pallas as pl
from jax.experimental.pallas import tpu as pltpu
from jax.sharding import PartitionSpec as P

F32 = jnp.float32
LANES = 128
HALO = 3
N = (16, 8, 4)
X = tuple(n + 2 * HALO for n in N)
RING = (24, 16, 16)
STEP = (1, 2, 4)
OWN = tuple(2 * n for n in N)
WIDE = tuple(2 * r for r in RING)
OBASE = (0, 512, 640)
OROWS = 672
XBASE = (0, 96, 144)
XROWS = 168
YBASE = (0, 132, 216)
YROWS = 280
PACKED = 112
UNROLL = 8
WBASE = (0, 1056, 1504)
WROWS = 1824
SOLROWS = 18 * 48
VMEM_LIMIT = 48 * 1024 * 1024


def lanes_of(rows):
    return lax.broadcasted_iota(jnp.int32, (rows, LANES), 1)


VM = pl.BlockSpec(memory_space=pltpu.VMEM)
HBM = pl.BlockSpec(memory_space=pl.ANY)


def call(kernel, outs, scratch, *args, out_specs=None, copies=0):
    return pl.pallas_call(
        kernel,
        out_shape=[jax.ShapeDtypeStruct((rows, LANES), F32) for rows in outs],
        in_specs=[VM] * len(args),
        out_specs=out_specs or [VM] * len(outs),
        scratch_shapes=[pltpu.VMEM((rows, LANES), F32) for rows in scratch]
        + ([pltpu.SemaphoreType.DMA((copies,))] if copies else []),
        compiler_params=pltpu.CompilerParams(vmem_limit_bytes=VMEM_LIMIT),
    )(*args)


def z_faces(fk_ref, up_ref, down_ref):
    quarter = lanes_of(16) // 32
    for field, ref in enumerate((fk_ref.at[pl.ds(0, 256), :], fk_ref.at[pl.ds(256, 256), :])):
        for g in range(4):
            slabs = [ref[pl.ds(16 * (4 * g + m), 16), :] for m in range(4)]
            up = pltpu.roll(slabs[0], 32, 1)
            down = slabs[0]
            for m in range(1, 4):
                shift = 32 * (m + 1) % LANES
                moved = pltpu.roll(slabs[m], shift, 1) if shift else slabs[m]
                up = jnp.where(quarter == m, moved, up)
                down = jnp.where(quarter == m, pltpu.roll(slabs[m], 32 * m, 1), down)
            at = pl.ds(64 * field + 16 * g, 16)
            up_ref[at, :] = up
            down_ref[at, :] = down


def coarsen(ref, level, base, tmp, scale):
    rows = OWN[level]
    half = rows // 2
    bit = STEP[level]
    even = (lanes_of(half) // bit) % 2 == 0
    for a in range(N[level] // 2):
        at = base + OBASE[level] + 2 * a * rows
        tmp[pl.ds(a * rows, rows), :] = ref[pl.ds(at, rows), :] + ref[pl.ds(at + rows, rows), :]
    for a in range(N[level] // 2):
        pair = tmp[pl.ds(a * rows, half, 2), :] + tmp[pl.ds(a * rows + 1, half, 2), :]
        other = jnp.where(even, pltpu.roll(pair, LANES - bit, 1), pltpu.roll(pair, bit, 1))
        ref[pl.ds(base + OBASE[level + 1] + a * half, half), :] = (pair + other) * scale


def x_faces(own_ref, base, up_ref, down_ref, xbase):
    centre = abs(lanes_of(16) - 63.5) < 32
    odd = lanes_of(16) % 2 == 1
    turn = lanes_of(8) % 4
    for dst, end in ((up_ref, 1), (down_ref, 0)):
        at = [base + OBASE[level] + end * (N[level] - HALO) * OWN[level] for level in range(3)]
        for i in range(HALO):
            dst[pl.ds(xbase + 16 * i, 16), :] = own_ref[pl.ds(at[0] + 32 * i, 16), :]
        z = [own_ref[pl.ds(at[0] + 32 * i + 16, 16), :] for i in range(HALO)]
        dst[pl.ds(xbase + 48, 16), :] = jnp.where(centre, pltpu.roll(z[1], 64, 1), z[0])
        dst[pl.ds(xbase + 64, 16), :] = z[2]
        c = [own_ref[pl.ds(at[1] + 16 * i, 16), :] for i in range(HALO)]
        dst[pl.ds(xbase + 80, 16), :] = jnp.where(odd, c[1], c[0])
        dst[pl.ds(xbase + 96, 8), :] = jnp.where(odd[:8], c[2][8:], c[2][:8])
        c = [own_ref[pl.ds(at[2] + 8 * i, 8), :] for i in range(HALO)]
        dst[pl.ds(xbase + 104, 8), :] = jnp.where(turn == 0, c[0], jnp.where(turn == 1, c[1], c[2]))


def unpack(src, at, dst, to):
    odd = lanes_of(16) % 2 == 1
    turn = lanes_of(8) % 4
    for i in range(HALO):
        dst[pl.ds(to + 32 * i, 16), :] = src[pl.ds(at + 16 * i, 16), :]
    z = src[pl.ds(at + 48, 16), :]
    for i, value in enumerate((z, pltpu.roll(z, 64, 1), src[pl.ds(at + 64, 16), :])):
        dst[pl.ds(to + 32 * i + 16, 16), :] = value

    def two(value):
        mask = odd[: value.shape[0]]
        return jnp.where(mask, pltpu.roll(value, 1, 1), value), jnp.where(mask, value, pltpu.roll(value, LANES - 1, 1))

    first = two(src[pl.ds(at + 80, 16), :])
    dst[pl.ds(to + 96, 16), :] = first[0]
    dst[pl.ds(to + 112, 16), :] = first[1]
    last = two(src[pl.ds(at + 96, 8), :])
    dst[pl.ds(to + 128, 8), :] = last[0]
    dst[pl.ds(to + 136, 8), :] = last[1]
    c = src[pl.ds(at + 104, 8), :]
    moved = {d: pltpu.roll(c, d % LANES, 1) if d else c for d in range(-2, 4)}
    for i in range(HALO):
        value = moved[-i]
        for lane in range(1, 4):
            value = jnp.where(turn == lane, moved[lane - i], value)
        dst[pl.ds(to + 144 + 8 * i, 8), :] = value


def begin(fk_ref, zl_ref, zr_ref, raw_ref, own_ref, w_ref, up_ref, down_ref, tmp):
    low = lanes_of(16) < 64
    for field, ref in enumerate((fk_ref.at[pl.ds(0, 256), :], fk_ref.at[pl.ds(256, 256), :])):
        base = field * OROWS
        for g in range(4):
            at = pl.ds(64 * field + 16 * g, 16)
            left, right = zl_ref[at, :], zr_ref[at, :]
            for m in range(4):
                slab = 4 * g + m
                shift_l, shift_r = (96 - 32 * m) % LANES, (-32 * m) % LANES
                from_l = pltpu.roll(left, shift_l, 1) if shift_l else left
                from_r = pltpu.roll(right, shift_r, 1) if shift_r else right
                raw_ref[pl.ds(base + 32 * slab, 16), :] = ref[pl.ds(16 * slab, 16), :]
                raw_ref[pl.ds(base + 32 * slab + 16, 16), :] = jnp.where(low, from_r, from_l)
        scale = 0.125 if field == 0 else 0.125 * 0.25
        coarsen(raw_ref, 0, base, tmp, scale)
        coarsen(raw_ref, 1, base, tmp, scale)
    for at in range(0, OROWS, 32):
        c = raw_ref[pl.ds(OROWS + at, 32), :]
        w = 0.8 / (14.0 * c + 1.0)
        w_ref[pl.ds(at, 32), :] = w
        own_ref[pl.ds(at, 32), :] = w * raw_ref[pl.ds(at, 32), :]
        own_ref[pl.ds(OROWS + at, 32), :] = 0.25 * (w * c)
    for field in range(2):
        x_faces(own_ref, field * OROWS, up_ref, down_ref, field * PACKED)


def y_faces(fields, own_ref, xl_packed, xr_packed, up_ref, down_ref, xl_ref, xr_ref):
    for field in range(fields):
        ob, xb, yb = field * OROWS, field * XROWS, field * YROWS
        unpack(xl_packed, field * PACKED, xl_ref, xb)
        unpack(xr_packed, field * PACKED, xr_ref, xb)
        for dst, first in ((up_ref, False), (down_ref, True)):
            for level in range(3):
                n, rows = N[level], OWN[level]
                for h in range(2):
                    for j in range(HALO):
                        row = h * n + (j if first else n - HALO + j)
                        off = yb + YBASE[level] + (h * HALO + j) * X[level]
                        dst[pl.ds(off, HALO), :] = xl_ref[pl.ds(xb + XBASE[level] + row, HALO, rows), :]
                        dst[pl.ds(off + HALO, n), :] = own_ref[pl.ds(ob + OBASE[level] + row, n, rows), :]
                        dst[pl.ds(off + HALO + n, HALO), :] = xr_ref[pl.ds(xb + XBASE[level] + row, HALO, rows), :]
            dst[pl.ds(yb + 276, 4), :] = jnp.zeros((4, LANES), F32)


def widen(field, own_ref, xl_ref, xr_ref, yl_ref, yr_ref, wide_ref):
    ob, xb, yb = field * OROWS, field * XROWS, field * YROWS
    for level in range(3):
        n, ring, rows = N[level], RING[level], OWN[level]
        for i in range(X[level]):
            if i < HALO:
                ref, at = xl_ref, xb + XBASE[level] + i * rows
            elif i < HALO + n:
                ref, at = own_ref, ob + OBASE[level] + (i - HALO) * rows
            else:
                ref, at = xr_ref, xb + XBASE[level] + (i - HALO - n) * rows
            for h in range(2):
                to = WBASE[level] + i * WIDE[level] + h * ring
                wide_ref[pl.ds(to, n), :] = ref[pl.ds(at + h * n, n), :]
                wide_ref[pl.ds(to + n, ring - n), :] = jnp.zeros((ring - n, LANES), F32)
        for h in range(2):
            for j in range(HALO):
                off = yb + YBASE[level] + (h * HALO + j) * X[level]
                to = WBASE[level] + h * ring
                wide_ref[pl.ds(to + n + j, X[level], WIDE[level]), :] = yr_ref[pl.ds(off, X[level]), :]
                wide_ref[pl.ds(to + ring - HALO + j, X[level], WIDE[level]), :] = yl_ref[pl.ds(off, X[level]), :]


def slab(ref, base, i, rows):
    return ref[pl.ds(pl.multiple_of(base + i * rows, 8), rows), :]


def put(ref, base, i, rows, value):
    ref[pl.ds(pl.multiple_of(base + i * rows, 8), rows), :] = value


def loop(low, high, value, store):
    groups = -(-(high - low) // UNROLL)
    size = -(-(high - low) // groups)
    lead = (high - low) - (groups - 1) * size

    def group(first, count):
        values = [value(first + u) for u in range(count)]
        for u in range(count):
            store(first + u, values[u])

    def step(g, carry):
        group(low + lead + g * size, size)
        return carry

    group(low, lead)
    if groups > 1:
        lax.fori_loop(0, groups - 1, step, 0)


def ring_sum(ref, base, i, ring, step):
    rows = 2 * ring
    mid = slab(ref, base, i, rows)
    total = slab(ref, base, i - 1, rows) + slab(ref, base, i + 1, rows) + (mid + mid)
    halves = []
    for h in range(2):
        t = total[h * ring : (h + 1) * ring]
        t = t + pltpu.roll(t, 1, 0)
        halves.append(t + pltpu.roll(t, ring - 1, 0))
    lane = lanes_of(ring)
    a, b = halves
    ra, rb = pltpu.roll(a, step, 1), pltpu.roll(b, step, 1)
    edge = lane < step
    a, b = a + jnp.where(edge, rb, ra), b + jnp.where(edge, ra, rb)
    ra, rb = pltpu.roll(a, LANES - step, 1), pltpu.roll(b, LANES - step, 1)
    edge = lane >= LANES - step
    a, b = a + jnp.where(edge, rb, ra), b + jnp.where(edge, ra, rb)
    return mid, a, b


def join(a, b):
    return jnp.concatenate([a, b], axis=0)


def sweeps(wide_b, wide_u, first, second):
    for level in range(3):
        rows, base, ring, step = WIDE[level], WBASE[level], RING[level], STEP[level]

        def sweep(low, high, src, dst):
            def value(i):
                mid, a, b = ring_sum(src, base, i, ring, step)
                around = slab(wide_u, base, i, rows) * (join(a, b) - 8.0 * mid)
                return 0.2 * mid + slab(wide_b, base, i, rows) + around

            loop(low, high, value, lambda i, new: put(dst, base, i, rows, new))

        sweep(1, X[level] - 1, wide_b, first)
        sweep(2, X[level] - 2, first, second)


def prolong(err, up3, up2):
    for q in range(6):
        for h in range(2):
            e3 = err[pl.ds(WBASE[2] + (q + 2) * 32 + h * 16, 16), :]
            to = q * 32 + h * 16
            up3[pl.ds(to, 5, 2), :] = e3[0:5]
            up3[pl.ds(to + 1, 5, 2), :] = e3[0:5]
            up3[pl.ds(to + 10, 4), :] = jnp.zeros((4, LANES), F32)
            up3[pl.ds(to + 14, 2), :] = jnp.broadcast_to(e3[15:16], (2, LANES))
    for a in range(10):
        for h in range(2):
            e2 = err[pl.ds(WBASE[1] + (a + 2) * 32 + h * 16, 16), :]
            e2 = e2 + up3[pl.ds(((a - 1) // 2 + 1) * 32 + h * 16, 16), :]
            to = a * 48 + h * 24
            up2[pl.ds(to, 9, 2), :] = e2[0:9]
            up2[pl.ds(to + 1, 9, 2), :] = e2[0:9]
            up2[pl.ds(to + 18, 4), :] = jnp.zeros((4, LANES), F32)
            up2[pl.ds(to + 22, 2), :] = jnp.broadcast_to(e2[15:16], (2, LANES))


def correct(err, up2, old_ref, sol_ref):
    for i in range(18):
        value = err[pl.ds((i + 2) * 48, 48), :] + up2[pl.ds(((i - 1) // 2 + 1) * 48, 48), :]
        if old_ref is not None:
            value = value + old_ref[pl.ds(i * 48, 48), :]
        sol_ref[pl.ds(i * 48, 48), :] = value


def first_round(
    raw_ref, own_ref, w_ref, xl_ref, xr_ref, yl_ref, yr_ref,
    next_ref, up_ref, down_ref, sol_ref, wide_u,
    wide_b, first, second, up3, up2, r_ref, tmp,
):
    widen(0, own_ref, xl_ref, xr_ref, yl_ref, yr_ref, wide_b)
    widen(1, own_ref, xl_ref, xr_ref, yl_ref, yr_ref, wide_u)
    sweeps(wide_b, wide_u, first, second)
    prolong(second, up3, up2)
    correct(second, up2, None, sol_ref)

    def resid(i):
        mid, a, b = ring_sum(sol_ref, 0, i + 1, 24, 1)
        halves = []
        for h, t in enumerate((a, b)):
            s = mid[h * 24 : h * 24 + 16]
            f = raw_ref[pl.ds(pl.multiple_of(i * 32 + h * 16, 16), 16), :]
            k = raw_ref[pl.ds(pl.multiple_of(OROWS + i * 32 + h * 16, 16), 16), :]
            halves.append(f - (k * (16.0 * s - 0.25 * t[:16]) + s))
        return join(*halves)

    loop(0, 16, resid, lambda i, new: put(r_ref, 0, i, 32, new))
    coarsen(r_ref, 0, 0, tmp, 0.125)
    coarsen(r_ref, 1, 0, tmp, 0.125)
    for at in range(0, OROWS, 32):
        next_ref[pl.ds(at, 32), :] = w_ref[pl.ds(at, 32), :] * r_ref[pl.ds(at, 32), :]
    x_faces(next_ref, 0, up_ref, down_ref, 0)


def second_round(
    fk_ref, own_ref, xl_ref, xr_ref, yl_ref, yr_ref, old_ref, wide_u,
    out_hbm, resid_hbm,
    wide_b, first, second, sol_ref, up3, up2, out_ref, resid_ref, sems,
):
    widen(0, own_ref, xl_ref, xr_ref, yl_ref, yr_ref, wide_b)
    sweeps(wide_b, wide_u, first, second)
    prolong(second, up3, up2)
    correct(second, up2, old_ref, sol_ref)
    for i in range(16):
        out_ref[pl.ds(16 * i, 16), :] = sol_ref[pl.ds(48 * (i + 1), 16), :]
    copies = [pltpu.make_async_copy(out_ref, out_hbm, sems.at[0])]
    copies[0].start()

    def resid(i):
        mid, a, _ = ring_sum(sol_ref, 0, i + 1, 24, 1)
        s = mid[:16]
        return slab(fk_ref, 0, i, 16) - (slab(fk_ref, 256, i, 16) * (16.0 * s - 0.25 * a[:16]) + s)

    for half in range(2):
        loop(8 * half, 8 * half + 8, resid, lambda i, new: put(resid_ref, 0, i, 16, new))
        at = pl.ds(128 * half, 128)
        copies.append(pltpu.make_async_copy(resid_ref.at[at, :], resid_hbm.at[at, :], sems.at[1 + half]))
        copies[-1].start()
    for copy in copies:
        copy.wait()


def shift(up, down, axis):
    size = lax.axis_size(axis)
    rising = [(i, i + 1) for i in range(size - 1)]
    falling = [(j, i) for i, j in rising]
    return lax.ppermute(up, axis, rising), lax.ppermute(down, axis, falling)


def swap(up, down, axis):
    size = lax.axis_size(axis)
    odd = lax.axis_index(axis) % 2 == 1
    inner = [(i, i ^ 1) for i in range(size)]
    outer = [(i, i + 1) for i in range(1, size - 1, 2)]
    outer = outer + [(j, i) for i, j in outer]
    one = lax.ppermute(jnp.where(odd, down, up), axis, inner)
    two = lax.ppermute(jnp.where(odd, up, down), axis, outer)
    return jnp.where(odd, one, two), jnp.where(odd, two, one)


def shards(forcing, kappa):
    shape = forcing.shape
    f = forcing.reshape(256, LANES)
    k = kappa.reshape(256, LANES)
    fk = lax.optimization_barrier(jnp.concatenate([f, k]))
    up, down = call(z_faces, [128, 128], [], fk)
    zl, zr = shift(up, down, "grp")
    raw, own, w, up, down = call(
        begin, [2 * OROWS, 2 * OROWS, OROWS, 2 * PACKED, 2 * PACKED], [256], fk, zl, zr
    )
    xl, xr = shift(up, down, "gx")

    def faces(fields, own, xl, xr):
        def kernel(*refs):
            y_faces(fields, *refs)

        return call(kernel, [fields * YROWS] * 2 + [fields * XROWS] * 2, [], own, xl, xr)

    up, down, xl, xr = faces(2, own, xl, xr)
    yl, yr = swap(up, down, "gy")
    own, up, down, sol, wide_u = call(
        first_round,
        [OROWS, PACKED, PACKED, SOLROWS, WROWS],
        [WROWS, WROWS, WROWS, 192, 480, OROWS, 256],
        raw, own, w, xl, xr, yl, yr,
    )
    xl, xr = shift(up, down, "gx")
    up, down, xl, xr = faces(1, own, xl, xr)
    yl, yr = swap(up, down, "gy")
    out, resid = call(
        second_round,
        [256, 256],
        [WROWS, WROWS, WROWS, SOLROWS, 192, 480, 256, 256],
        fk, own, xl, xr, yl, yr, sol, wide_u,
        out_specs=[HBM, HBM], copies=3,
    )
    return out.reshape(shape), resid.reshape(shape)


def solution(mesh):
    placed = (P("gx", "gy", "grp"), P("gx", "gy", "grp"))
    return jax.shard_map(shards, mesh=mesh, in_specs=placed, out_specs=placed, check_vma=False)
```

```python
import jax
import jax.numpy as jnp
from jax import lax
from jax.experimental import pallas as pl
from jax.experimental.pallas import tpu as pltpu
from jax.sharding import PartitionSpec as P

F32 = jnp.float32
LANES = 128
HALO = 3
N = (16, 8, 4)
X = tuple(n + 2 * HALO for n in N)
RING = (24, 16, 16)
STEP = (1, 2, 4)
OWN = tuple(2 * n for n in N)
WIDE = tuple(2 * r for r in RING)
OBASE = (0, 512, 640)
OROWS = 672
XBASE = (0, 96, 144)
XROWS = 168
YBASE = (0, 132, 216)
YROWS = 280
PACKED = 112
UNROLL = 8
WBASE = (0, 1056, 1504)
WROWS = 1824
SOLROWS = 18 * 48
VMEM_LIMIT = 48 * 1024 * 1024


def lanes_of(rows):
    return lax.broadcasted_iota(jnp.int32, (rows, LANES), 1)


VM = pl.BlockSpec(memory_space=pltpu.VMEM)
HBM = pl.BlockSpec(memory_space=pl.ANY)


def call(kernel, outs, scratch, *args, out_specs=None, copies=0):
    return pl.pallas_call(
        kernel,
        out_shape=[jax.ShapeDtypeStruct((rows, LANES), F32) for rows in outs],
        in_specs=[VM] * len(args),
        out_specs=out_specs or [VM] * len(outs),
        scratch_shapes=[pltpu.VMEM((rows, LANES), F32) for rows in scratch]
        + ([pltpu.SemaphoreType.DMA((copies,))] if copies else []),
        compiler_params=pltpu.CompilerParams(vmem_limit_bytes=VMEM_LIMIT),
    )(*args)


def z_faces(fk_ref, up_ref, down_ref):
    quarter = lanes_of(16) // 32
    for field, ref in enumerate((fk_ref.at[pl.ds(0, 256), :], fk_ref.at[pl.ds(256, 256), :])):
        for g in range(4):
            slabs = [ref[pl.ds(16 * (4 * g + m), 16), :] for m in range(4)]
            up = pltpu.roll(slabs[0], 32, 1)
            down = slabs[0]
            for m in range(1, 4):
                shift = 32 * (m + 1) % LANES
                moved = pltpu.roll(slabs[m], shift, 1) if shift else slabs[m]
                up = jnp.where(quarter == m, moved, up)
                down = jnp.where(quarter == m, pltpu.roll(slabs[m], 32 * m, 1), down)
            at = pl.ds(64 * field + 16 * g, 16)
            up_ref[at, :] = up
            down_ref[at, :] = down


def coarsen(ref, level, base, tmp, scale):
    rows = OWN[level]
    half = rows // 2
    bit = STEP[level]
    even = (lanes_of(half) // bit) % 2 == 0
    for a in range(N[level] // 2):
        at = base + OBASE[level] + 2 * a * rows
        tmp[pl.ds(a * rows, rows), :] = ref[pl.ds(at, rows), :] + ref[pl.ds(at + rows, rows), :]
    for a in range(N[level] // 2):
        pair = tmp[pl.ds(a * rows, half, 2), :] + tmp[pl.ds(a * rows + 1, half, 2), :]
        other = jnp.where(even, pltpu.roll(pair, LANES - bit, 1), pltpu.roll(pair, bit, 1))
        ref[pl.ds(base + OBASE[level + 1] + a * half, half), :] = (pair + other) * scale


def x_faces(own_ref, base, up_ref, down_ref, xbase):
    centre = abs(lanes_of(16) - 63.5) < 32
    odd = lanes_of(16) % 2 == 1
    turn = lanes_of(8) % 4
    for dst, end in ((up_ref, 1), (down_ref, 0)):
        at = [base + OBASE[level] + end * (N[level] - HALO) * OWN[level] for level in range(3)]
        for i in range(HALO):
            dst[pl.ds(xbase + 16 * i, 16), :] = own_ref[pl.ds(at[0] + 32 * i, 16), :]
        z = [own_ref[pl.ds(at[0] + 32 * i + 16, 16), :] for i in range(HALO)]
        dst[pl.ds(xbase + 48, 16), :] = jnp.where(centre, pltpu.roll(z[1], 64, 1), z[0])
        dst[pl.ds(xbase + 64, 16), :] = z[2]
        c = [own_ref[pl.ds(at[1] + 16 * i, 16), :] for i in range(HALO)]
        dst[pl.ds(xbase + 80, 16), :] = jnp.where(odd, c[1], c[0])
        dst[pl.ds(xbase + 96, 8), :] = jnp.where(odd[:8], c[2][8:], c[2][:8])
        c = [own_ref[pl.ds(at[2] + 8 * i, 8), :] for i in range(HALO)]
        dst[pl.ds(xbase + 104, 8), :] = jnp.where(turn == 0, c[0], jnp.where(turn == 1, c[1], c[2]))


def unpack(src, at, dst, to):
    odd = lanes_of(16) % 2 == 1
    turn = lanes_of(8) % 4
    for i in range(HALO):
        dst[pl.ds(to + 32 * i, 16), :] = src[pl.ds(at + 16 * i, 16), :]
    z = src[pl.ds(at + 48, 16), :]
    for i, value in enumerate((z, pltpu.roll(z, 64, 1), src[pl.ds(at + 64, 16), :])):
        dst[pl.ds(to + 32 * i + 16, 16), :] = value

    def two(value):
        mask = odd[: value.shape[0]]
        return jnp.where(mask, pltpu.roll(value, 1, 1), value), jnp.where(mask, value, pltpu.roll(value, LANES - 1, 1))

    first = two(src[pl.ds(at + 80, 16), :])
    dst[pl.ds(to + 96, 16), :] = first[0]
    dst[pl.ds(to + 112, 16), :] = first[1]
    last = two(src[pl.ds(at + 96, 8), :])
    dst[pl.ds(to + 128, 8), :] = last[0]
    dst[pl.ds(to + 136, 8), :] = last[1]
    c = src[pl.ds(at + 104, 8), :]
    moved = {d: pltpu.roll(c, d % LANES, 1) if d else c for d in range(-2, 4)}
    for i in range(HALO):
        value = moved[-i]
        for lane in range(1, 4):
            value = jnp.where(turn == lane, moved[lane - i], value)
        dst[pl.ds(to + 144 + 8 * i, 8), :] = value


def begin(fk_ref, zl_ref, zr_ref, raw_ref, own_ref, w_ref, up_ref, down_ref, tmp):
    low = lanes_of(16) < 64
    for field, ref in enumerate((fk_ref.at[pl.ds(0, 256), :], fk_ref.at[pl.ds(256, 256), :])):
        base = field * OROWS
        for g in range(4):
            at = pl.ds(64 * field + 16 * g, 16)
            left, right = zl_ref[at, :], zr_ref[at, :]
            for m in range(4):
                slab = 4 * g + m
                shift_l, shift_r = (96 - 32 * m) % LANES, (-32 * m) % LANES
                from_l = pltpu.roll(left, shift_l, 1) if shift_l else left
                from_r = pltpu.roll(right, shift_r, 1) if shift_r else right
                raw_ref[pl.ds(base + 32 * slab, 16), :] = ref[pl.ds(16 * slab, 16), :]
                raw_ref[pl.ds(base + 32 * slab + 16, 16), :] = jnp.where(low, from_r, from_l)
        scale = 0.125 if field == 0 else 0.125 * 0.25
        coarsen(raw_ref, 0, base, tmp, scale)
        coarsen(raw_ref, 1, base, tmp, scale)
    for at in range(0, OROWS, 32):
        c = raw_ref[pl.ds(OROWS + at, 32), :]
        w = 0.8 / (14.0 * c + 1.0)
        w_ref[pl.ds(at, 32), :] = w
        own_ref[pl.ds(at, 32), :] = w * raw_ref[pl.ds(at, 32), :]
        own_ref[pl.ds(OROWS + at, 32), :] = 0.25 * (w * c)
    for field in range(2):
        x_faces(own_ref, field * OROWS, up_ref, down_ref, field * PACKED)


def y_faces(fields, own_ref, xl_packed, xr_packed, up_ref, down_ref, xl_ref, xr_ref):
    for field in range(fields):
        ob, xb, yb = field * OROWS, field * XROWS, field * YROWS
        unpack(xl_packed, field * PACKED, xl_ref, xb)
        unpack(xr_packed, field * PACKED, xr_ref, xb)
        for dst, first in ((up_ref, False), (down_ref, True)):
            for level in range(3):
                n, rows = N[level], OWN[level]
                for h in range(2):
                    for j in range(HALO):
                        row = h * n + (j if first else n - HALO + j)
                        off = yb + YBASE[level] + (h * HALO + j) * X[level]
                        dst[pl.ds(off, HALO), :] = xl_ref[pl.ds(xb + XBASE[level] + row, HALO, rows), :]
                        dst[pl.ds(off + HALO, n), :] = own_ref[pl.ds(ob + OBASE[level] + row, n, rows), :]
                        dst[pl.ds(off + HALO + n, HALO), :] = xr_ref[pl.ds(xb + XBASE[level] + row, HALO, rows), :]
            dst[pl.ds(yb + 276, 4), :] = jnp.zeros((4, LANES), F32)


def widen(field, own_ref, xl_ref, xr_ref, yl_ref, yr_ref, wide_ref):
    ob, xb, yb = field * OROWS, field * XROWS, field * YROWS
    for level in range(3):
        n, ring, rows = N[level], RING[level], OWN[level]
        for i in range(X[level]):
            if i < HALO:
                ref, at = xl_ref, xb + XBASE[level] + i * rows
            elif i < HALO + n:
                ref, at = own_ref, ob + OBASE[level] + (i - HALO) * rows
            else:
                ref, at = xr_ref, xb + XBASE[level] + (i - HALO - n) * rows
            for h in range(2):
                to = WBASE[level] + i * WIDE[level] + h * ring
                wide_ref[pl.ds(to, n), :] = ref[pl.ds(at + h * n, n), :]
                wide_ref[pl.ds(to + n, ring - n), :] = jnp.zeros((ring - n, LANES), F32)
        for h in range(2):
            for j in range(HALO):
                off = yb + YBASE[level] + (h * HALO + j) * X[level]
                to = WBASE[level] + h * ring
                wide_ref[pl.ds(to + n + j, X[level], WIDE[level]), :] = yr_ref[pl.ds(off, X[level]), :]
                wide_ref[pl.ds(to + ring - HALO + j, X[level], WIDE[level]), :] = yl_ref[pl.ds(off, X[level]), :]


def slab(ref, base, i, rows):
    return ref[pl.ds(pl.multiple_of(base + i * rows, 8), rows), :]


def put(ref, base, i, rows, value):
    ref[pl.ds(pl.multiple_of(base + i * rows, 8), rows), :] = value


def loop(low, high, value, store):
    groups = -(-(high - low) // UNROLL)
    size = -(-(high - low) // groups)
    lead = (high - low) - (groups - 1) * size

    def group(first, count):
        values = [value(first + u) for u in range(count)]
        for u in range(count):
            store(first + u, values[u])

    def step(g, carry):
        group(low + lead + g * size, size)
        return carry

    group(low, lead)
    if groups > 1:
        lax.fori_loop(0, groups - 1, step, 0)


def ring_sum(ref, base, i, ring, step):
    rows = 2 * ring
    mid = slab(ref, base, i, rows)
    total = slab(ref, base, i - 1, rows) + slab(ref, base, i + 1, rows) + (mid + mid)
    halves = []
    for h in range(2):
        t = total[h * ring : (h + 1) * ring]
        t = t + pltpu.roll(t, 1, 0)
        halves.append(t + pltpu.roll(t, ring - 1, 0))
    lane = lanes_of(ring)
    a, b = halves
    ra, rb = pltpu.roll(a, step, 1), pltpu.roll(b, step, 1)
    edge = lane < step
    a, b = a + jnp.where(edge, rb, ra), b + jnp.where(edge, ra, rb)
    ra, rb = pltpu.roll(a, LANES - step, 1), pltpu.roll(b, LANES - step, 1)
    edge = lane >= LANES - step
    a, b = a + jnp.where(edge, rb, ra), b + jnp.where(edge, ra, rb)
    return mid, a, b


def join(a, b):
    return jnp.concatenate([a, b], axis=0)


def sweeps(wide_b, wide_u, first, second):
    for level in range(3):
        rows, base, ring, step = WIDE[level], WBASE[level], RING[level], STEP[level]

        def sweep(low, high, src, dst):
            def value(i):
                mid, a, b = ring_sum(src, base, i, ring, step)
                around = slab(wide_u, base, i, rows) * (join(a, b) - 8.0 * mid)
                return 0.2 * mid + slab(wide_b, base, i, rows) + around

            loop(low, high, value, lambda i, new: put(dst, base, i, rows, new))

        sweep(1, X[level] - 1, wide_b, first)
        sweep(2, X[level] - 2, first, second)


def prolong(err, up3, up2):
    for q in range(6):
        for h in range(2):
            e3 = err[pl.ds(WBASE[2] + (q + 2) * 32 + h * 16, 16), :]
            to = q * 32 + h * 16
            up3[pl.ds(to, 5, 2), :] = e3[0:5]
            up3[pl.ds(to + 1, 5, 2), :] = e3[0:5]
            up3[pl.ds(to + 10, 4), :] = jnp.zeros((4, LANES), F32)
            up3[pl.ds(to + 14, 2), :] = jnp.broadcast_to(e3[15:16], (2, LANES))
    for a in range(10):
        for h in range(2):
            e2 = err[pl.ds(WBASE[1] + (a + 2) * 32 + h * 16, 16), :]
            e2 = e2 + up3[pl.ds(((a - 1) // 2 + 1) * 32 + h * 16, 16), :]
            to = a * 48 + h * 24
            up2[pl.ds(to, 9, 2), :] = e2[0:9]
            up2[pl.ds(to + 1, 9, 2), :] = e2[0:9]
            up2[pl.ds(to + 18, 4), :] = jnp.zeros((4, LANES), F32)
            up2[pl.ds(to + 22, 2), :] = jnp.broadcast_to(e2[15:16], (2, LANES))


def correct(err, up2, old_ref, sol_ref):
    for i in range(18):
        value = err[pl.ds((i + 2) * 48, 48), :] + up2[pl.ds(((i - 1) // 2 + 1) * 48, 48), :]
        if old_ref is not None:
            value = value + old_ref[pl.ds(i * 48, 48), :]
        sol_ref[pl.ds(i * 48, 48), :] = value


def first_round(
    raw_ref, own_ref, w_ref, xl_ref, xr_ref, yl_ref, yr_ref,
    next_ref, up_ref, down_ref, sol_ref, wide_u,
    wide_b, first, second, up3, up2, r_ref, tmp,
):
    widen(0, own_ref, xl_ref, xr_ref, yl_ref, yr_ref, wide_b)
    widen(1, own_ref, xl_ref, xr_ref, yl_ref, yr_ref, wide_u)
    sweeps(wide_b, wide_u, first, second)
    prolong(second, up3, up2)
    correct(second, up2, None, sol_ref)

    def resid(i):
        mid, a, b = ring_sum(sol_ref, 0, i + 1, 24, 1)
        halves = []
        for h, t in enumerate((a, b)):
            s = mid[h * 24 : h * 24 + 16]
            f = raw_ref[pl.ds(pl.multiple_of(i * 32 + h * 16, 16), 16), :]
            k = raw_ref[pl.ds(pl.multiple_of(OROWS + i * 32 + h * 16, 16), 16), :]
            halves.append(f - (k * (16.0 * s - 0.25 * t[:16]) + s))
        return join(*halves)

    loop(0, 16, resid, lambda i, new: put(r_ref, 0, i, 32, new))
    coarsen(r_ref, 0, 0, tmp, 0.125)
    coarsen(r_ref, 1, 0, tmp, 0.125)
    for at in range(0, OROWS, 32):
        next_ref[pl.ds(at, 32), :] = w_ref[pl.ds(at, 32), :] * r_ref[pl.ds(at, 32), :]
    x_faces(next_ref, 0, up_ref, down_ref, 0)


def second_round(
    fk_ref, own_ref, xl_ref, xr_ref, yl_ref, yr_ref, old_ref, wide_u,
    out_hbm, resid_hbm,
    wide_b, first, second, sol_ref, up3, up2, out_ref, resid_ref, sems,
):
    widen(0, own_ref, xl_ref, xr_ref, yl_ref, yr_ref, wide_b)
    sweeps(wide_b, wide_u, first, second)
    prolong(second, up3, up2)
    correct(second, up2, old_ref, sol_ref)
    for i in range(16):
        out_ref[pl.ds(16 * i, 16), :] = sol_ref[pl.ds(48 * (i + 1), 16), :]
    copies = [pltpu.make_async_copy(out_ref, out_hbm, sems.at[0])]
    copies[0].start()

    def resid(i):
        mid, a, _ = ring_sum(sol_ref, 0, i + 1, 24, 1)
        s = mid[:16]
        return slab(fk_ref, 0, i, 16) - (slab(fk_ref, 256, i, 16) * (16.0 * s - 0.25 * a[:16]) + s)

    for half in range(2):
        loop(8 * half, 8 * half + 8, resid, lambda i, new: put(resid_ref, 0, i, 16, new))
        at = pl.ds(128 * half, 128)
        copies.append(pltpu.make_async_copy(resid_ref.at[at, :], resid_hbm.at[at, :], sems.at[1 + half]))
        copies[-1].start()
    for copy in copies:
        copy.wait()


def exchange(up, down, axis):
    size = lax.axis_size(axis)
    odd = lax.axis_index(axis) % 2 == 1
    outer = [(i, i + 1) for i in range(1, size - 1, 2)]
    outer = outer + [(j, i) for i, j in outer]
    inner = [[i, i + 1] for i in range(0, size, 2)]
    two = lax.ppermute(jnp.where(odd, up, down), axis, outer)
    one = lax.all_gather(jnp.where(odd, down, up), axis, axis_index_groups=inner)
    return jnp.where(odd, one[0], two), jnp.where(odd, two, one[1])


def swap(up, down, axis):
    size = lax.axis_size(axis)
    odd = lax.axis_index(axis) % 2 == 1
    inner = [(i, i ^ 1) for i in range(size)]
    outer = [(i, i + 1) for i in range(1, size - 1, 2)]
    outer = outer + [(j, i) for i, j in outer]
    one = lax.ppermute(jnp.where(odd, down, up), axis, inner)
    two = lax.ppermute(jnp.where(odd, up, down), axis, outer)
    return jnp.where(odd, one, two), jnp.where(odd, two, one)


def shards(forcing, kappa):
    shape = forcing.shape
    f = forcing.reshape(256, LANES)
    k = kappa.reshape(256, LANES)
    fk = lax.optimization_barrier(jnp.concatenate([f, k]))
    up, down = call(z_faces, [128, 128], [], fk)
    zl, zr = exchange(up, down, "grp")
    raw, own, w, up, down = call(
        begin, [2 * OROWS, 2 * OROWS, OROWS, 2 * PACKED, 2 * PACKED], [256], fk, zl, zr
    )
    xl, xr = exchange(up, down, "gx")

    def faces(fields, own, xl, xr):
        def kernel(*refs):
            y_faces(fields, *refs)

        return call(kernel, [fields * YROWS] * 2 + [fields * XROWS] * 2, [], own, xl, xr)

    up, down, xl, xr = faces(2, own, xl, xr)
    yl, yr = swap(up, down, "gy")
    own, up, down, sol, wide_u = call(
        first_round,
        [OROWS, PACKED, PACKED, SOLROWS, WROWS],
        [WROWS, WROWS, WROWS, 192, 480, OROWS, 256],
        raw, own, w, xl, xr, yl, yr,
    )
    xl, xr = exchange(up, down, "gx")
    up, down, xl, xr = faces(1, own, xl, xr)
    yl, yr = swap(up, down, "gy")
    out, resid = call(
        second_round,
        [256, 256],
        [WROWS, WROWS, WROWS, SOLROWS, 192, 480, 256, 256],
        fk, own, xl, xr, yl, yr, sol, wide_u,
        out_specs=[HBM, HBM], copies=3,
    )
    return out.reshape(shape), resid.reshape(shape)


def solution(mesh):
    placed = (P("gx", "gy", "grp"), P("gx", "gy", "grp"))
    return jax.shard_map(shards, mesh=mesh, in_specs=placed, out_specs=placed, check_vma=False)
```

```python
import jax
import jax.numpy as jnp
from jax import lax
from jax.experimental import pallas as pl
from jax.experimental.pallas import tpu as pltpu
from jax.sharding import PartitionSpec as P

F32 = jnp.float32
LANES = 128
HALO = 3
N = (16, 8, 4)
X = tuple(n + 2 * HALO for n in N)
RING = (24, 16, 16)
STEP = (1, 2, 4)
OWN = tuple(2 * n for n in N)
WIDE = tuple(2 * r for r in RING)
OBASE = (0, 512, 640)
OROWS = 672
XBASE = (0, 96, 144)
XROWS = 168
YBASE = (0, 132, 216)
YROWS = 280
PACKED = (0, 96, 168)
LAYERS = (3, 2)
UNROLL = 8
GROUPS = (4, 3)
WBASE = (0, 1056, 1504)
WROWS = 1824
SOLROWS = 18 * 48
VMEM_LIMIT = 48 * 1024 * 1024


def lanes_of(rows):
    return lax.broadcasted_iota(jnp.int32, (rows, LANES), 1)


VM = pl.BlockSpec(memory_space=pltpu.VMEM)
HBM = pl.BlockSpec(memory_space=pl.ANY)


def call(kernel, outs, scratch, *args, out_specs=None, copies=0):
    return pl.pallas_call(
        kernel,
        out_shape=[jax.ShapeDtypeStruct((rows, LANES), F32) for rows in outs],
        in_specs=[VM] * len(args),
        out_specs=out_specs or [VM] * len(outs),
        scratch_shapes=[pltpu.VMEM((rows, LANES), F32) for rows in scratch]
        + ([pltpu.SemaphoreType.DMA((copies,))] if copies else []),
        compiler_params=pltpu.CompilerParams(vmem_limit_bytes=VMEM_LIMIT),
    )(*args)


def z_faces(fk_ref, up_ref, down_ref):
    quarter = lanes_of(16) // 32
    for field, ref in enumerate((fk_ref.at[pl.ds(0, 256), :], fk_ref.at[pl.ds(256, 256), :])):
        for g in range(4):
            slabs = [ref[pl.ds(16 * (4 * g + m), 16), :] for m in range(4)]
            up = pltpu.roll(slabs[0], 32, 1)
            down = slabs[0]
            for m in range(1, 4):
                shift = 32 * (m + 1) % LANES
                moved = pltpu.roll(slabs[m], shift, 1) if shift else slabs[m]
                up = jnp.where(quarter == m, moved, up)
                down = jnp.where(quarter == m, pltpu.roll(slabs[m], 32 * m, 1), down)
            at = pl.ds(64 * field + 16 * g, 16)
            up_ref[at, :] = up
            down_ref[at, :] = down


def coarsen(ref, level, base, tmp, scale):
    rows = OWN[level]
    half = rows // 2
    bit = STEP[level]
    even = (lanes_of(half) // bit) % 2 == 0
    for a in range(N[level] // 2):
        at = base + OBASE[level] + 2 * a * rows
        tmp[pl.ds(a * rows, rows), :] = ref[pl.ds(at, rows), :] + ref[pl.ds(at + rows, rows), :]
    for a in range(N[level] // 2):
        pair = tmp[pl.ds(a * rows, half, 2), :] + tmp[pl.ds(a * rows + 1, half, 2), :]
        other = jnp.where(even, pltpu.roll(pair, LANES - bit, 1), pltpu.roll(pair, bit, 1))
        ref[pl.ds(base + OBASE[level + 1] + a * half, half), :] = (pair + other) * scale


def x_faces(own_ref, base, up_ref, down_ref, xbase, count):
    lane = lanes_of(16)
    odd = lane % 2 == 1
    turn = lanes_of(8) % 4
    for dst, end in ((up_ref, 1), (down_ref, 0)):
        at = [base + OBASE[level] + end * (N[level] - count) * OWN[level] for level in range(3)]
        to = xbase
        for i in range(count):
            dst[pl.ds(to, 16), :] = own_ref[pl.ds(at[0] + 32 * i, 16), :]
            to += 16
        shared = own_ref[pl.ds(at[0] + 16, 16), :]
        for i in range(1, count):
            moved = pltpu.roll(own_ref[pl.ds(at[0] + 32 * i + 16, 16), :], 32 * i, 1)
            shared = jnp.where((lane + 16) // 32 == i, moved, shared)
        dst[pl.ds(to, 16), :] = shared
        c = [own_ref[pl.ds(at[1] + 16 * i, 16), :] for i in range(count)]
        dst[pl.ds(to + 16, 16), :] = jnp.where(odd, c[1], c[0])
        to += 32
        if count == 3:
            dst[pl.ds(to, 8), :] = jnp.where(odd[:8], c[2][8:], c[2][:8])
            to += 8
        c = [own_ref[pl.ds(at[2] + 8 * i, 8), :] for i in range(count)]
        shared = c[0]
        for i in range(1, count):
            shared = jnp.where(turn == i, c[i], shared)
        dst[pl.ds(to, 8), :] = shared


def unpack(src, at, dst, to, count, skip):
    odd = lanes_of(16) % 2 == 1
    turn = lanes_of(8) % 4
    for level in range(3):
        rows = OWN[level]
        for i in range(HALO):
            if not skip <= i < skip + count:
                dst[pl.ds(to + XBASE[level] + rows * i, rows), :] = jnp.zeros((rows, LANES), F32)
    to1, to2, to3 = (to + XBASE[level] + skip * OWN[level] for level in range(3))
    for i in range(count):
        dst[pl.ds(to1 + 32 * i, 16), :] = src[pl.ds(at, 16), :]
        at += 16
    shared = src[pl.ds(at, 16), :]
    for i in range(count):
        dst[pl.ds(to1 + 32 * i + 16, 16), :] = pltpu.roll(shared, LANES - 32 * i, 1) if i else shared

    def two(value):
        mask = odd[: value.shape[0]]
        return jnp.where(mask, pltpu.roll(value, 1, 1), value), jnp.where(mask, value, pltpu.roll(value, LANES - 1, 1))

    first = two(src[pl.ds(at + 16, 16), :])
    dst[pl.ds(to2, 16), :] = first[0]
    dst[pl.ds(to2 + 16, 16), :] = first[1]
    at += 32
    if count == 3:
        last = two(src[pl.ds(at, 8), :])
        dst[pl.ds(to2 + 32, 8), :] = last[0]
        dst[pl.ds(to2 + 40, 8), :] = last[1]
        at += 8
    c = src[pl.ds(at, 8), :]
    moved = {d: pltpu.roll(c, d % LANES, 1) if d else c for d in range(1 - count, 4)}
    for i in range(count):
        value = moved[-i]
        for lane in range(1, 4):
            value = jnp.where(turn == lane, moved[lane - i], value)
        dst[pl.ds(to3 + 8 * i, 8), :] = value


def begin(fk_ref, zl_ref, zr_ref, raw_ref, own_ref, w_ref, up_ref, down_ref, tmp):
    low = lanes_of(16) < 64
    for field, ref in enumerate((fk_ref.at[pl.ds(0, 256), :], fk_ref.at[pl.ds(256, 256), :])):
        base = field * OROWS
        for g in range(4):
            at = pl.ds(64 * field + 16 * g, 16)
            left, right = zl_ref[at, :], zr_ref[at, :]
            for m in range(4):
                slab = 4 * g + m
                shift_l, shift_r = (96 - 32 * m) % LANES, (-32 * m) % LANES
                from_l = pltpu.roll(left, shift_l, 1) if shift_l else left
                from_r = pltpu.roll(right, shift_r, 1) if shift_r else right
                raw_ref[pl.ds(base + 32 * slab, 16), :] = ref[pl.ds(16 * slab, 16), :]
                raw_ref[pl.ds(base + 32 * slab + 16, 16), :] = jnp.where(low, from_r, from_l)
        scale = 0.125 if field == 0 else 0.125 * 0.25
        coarsen(raw_ref, 0, base, tmp, scale)
        coarsen(raw_ref, 1, base, tmp, scale)
    for at in range(0, OROWS, 32):
        c = raw_ref[pl.ds(OROWS + at, 32), :]
        w = 0.8 / (14.0 * c + 1.0)
        w_ref[pl.ds(at, 32), :] = w
        own_ref[pl.ds(at, 32), :] = w * raw_ref[pl.ds(at, 32), :]
        own_ref[pl.ds(OROWS + at, 32), :] = 0.25 * (w * c)
    for field in range(2):
        x_faces(own_ref, field * OROWS, up_ref, down_ref, PACKED[field], LAYERS[field])


def y_faces(fields, own_ref, xl_packed, xr_packed, up_ref, down_ref, xl_ref, xr_ref):
    for field in range(fields):
        ob, xb, yb = field * OROWS, field * XROWS, field * YROWS
        count = LAYERS[field]
        unpack(xl_packed, PACKED[field], xl_ref, xb, count, HALO - count)
        unpack(xr_packed, PACKED[field], xr_ref, xb, count, 0)
        for dst, first in ((up_ref, False), (down_ref, True)):
            for level in range(3):
                n, rows = N[level], OWN[level]
                for h in range(2):
                    for j in range(HALO):
                        row = h * n + (j if first else n - HALO + j)
                        off = yb + YBASE[level] + (h * HALO + j) * X[level]
                        dst[pl.ds(off, HALO), :] = xl_ref[pl.ds(xb + XBASE[level] + row, HALO, rows), :]
                        dst[pl.ds(off + HALO, n), :] = own_ref[pl.ds(ob + OBASE[level] + row, n, rows), :]
                        dst[pl.ds(off + HALO + n, HALO), :] = xr_ref[pl.ds(xb + XBASE[level] + row, HALO, rows), :]
            dst[pl.ds(yb + 276, 4), :] = jnp.zeros((4, LANES), F32)


def widen(field, own_ref, xl_ref, xr_ref, yl_ref, yr_ref, wide_ref):
    ob, xb, yb = field * OROWS, field * XROWS, field * YROWS
    for level in range(3):
        n, ring, rows = N[level], RING[level], OWN[level]
        for i in range(X[level]):
            if i < HALO:
                ref, at = xl_ref, xb + XBASE[level] + i * rows
            elif i < HALO + n:
                ref, at = own_ref, ob + OBASE[level] + (i - HALO) * rows
            else:
                ref, at = xr_ref, xb + XBASE[level] + (i - HALO - n) * rows
            for h in range(2):
                to = WBASE[level] + i * WIDE[level] + h * ring
                wide_ref[pl.ds(to, n), :] = ref[pl.ds(at + h * n, n), :]
                wide_ref[pl.ds(to + n, ring - n), :] = jnp.zeros((ring - n, LANES), F32)
        for h in range(2):
            for j in range(HALO):
                off = yb + YBASE[level] + (h * HALO + j) * X[level]
                to = WBASE[level] + h * ring
                wide_ref[pl.ds(to + n + j, X[level], WIDE[level]), :] = yr_ref[pl.ds(off, X[level]), :]
                wide_ref[pl.ds(to + ring - HALO + j, X[level], WIDE[level]), :] = yl_ref[pl.ds(off, X[level]), :]


def slab(ref, base, i, rows):
    return ref[pl.ds(pl.multiple_of(base + i * rows, 8), rows), :]


def put(ref, base, i, rows, value):
    ref[pl.ds(pl.multiple_of(base + i * rows, 8), rows), :] = value


def loop(low, high, value, store):
    groups = -(-(high - low) // UNROLL)
    size = -(-(high - low) // groups)
    lead = (high - low) - (groups - 1) * size

    def group(first, count):
        values = [value(first + u) for u in range(count)]
        for u in range(count):
            store(first + u, values[u])

    def step(g, carry):
        group(low + lead + g * size, size)
        return carry

    group(low, lead)
    if groups > 1:
        lax.fori_loop(0, groups - 1, step, 0)


def ring_sum(ref, base, i, ring, step):
    rows = 2 * ring
    mid = slab(ref, base, i, rows)
    total = slab(ref, base, i - 1, rows) + slab(ref, base, i + 1, rows) + (mid + mid)
    halves = []
    for h in range(2):
        t = total[h * ring : (h + 1) * ring]
        t = t + pltpu.roll(t, 1, 0)
        halves.append(t + pltpu.roll(t, ring - 1, 0))
    lane = lanes_of(ring)
    a, b = halves
    ra, rb = pltpu.roll(a, step, 1), pltpu.roll(b, step, 1)
    edge = lane < step
    a, b = a + jnp.where(edge, rb, ra), b + jnp.where(edge, ra, rb)
    ra, rb = pltpu.roll(a, LANES - step, 1), pltpu.roll(b, LANES - step, 1)
    edge = lane >= LANES - step
    a, b = a + jnp.where(edge, rb, ra), b + jnp.where(edge, ra, rb)
    return mid, a, b


def join(a, b):
    return jnp.concatenate([a, b], axis=0)


def sweeps(wide_b, wide_u, first, second):
    def sweep(edge, groups, src, dst):
        def value(level, i):
            rows, base = WIDE[level], WBASE[level]
            mid, a, b = ring_sum(src, base, i, RING[level], STEP[level])
            around = slab(wide_u, base, i, rows) * (join(a, b) - 8.0 * mid)
            return 0.2 * mid + slab(wide_b, base, i, rows) + around

        def group(g):
            done = []
            for level in range(3):
                high = X[level] - edge
                size = -(-(high - edge) // groups)
                start = jnp.minimum(edge + g * size, high - size)
                done += [(level, start + u, value(level, start + u)) for u in range(size)]
            for level, i, new in done:
                put(dst, WBASE[level], i, WIDE[level], new)

        pl.loop(0, groups)(group)

    sweep(1, GROUPS[0], wide_b, first)
    sweep(2, GROUPS[1], first, second)


def prolong(err, up3, up2):
    for q in range(6):
        for h in range(2):
            e3 = err[pl.ds(WBASE[2] + (q + 2) * 32 + h * 16, 16), :]
            to = q * 32 + h * 16
            up3[pl.ds(to, 5, 2), :] = e3[0:5]
            up3[pl.ds(to + 1, 5, 2), :] = e3[0:5]
            up3[pl.ds(to + 10, 4), :] = jnp.zeros((4, LANES), F32)
            up3[pl.ds(to + 14, 2), :] = jnp.broadcast_to(e3[15:16], (2, LANES))
    for a in range(10):
        for h in range(2):
            e2 = err[pl.ds(WBASE[1] + (a + 2) * 32 + h * 16, 16), :]
            e2 = e2 + up3[pl.ds(((a - 1) // 2 + 1) * 32 + h * 16, 16), :]
            to = a * 48 + h * 24
            up2[pl.ds(to, 9, 2), :] = e2[0:9]
            up2[pl.ds(to + 1, 9, 2), :] = e2[0:9]
            up2[pl.ds(to + 18, 4), :] = jnp.zeros((4, LANES), F32)
            up2[pl.ds(to + 22, 2), :] = jnp.broadcast_to(e2[15:16], (2, LANES))


def correct(err, up2, old_ref, sol_ref):
    for i in range(18):
        value = err[pl.ds((i + 2) * 48, 48), :] + up2[pl.ds(((i - 1) // 2 + 1) * 48, 48), :]
        if old_ref is not None:
            value = value + old_ref[pl.ds(i * 48, 48), :]
        sol_ref[pl.ds(i * 48, 48), :] = value


def first_round(
    raw_ref, own_ref, w_ref, xl_ref, xr_ref, yl_ref, yr_ref,
    next_ref, up_ref, down_ref, sol_ref, wide_u,
    wide_b, first, second, up3, up2, r_ref, tmp,
):
    widen(0, own_ref, xl_ref, xr_ref, yl_ref, yr_ref, wide_b)
    widen(1, own_ref, xl_ref, xr_ref, yl_ref, yr_ref, wide_u)
    sweeps(wide_b, wide_u, first, second)
    prolong(second, up3, up2)
    correct(second, up2, None, sol_ref)

    def resid(i):
        mid, a, b = ring_sum(sol_ref, 0, i + 1, 24, 1)
        halves = []
        for h, t in enumerate((a, b)):
            s = mid[h * 24 : h * 24 + 16]
            f = raw_ref[pl.ds(pl.multiple_of(i * 32 + h * 16, 16), 16), :]
            k = raw_ref[pl.ds(pl.multiple_of(OROWS + i * 32 + h * 16, 16), 16), :]
            halves.append(f - (k * (16.0 * s - 0.25 * t[:16]) + s))
        return join(*halves)

    loop(0, 16, resid, lambda i, new: put(r_ref, 0, i, 32, new))
    coarsen(r_ref, 0, 0, tmp, 0.125)
    coarsen(r_ref, 1, 0, tmp, 0.125)
    for at in range(0, OROWS, 32):
        next_ref[pl.ds(at, 32), :] = w_ref[pl.ds(at, 32), :] * r_ref[pl.ds(at, 32), :]
    x_faces(next_ref, 0, up_ref, down_ref, 0, LAYERS[0])


def second_round(
    fk_ref, own_ref, xl_ref, xr_ref, yl_ref, yr_ref, old_ref, wide_u,
    out_hbm, resid_hbm,
    wide_b, first, second, sol_ref, up3, up2, out_ref, resid_ref, sems,
):
    widen(0, own_ref, xl_ref, xr_ref, yl_ref, yr_ref, wide_b)
    sweeps(wide_b, wide_u, first, second)
    prolong(second, up3, up2)
    correct(second, up2, old_ref, sol_ref)
    for i in range(16):
        out_ref[pl.ds(16 * i, 16), :] = sol_ref[pl.ds(48 * (i + 1), 16), :]
    copies = [pltpu.make_async_copy(out_ref, out_hbm, sems.at[0])]
    copies[0].start()

    def resid(i):
        mid, a, _ = ring_sum(sol_ref, 0, i + 1, 24, 1)
        s = mid[:16]
        return slab(fk_ref, 0, i, 16) - (slab(fk_ref, 256, i, 16) * (16.0 * s - 0.25 * a[:16]) + s)

    for half in range(2):
        loop(8 * half, 8 * half + 8, resid, lambda i, new: put(resid_ref, 0, i, 16, new))
        at = pl.ds(128 * half, 128)
        copies.append(pltpu.make_async_copy(resid_ref.at[at, :], resid_hbm.at[at, :], sems.at[1 + half]))
        copies[-1].start()
    for copy in copies:
        copy.wait()


def exchange(up, down, axis):
    size = lax.axis_size(axis)
    odd = lax.axis_index(axis) % 2 == 1
    outer = [(i, i + 1) for i in range(1, size - 1, 2)]
    outer = outer + [(j, i) for i, j in outer]
    inner = [[i, i + 1] for i in range(0, size, 2)]
    two = lax.ppermute(jnp.where(odd, up, down), axis, outer)
    one = lax.all_gather(jnp.where(odd, down, up), axis, axis_index_groups=inner)
    return jnp.where(odd, one[0], two), jnp.where(odd, two, one[1])


def shards(forcing, kappa):
    shape = forcing.shape
    f = forcing.reshape(256, LANES)
    k = kappa.reshape(256, LANES)
    fk = lax.optimization_barrier(jnp.concatenate([f, k]))
    up, down = call(z_faces, [128, 128], [], fk)
    zl, zr = exchange(up, down, "grp")
    raw, own, w, up, down = call(
        begin, [2 * OROWS, 2 * OROWS, OROWS, PACKED[2], PACKED[2]], [256], fk, zl, zr
    )
    xl, xr = exchange(up, down, "gx")

    def faces(fields, own, xl, xr):
        def kernel(*refs):
            y_faces(fields, *refs)

        return call(kernel, [fields * YROWS] * 2 + [fields * XROWS] * 2, [], own, xl, xr)

    up, down, xl, xr = faces(2, own, xl, xr)
    yl, yr = exchange(up, down, "gy")
    own, up, down, sol, wide_u = call(
        first_round,
        [OROWS, PACKED[1], PACKED[1], SOLROWS, WROWS],
        [WROWS, WROWS, WROWS, 192, 480, OROWS, 256],
        raw, own, w, xl, xr, yl, yr,
    )
    xl, xr = exchange(up, down, "gx")
    up, down, xl, xr = faces(1, own, xl, xr)
    yl, yr = exchange(up, down, "gy")
    out, resid = call(
        second_round,
        [256, 256],
        [WROWS, WROWS, WROWS, SOLROWS, 192, 480, 256, 256],
        fk, own, xl, xr, yl, yr, sol, wide_u,
        out_specs=[HBM, HBM], copies=3,
    )
    return out.reshape(shape), resid.reshape(shape)


def solution(mesh):
    placed = (P("gx", "gy", "grp"), P("gx", "gy", "grp"))
    return jax.shard_map(shards, mesh=mesh, in_specs=placed, out_specs=placed, check_vma=False)
```

```python
import jax
import jax.numpy as jnp
from jax import lax
from jax.experimental import pallas as pl
from jax.experimental.pallas import tpu as pltpu
from jax.sharding import PartitionSpec as P

F32 = jnp.float32
LANES = 128
HALO = 3
N = (16, 8, 4)
X = tuple(n + 2 * HALO for n in N)
RING = (24, 16, 16)
STEP = (1, 2, 4)
OWN = tuple(2 * n for n in N)
WIDE = tuple(2 * r for r in RING)
OBASE = (0, 512, 640)
OROWS = 672
XBASE = (0, 96, 144)
XROWS = 168
YROWS = (0, 152, 256)
PACKED = (0, 96, 168)
LAYERS = (3, 2)
UNROLL = 8
GROUPS = (4, 3)
WBASE = (0, 1056, 1504)
WROWS = 1824
SOLROWS = 18 * 48
VMEM_LIMIT = 48 * 1024 * 1024


def lanes_of(rows):
    return lax.broadcasted_iota(jnp.int32, (rows, LANES), 1)


VM = pl.BlockSpec(memory_space=pltpu.VMEM)
HBM = pl.BlockSpec(memory_space=pl.ANY)


def call(kernel, outs, scratch, *args, out_specs=None, copies=0):
    return pl.pallas_call(
        kernel,
        out_shape=[jax.ShapeDtypeStruct((rows, LANES), F32) for rows in outs],
        in_specs=[VM] * len(args),
        out_specs=out_specs or [VM] * len(outs),
        scratch_shapes=[pltpu.VMEM((rows, LANES), F32) for rows in scratch]
        + ([pltpu.SemaphoreType.DMA((copies,))] if copies else []),
        compiler_params=pltpu.CompilerParams(vmem_limit_bytes=VMEM_LIMIT),
    )(*args)


def z_faces(fk_ref, up_ref, down_ref):
    quarter = lanes_of(16) // 32
    for field, ref in enumerate((fk_ref.at[pl.ds(0, 256), :], fk_ref.at[pl.ds(256, 256), :])):
        for g in range(4):
            slabs = [ref[pl.ds(16 * (4 * g + m), 16), :] for m in range(4)]
            up = pltpu.roll(slabs[0], 32, 1)
            down = slabs[0]
            for m in range(1, 4):
                shift = 32 * (m + 1) % LANES
                moved = pltpu.roll(slabs[m], shift, 1) if shift else slabs[m]
                up = jnp.where(quarter == m, moved, up)
                down = jnp.where(quarter == m, pltpu.roll(slabs[m], 32 * m, 1), down)
            at = pl.ds(64 * field + 16 * g, 16)
            up_ref[at, :] = up
            down_ref[at, :] = down


def coarsen(ref, level, base, tmp, scale):
    rows = OWN[level]
    half = rows // 2
    bit = STEP[level]
    even = (lanes_of(half) // bit) % 2 == 0
    for a in range(N[level] // 2):
        at = base + OBASE[level] + 2 * a * rows
        tmp[pl.ds(a * rows, rows), :] = ref[pl.ds(at, rows), :] + ref[pl.ds(at + rows, rows), :]
    for a in range(N[level] // 2):
        pair = tmp[pl.ds(a * rows, half, 2), :] + tmp[pl.ds(a * rows + 1, half, 2), :]
        other = jnp.where(even, pltpu.roll(pair, LANES - bit, 1), pltpu.roll(pair, bit, 1))
        ref[pl.ds(base + OBASE[level + 1] + a * half, half), :] = (pair + other) * scale


def x_faces(own_ref, base, up_ref, down_ref, xbase, count):
    lane = lanes_of(16)
    odd = lane % 2 == 1
    turn = lanes_of(8) % 4
    for dst, end in ((up_ref, 1), (down_ref, 0)):
        at = [base + OBASE[level] + end * (N[level] - count) * OWN[level] for level in range(3)]
        to = xbase
        for i in range(count):
            dst[pl.ds(to, 16), :] = own_ref[pl.ds(at[0] + 32 * i, 16), :]
            to += 16
        shared = own_ref[pl.ds(at[0] + 16, 16), :]
        for i in range(1, count):
            moved = pltpu.roll(own_ref[pl.ds(at[0] + 32 * i + 16, 16), :], 32 * i, 1)
            shared = jnp.where((lane + 16) // 32 == i, moved, shared)
        dst[pl.ds(to, 16), :] = shared
        c = [own_ref[pl.ds(at[1] + 16 * i, 16), :] for i in range(count)]
        dst[pl.ds(to + 16, 16), :] = jnp.where(odd, c[1], c[0])
        to += 32
        if count == 3:
            dst[pl.ds(to, 8), :] = jnp.where(odd[:8], c[2][8:], c[2][:8])
            to += 8
        c = [own_ref[pl.ds(at[2] + 8 * i, 8), :] for i in range(count)]
        shared = c[0]
        for i in range(1, count):
            shared = jnp.where(turn == i, c[i], shared)
        dst[pl.ds(to, 8), :] = shared


def unpack(src, at, dst, to, count, skip):
    odd = lanes_of(16) % 2 == 1
    turn = lanes_of(8) % 4
    for level in range(3):
        rows = OWN[level]
        for i in range(HALO):
            if not skip <= i < skip + count:
                dst[pl.ds(to + XBASE[level] + rows * i, rows), :] = jnp.zeros((rows, LANES), F32)
    to1, to2, to3 = (to + XBASE[level] + skip * OWN[level] for level in range(3))
    for i in range(count):
        dst[pl.ds(to1 + 32 * i, 16), :] = src[pl.ds(at, 16), :]
        at += 16
    shared = src[pl.ds(at, 16), :]
    for i in range(count):
        dst[pl.ds(to1 + 32 * i + 16, 16), :] = pltpu.roll(shared, LANES - 32 * i, 1) if i else shared

    def two(value):
        mask = odd[: value.shape[0]]
        return jnp.where(mask, pltpu.roll(value, 1, 1), value), jnp.where(mask, value, pltpu.roll(value, LANES - 1, 1))

    first = two(src[pl.ds(at + 16, 16), :])
    dst[pl.ds(to2, 16), :] = first[0]
    dst[pl.ds(to2 + 16, 16), :] = first[1]
    at += 32
    if count == 3:
        last = two(src[pl.ds(at, 8), :])
        dst[pl.ds(to2 + 32, 8), :] = last[0]
        dst[pl.ds(to2 + 40, 8), :] = last[1]
        at += 8
    c = src[pl.ds(at, 8), :]
    moved = {d: pltpu.roll(c, d % LANES, 1) if d else c for d in range(1 - count, 4)}
    for i in range(count):
        value = moved[-i]
        for lane in range(1, 4):
            value = jnp.where(turn == lane, moved[lane - i], value)
        dst[pl.ds(to3 + 8 * i, 8), :] = value


def begin(fk_ref, zl_ref, zr_ref, raw_ref, own_ref, w_ref, up_ref, down_ref, tmp):
    low = lanes_of(16) < 64
    for field, ref in enumerate((fk_ref.at[pl.ds(0, 256), :], fk_ref.at[pl.ds(256, 256), :])):
        base = field * OROWS
        for g in range(4):
            at = pl.ds(64 * field + 16 * g, 16)
            left, right = zl_ref[at, :], zr_ref[at, :]
            for m in range(4):
                slab = 4 * g + m
                shift_l, shift_r = (96 - 32 * m) % LANES, (-32 * m) % LANES
                from_l = pltpu.roll(left, shift_l, 1) if shift_l else left
                from_r = pltpu.roll(right, shift_r, 1) if shift_r else right
                raw_ref[pl.ds(base + 32 * slab, 16), :] = ref[pl.ds(16 * slab, 16), :]
                raw_ref[pl.ds(base + 32 * slab + 16, 16), :] = jnp.where(low, from_r, from_l)
        scale = 0.125 if field == 0 else 0.125 * 0.25
        coarsen(raw_ref, 0, base, tmp, scale)
        coarsen(raw_ref, 1, base, tmp, scale)
    for at in range(0, OROWS, 32):
        c = raw_ref[pl.ds(OROWS + at, 32), :]
        w = 0.8 / (14.0 * c + 1.0)
        w_ref[pl.ds(at, 32), :] = w
        own_ref[pl.ds(at, 32), :] = w * raw_ref[pl.ds(at, 32), :]
        own_ref[pl.ds(OROWS + at, 32), :] = 0.25 * (w * c)
    for field in range(2):
        x_faces(own_ref, field * OROWS, up_ref, down_ref, PACKED[field], LAYERS[field])


def y_parts(count):
    parts, at = [], 0
    for j in range(count):
        parts.append((at, 0, ((0, j),), None))
        at += X[0]
    parts.append((at, 0, tuple((1, j) for j in range(count)), "lanes"))
    at += X[0]
    for j in range(count):
        parts.append((at, 1, ((0, j), (1, j)), "turns"))
        at += X[1]
    for j in range(0, count, 2):
        members = tuple((h, k) for k in range(j, min(j + 2, count)) for h in range(2))
        parts.append((at, 2, members, "turns"))
        at += X[2]
    return parts


def share(vectors, how):
    shared = vectors[0]
    lane = lanes_of(shared.shape[0])
    for i in range(1, len(vectors)):
        if how == "lanes":
            shared = jnp.where((lane + 16) // 32 == i, pltpu.roll(vectors[i], 32 * i, 1), shared)
        else:
            shared = jnp.where(lane % len(vectors) == i, vectors[i], shared)
    return shared


def unshare(shared, number, how):
    if how != "turns":
        return [pltpu.roll(shared, LANES - 32 * i, 1) if i else shared for i in range(number)]
    turn = lanes_of(shared.shape[0]) % number
    moved = {d: pltpu.roll(shared, d % LANES, 1) if d else shared for d in range(1 - number, number)}
    vectors = []
    for i in range(number):
        value = moved[-i]
        for lane in range(1, number):
            value = jnp.where(turn == lane, moved[lane - i], value)
        vectors.append(value)
    return vectors


def y_faces(fields, own_ref, xl_packed, xr_packed, up_ref, down_ref, xl_ref, xr_ref, rows_ref):
    for ref in (up_ref, down_ref):
        ref[pl.ds(150, 2), :] = jnp.zeros((2, LANES), F32)
    for field in range(fields):
        ob, xb, yb, count = field * OROWS, field * XROWS, YROWS[field], LAYERS[field]
        unpack(xl_packed, PACKED[field], xl_ref, xb, count, HALO - count)
        unpack(xr_packed, PACKED[field], xr_ref, xb, count, 0)
        for side, (dst, first) in enumerate(((up_ref, False), (down_ref, True))):
            for at, level, members, how in y_parts(count):
                n, rows, size = N[level], OWN[level], X[level]
                vectors = []
                for m, (h, j) in enumerate(members):
                    row = h * n + (j if first else n - count + j)
                    to = 24 * (m + 4 * (side + 2 * field))
                    if len(members) == 1:
                        ref, to = dst, yb + at
                    else:
                        ref = rows_ref
                    ref[pl.ds(to, HALO), :] = xl_ref[pl.ds(xb + XBASE[level] + row, HALO, rows), :]
                    ref[pl.ds(to + HALO, n), :] = own_ref[pl.ds(ob + OBASE[level] + row, n, rows), :]
                    ref[pl.ds(to + HALO + n, HALO), :] = xr_ref[pl.ds(xb + XBASE[level] + row, HALO, rows), :]
                    if len(members) > 1:
                        vectors.append(ref[pl.ds(to, size), :])
                if vectors:
                    dst[pl.ds(yb + at, size), :] = share(vectors, how)


def widen(field, own_ref, xl_ref, xr_ref, yl_ref, yr_ref, wide_ref):
    ob, xb, yb, count = field * OROWS, field * XROWS, YROWS[field], LAYERS[field]
    for level in range(3):
        n, ring, rows = N[level], RING[level], OWN[level]
        for i in range(X[level]):
            if i < HALO:
                ref, at = xl_ref, xb + XBASE[level] + i * rows
            elif i < HALO + n:
                ref, at = own_ref, ob + OBASE[level] + (i - HALO) * rows
            else:
                ref, at = xr_ref, xb + XBASE[level] + (i - HALO - n) * rows
            for h in range(2):
                to = WBASE[level] + i * WIDE[level] + h * ring
                wide_ref[pl.ds(to, n), :] = ref[pl.ds(at + h * n, n), :]
                wide_ref[pl.ds(to + n, ring - n), :] = jnp.zeros((ring - n, LANES), F32)
    for at, level, members, how in y_parts(count):
        n, ring, size = N[level], RING[level], X[level]
        for ref, start in ((yr_ref, n), (yl_ref, ring - count)):
            shared = ref[pl.ds(yb + at, size), :]
            for (h, j), vector in zip(members, unshare(shared, len(members), how)):
                wide_ref[pl.ds(WBASE[level] + h * ring + start + j, size, WIDE[level]), :] = vector


def slab(ref, base, i, rows):
    return ref[pl.ds(pl.multiple_of(base + i * rows, 8), rows), :]


def put(ref, base, i, rows, value):
    ref[pl.ds(pl.multiple_of(base + i * rows, 8), rows), :] = value


def loop(low, high, value, store):
    groups = -(-(high - low) // UNROLL)
    size = -(-(high - low) // groups)
    lead = (high - low) - (groups - 1) * size

    def group(first, count):
        values = [value(first + u) for u in range(count)]
        for u in range(count):
            store(first + u, values[u])

    def step(g, carry):
        group(low + lead + g * size, size)
        return carry

    group(low, lead)
    if groups > 1:
        lax.fori_loop(0, groups - 1, step, 0)


def ring_sum(ref, base, i, ring, step):
    rows = 2 * ring
    mid = slab(ref, base, i, rows)
    total = slab(ref, base, i - 1, rows) + slab(ref, base, i + 1, rows) + (mid + mid)
    halves = []
    for h in range(2):
        t = total[h * ring : (h + 1) * ring]
        t = t + pltpu.roll(t, 1, 0)
        halves.append(t + pltpu.roll(t, ring - 1, 0))
    lane = lanes_of(ring)
    a, b = halves
    ra, rb = pltpu.roll(a, step, 1), pltpu.roll(b, step, 1)
    edge = lane < step
    a, b = a + jnp.where(edge, rb, ra), b + jnp.where(edge, ra, rb)
    ra, rb = pltpu.roll(a, LANES - step, 1), pltpu.roll(b, LANES - step, 1)
    edge = lane >= LANES - step
    a, b = a + jnp.where(edge, rb, ra), b + jnp.where(edge, ra, rb)
    return mid, a, b


def join(a, b):
    return jnp.concatenate([a, b], axis=0)


def sweeps(wide_b, wide_u, first, second):
    def sweep(edge, groups, src, dst):
        def value(level, i):
            rows, base = WIDE[level], WBASE[level]
            mid, a, b = ring_sum(src, base, i, RING[level], STEP[level])
            around = slab(wide_u, base, i, rows) * (join(a, b) - 8.0 * mid)
            return 0.2 * mid + slab(wide_b, base, i, rows) + around

        def group(g):
            done = []
            for level in range(3):
                high = X[level] - edge
                size = -(-(high - edge) // groups)
                start = jnp.minimum(edge + g * size, high - size)
                done += [(level, start + u, value(level, start + u)) for u in range(size)]
            for level, i, new in done:
                put(dst, WBASE[level], i, WIDE[level], new)

        pl.loop(0, groups)(group)

    sweep(1, GROUPS[0], wide_b, first)
    sweep(2, GROUPS[1], first, second)


def prolong(err, up3, up2):
    for q in range(6):
        for h in range(2):
            e3 = err[pl.ds(WBASE[2] + (q + 2) * 32 + h * 16, 16), :]
            to = q * 32 + h * 16
            up3[pl.ds(to, 5, 2), :] = e3[0:5]
            up3[pl.ds(to + 1, 5, 2), :] = e3[0:5]
            up3[pl.ds(to + 10, 4), :] = jnp.zeros((4, LANES), F32)
            up3[pl.ds(to + 14, 2), :] = jnp.broadcast_to(e3[15:16], (2, LANES))
    for a in range(10):
        for h in range(2):
            e2 = err[pl.ds(WBASE[1] + (a + 2) * 32 + h * 16, 16), :]
            e2 = e2 + up3[pl.ds(((a - 1) // 2 + 1) * 32 + h * 16, 16), :]
            to = a * 48 + h * 24
            up2[pl.ds(to, 9, 2), :] = e2[0:9]
            up2[pl.ds(to + 1, 9, 2), :] = e2[0:9]
            up2[pl.ds(to + 18, 4), :] = jnp.zeros((4, LANES), F32)
            up2[pl.ds(to + 22, 2), :] = jnp.broadcast_to(e2[15:16], (2, LANES))


def correct(err, up2, old_ref, sol_ref):
    for i in range(18):
        value = err[pl.ds((i + 2) * 48, 48), :] + up2[pl.ds(((i - 1) // 2 + 1) * 48, 48), :]
        if old_ref is not None:
            value = value + old_ref[pl.ds(i * 48, 48), :]
        sol_ref[pl.ds(i * 48, 48), :] = value


def first_round(
    raw_ref, own_ref, w_ref, xl_ref, xr_ref, yl_ref, yr_ref,
    next_ref, up_ref, down_ref, sol_ref, wide_u,
    wide_b, first, second, up3, up2, r_ref, tmp,
):
    widen(0, own_ref, xl_ref, xr_ref, yl_ref, yr_ref, wide_b)
    widen(1, own_ref, xl_ref, xr_ref, yl_ref, yr_ref, wide_u)
    sweeps(wide_b, wide_u, first, second)
    prolong(second, up3, up2)
    correct(second, up2, None, sol_ref)

    def resid(i):
        mid, a, b = ring_sum(sol_ref, 0, i + 1, 24, 1)
        halves = []
        for h, t in enumerate((a, b)):
            s = mid[h * 24 : h * 24 + 16]
            f = raw_ref[pl.ds(pl.multiple_of(i * 32 + h * 16, 16), 16), :]
            k = raw_ref[pl.ds(pl.multiple_of(OROWS + i * 32 + h * 16, 16), 16), :]
            halves.append(f - (k * (16.0 * s - 0.25 * t[:16]) + s))
        return join(*halves)

    loop(0, 16, resid, lambda i, new: put(r_ref, 0, i, 32, new))
    coarsen(r_ref, 0, 0, tmp, 0.125)
    coarsen(r_ref, 1, 0, tmp, 0.125)
    for at in range(0, OROWS, 32):
        next_ref[pl.ds(at, 32), :] = w_ref[pl.ds(at, 32), :] * r_ref[pl.ds(at, 32), :]
    x_faces(next_ref, 0, up_ref, down_ref, 0, LAYERS[0])


def second_round(
    fk_ref, own_ref, xl_ref, xr_ref, yl_ref, yr_ref, old_ref, wide_u,
    out_hbm, resid_hbm,
    wide_b, first, second, sol_ref, up3, up2, out_ref, resid_ref, sems,
):
    widen(0, own_ref, xl_ref, xr_ref, yl_ref, yr_ref, wide_b)
    sweeps(wide_b, wide_u, first, second)
    prolong(second, up3, up2)
    correct(second, up2, old_ref, sol_ref)
    for i in range(16):
        out_ref[pl.ds(16 * i, 16), :] = sol_ref[pl.ds(48 * (i + 1), 16), :]
    copies = [pltpu.make_async_copy(out_ref, out_hbm, sems.at[0])]
    copies[0].start()

    def resid(i):
        mid, a, _ = ring_sum(sol_ref, 0, i + 1, 24, 1)
        s = mid[:16]
        return slab(fk_ref, 0, i, 16) - (slab(fk_ref, 256, i, 16) * (16.0 * s - 0.25 * a[:16]) + s)

    for half in range(2):
        loop(8 * half, 8 * half + 8, resid, lambda i, new: put(resid_ref, 0, i, 16, new))
        at = pl.ds(128 * half, 128)
        copies.append(pltpu.make_async_copy(resid_ref.at[at, :], resid_hbm.at[at, :], sems.at[1 + half]))
        copies[-1].start()
    for copy in copies:
        copy.wait()


def exchange(up, down, axis):
    size = lax.axis_size(axis)
    odd = lax.axis_index(axis) % 2 == 1
    outer = [(i, i + 1) for i in range(1, size - 1, 2)]
    outer = outer + [(j, i) for i, j in outer]
    inner = [[i, i + 1] for i in range(0, size, 2)]
    two = lax.ppermute(jnp.where(odd, up, down), axis, outer)
    one = lax.all_gather(jnp.where(odd, down, up), axis, axis_index_groups=inner)
    return jnp.where(odd, one[0], two), jnp.where(odd, two, one[1])


def shards(forcing, kappa):
    shape = forcing.shape
    f = forcing.reshape(256, LANES)
    k = kappa.reshape(256, LANES)
    fk = lax.optimization_barrier(jnp.concatenate([f, k]))
    up, down = call(z_faces, [128, 128], [], fk)
    zl, zr = exchange(up, down, "grp")
    raw, own, w, up, down = call(
        begin, [2 * OROWS, 2 * OROWS, OROWS, PACKED[2], PACKED[2]], [256], fk, zl, zr
    )
    xl, xr = exchange(up, down, "gx")

    def faces(fields, own, xl, xr):
        def kernel(*refs):
            y_faces(fields, *refs)

        return call(kernel, [YROWS[fields]] * 2 + [fields * XROWS] * 2, [24 * 16], own, xl, xr)

    up, down, xl, xr = faces(2, own, xl, xr)
    yl, yr = exchange(up, down, "gy")
    own, up, down, sol, wide_u = call(
        first_round,
        [OROWS, PACKED[1], PACKED[1], SOLROWS, WROWS],
        [WROWS, WROWS, WROWS, 192, 480, OROWS, 256],
        raw, own, w, xl, xr, yl, yr,
    )
    xl, xr = exchange(up, down, "gx")
    up, down, xl, xr = faces(1, own, xl, xr)
    yl, yr = exchange(up, down, "gy")
    out, resid = call(
        second_round,
        [256, 256],
        [WROWS, WROWS, WROWS, SOLROWS, 192, 480, 256, 256],
        fk, own, xl, xr, yl, yr, sol, wide_u,
        out_specs=[HBM, HBM], copies=3,
    )
    return out.reshape(shape), resid.reshape(shape)


def solution(mesh):
    placed = (P("gx", "gy", "grp"), P("gx", "gy", "grp"))
    return jax.shard_map(shards, mesh=mesh, in_specs=placed, out_specs=placed, check_vma=False)
```

```python
import jax
import jax.numpy as jnp
from jax import lax
from jax.experimental import pallas as pl
from jax.experimental.pallas import tpu as pltpu
from jax.sharding import PartitionSpec as P

F32 = jnp.float32
LANES = 128
HALO = 3
N = (16, 8, 4)
X = tuple(n + 2 * HALO for n in N)
RING = (24, 16, 16)
STEP = (1, 2, 4)
OWN = tuple(2 * n for n in N)
WIDE = tuple(2 * r for r in RING)
OBASE = (0, 512, 640)
OROWS = 672
XBASE = (0, 96, 144)
XROWS = 168
YROWS = (0, 152, 256)
PACKED = (0, 96, 168)
LAYERS = (3, 2)
UNROLL = 8
GROUPS = (3, 3)
WBASE = (0, 1056, 1504)
WROWS = 1824
SOLROWS = 18 * 48
VMEM_LIMIT = 48 * 1024 * 1024


def lanes_of(rows):
    return lax.broadcasted_iota(jnp.int32, (rows, LANES), 1)


VM = pl.BlockSpec(memory_space=pltpu.VMEM)
HBM = pl.BlockSpec(memory_space=pl.ANY)


def call(kernel, outs, scratch, *args, out_specs=None, copies=0):
    return pl.pallas_call(
        kernel,
        out_shape=[jax.ShapeDtypeStruct((rows, LANES), F32) for rows in outs],
        in_specs=[VM] * len(args),
        out_specs=out_specs or [VM] * len(outs),
        scratch_shapes=[pltpu.VMEM((rows, LANES), F32) for rows in scratch]
        + ([pltpu.SemaphoreType.DMA((copies,))] if copies else []),
        compiler_params=pltpu.CompilerParams(vmem_limit_bytes=VMEM_LIMIT),
    )(*args)


def z_faces(fk_ref, up_ref, down_ref):
    quarter = lanes_of(16) // 32
    for field, ref in enumerate((fk_ref.at[pl.ds(0, 256), :], fk_ref.at[pl.ds(256, 256), :])):
        for g in range(4):
            slabs = [ref[pl.ds(16 * (4 * g + m), 16), :] for m in range(4)]
            up = pltpu.roll(slabs[0], 32, 1)
            down = slabs[0]
            for m in range(1, 4):
                shift = 32 * (m + 1) % LANES
                moved = pltpu.roll(slabs[m], shift, 1) if shift else slabs[m]
                up = jnp.where(quarter == m, moved, up)
                down = jnp.where(quarter == m, pltpu.roll(slabs[m], 32 * m, 1), down)
            at = pl.ds(64 * field + 16 * g, 16)
            up_ref[at, :] = up
            down_ref[at, :] = down


def coarsen(ref, level, base, tmp, scale):
    rows = OWN[level]
    half = rows // 2
    bit = STEP[level]
    even = (lanes_of(half) // bit) % 2 == 0
    for a in range(N[level] // 2):
        at = base + OBASE[level] + 2 * a * rows
        tmp[pl.ds(a * rows, rows), :] = ref[pl.ds(at, rows), :] + ref[pl.ds(at + rows, rows), :]
    for a in range(N[level] // 2):
        pair = tmp[pl.ds(a * rows, half, 2), :] + tmp[pl.ds(a * rows + 1, half, 2), :]
        other = jnp.where(even, pltpu.roll(pair, LANES - bit, 1), pltpu.roll(pair, bit, 1))
        ref[pl.ds(base + OBASE[level + 1] + a * half, half), :] = (pair + other) * scale


def x_faces(own_ref, base, up_ref, down_ref, xbase, count):
    lane = lanes_of(16)
    odd = lane % 2 == 1
    turn = lanes_of(8) % 4
    for dst, end in ((up_ref, 1), (down_ref, 0)):
        at = [base + OBASE[level] + end * (N[level] - count) * OWN[level] for level in range(3)]
        to = xbase
        for i in range(count):
            dst[pl.ds(to, 16), :] = own_ref[pl.ds(at[0] + 32 * i, 16), :]
            to += 16
        shared = own_ref[pl.ds(at[0] + 16, 16), :]
        for i in range(1, count):
            moved = pltpu.roll(own_ref[pl.ds(at[0] + 32 * i + 16, 16), :], 32 * i, 1)
            shared = jnp.where((lane + 16) // 32 == i, moved, shared)
        dst[pl.ds(to, 16), :] = shared
        c = [own_ref[pl.ds(at[1] + 16 * i, 16), :] for i in range(count)]
        dst[pl.ds(to + 16, 16), :] = jnp.where(odd, c[1], c[0])
        to += 32
        if count == 3:
            dst[pl.ds(to, 8), :] = jnp.where(odd[:8], c[2][8:], c[2][:8])
            to += 8
        c = [own_ref[pl.ds(at[2] + 8 * i, 8), :] for i in range(count)]
        shared = c[0]
        for i in range(1, count):
            shared = jnp.where(turn == i, c[i], shared)
        dst[pl.ds(to, 8), :] = shared


def unpack(src, at, dst, to, count, skip):
    odd = lanes_of(16) % 2 == 1
    turn = lanes_of(8) % 4
    for level in range(3):
        rows = OWN[level]
        for i in range(HALO):
            if not skip <= i < skip + count:
                dst[pl.ds(to + XBASE[level] + rows * i, rows), :] = jnp.zeros((rows, LANES), F32)
    to1, to2, to3 = (to + XBASE[level] + skip * OWN[level] for level in range(3))
    for i in range(count):
        dst[pl.ds(to1 + 32 * i, 16), :] = src[pl.ds(at, 16), :]
        at += 16
    shared = src[pl.ds(at, 16), :]
    for i in range(count):
        dst[pl.ds(to1 + 32 * i + 16, 16), :] = pltpu.roll(shared, LANES - 32 * i, 1) if i else shared

    def two(value):
        mask = odd[: value.shape[0]]
        return jnp.where(mask, pltpu.roll(value, 1, 1), value), jnp.where(mask, value, pltpu.roll(value, LANES - 1, 1))

    first = two(src[pl.ds(at + 16, 16), :])
    dst[pl.ds(to2, 16), :] = first[0]
    dst[pl.ds(to2 + 16, 16), :] = first[1]
    at += 32
    if count == 3:
        last = two(src[pl.ds(at, 8), :])
        dst[pl.ds(to2 + 32, 8), :] = last[0]
        dst[pl.ds(to2 + 40, 8), :] = last[1]
        at += 8
    c = src[pl.ds(at, 8), :]
    moved = {d: pltpu.roll(c, d % LANES, 1) if d else c for d in range(1 - count, 4)}
    for i in range(count):
        value = moved[-i]
        for lane in range(1, 4):
            value = jnp.where(turn == lane, moved[lane - i], value)
        dst[pl.ds(to3 + 8 * i, 8), :] = value


def begin(fk_ref, zl_ref, zr_ref, raw_ref, own_ref, w_ref, up_ref, down_ref, tmp):
    low = lanes_of(16) < 64
    for field, ref in enumerate((fk_ref.at[pl.ds(0, 256), :], fk_ref.at[pl.ds(256, 256), :])):
        base = field * OROWS
        for g in range(4):
            at = pl.ds(64 * field + 16 * g, 16)
            left, right = zl_ref[at, :], zr_ref[at, :]
            for m in range(4):
                slab = 4 * g + m
                shift_l, shift_r = (96 - 32 * m) % LANES, (-32 * m) % LANES
                from_l = pltpu.roll(left, shift_l, 1) if shift_l else left
                from_r = pltpu.roll(right, shift_r, 1) if shift_r else right
                raw_ref[pl.ds(base + 32 * slab, 16), :] = ref[pl.ds(16 * slab, 16), :]
                raw_ref[pl.ds(base + 32 * slab + 16, 16), :] = jnp.where(low, from_r, from_l)
        scale = 0.125 if field == 0 else 0.125 * 0.25
        coarsen(raw_ref, 0, base, tmp, scale)
        coarsen(raw_ref, 1, base, tmp, scale)
    for at in range(0, OROWS, 32):
        c = raw_ref[pl.ds(OROWS + at, 32), :]
        w = 0.8 / (14.0 * c + 1.0)
        w_ref[pl.ds(at, 32), :] = w
        own_ref[pl.ds(at, 32), :] = w * raw_ref[pl.ds(at, 32), :]
        own_ref[pl.ds(OROWS + at, 32), :] = 0.25 * (w * c)
    for field in range(2):
        x_faces(own_ref, field * OROWS, up_ref, down_ref, PACKED[field], LAYERS[field])


def y_parts(count):
    parts, at = [], 0
    for j in range(count):
        parts.append((at, 0, ((0, j),), None))
        at += X[0]
    parts.append((at, 0, tuple((1, j) for j in range(count)), "lanes"))
    at += X[0]
    for j in range(count):
        parts.append((at, 1, ((0, j), (1, j)), "turns"))
        at += X[1]
    for j in range(0, count, 2):
        members = tuple((h, k) for k in range(j, min(j + 2, count)) for h in range(2))
        parts.append((at, 2, members, "turns"))
        at += X[2]
    return parts


def share(vectors, how):
    shared = vectors[0]
    lane = lanes_of(shared.shape[0])
    for i in range(1, len(vectors)):
        if how == "lanes":
            shared = jnp.where((lane + 16) // 32 == i, pltpu.roll(vectors[i], 32 * i, 1), shared)
        else:
            shared = jnp.where(lane % len(vectors) == i, vectors[i], shared)
    return shared


def unshare(shared, number, how):
    if how != "turns":
        return [pltpu.roll(shared, LANES - 32 * i, 1) if i else shared for i in range(number)]
    turn = lanes_of(shared.shape[0]) % number
    moved = {d: pltpu.roll(shared, d % LANES, 1) if d else shared for d in range(1 - number, number)}
    vectors = []
    for i in range(number):
        value = moved[-i]
        for lane in range(1, number):
            value = jnp.where(turn == lane, moved[lane - i], value)
        vectors.append(value)
    return vectors


def y_faces(fields, own_ref, xl_packed, xr_packed, up_ref, down_ref, xl_ref, xr_ref, rows_ref):
    for ref in (up_ref, down_ref):
        ref[pl.ds(150, 2), :] = jnp.zeros((2, LANES), F32)
    for field in range(fields):
        ob, xb, yb, count = field * OROWS, field * XROWS, YROWS[field], LAYERS[field]
        unpack(xl_packed, PACKED[field], xl_ref, xb, count, HALO - count)
        unpack(xr_packed, PACKED[field], xr_ref, xb, count, 0)
        for side, (dst, first) in enumerate(((up_ref, False), (down_ref, True))):
            for at, level, members, how in y_parts(count):
                n, rows, size = N[level], OWN[level], X[level]
                vectors = []
                for m, (h, j) in enumerate(members):
                    row = h * n + (j if first else n - count + j)
                    to = 24 * (m + 4 * (side + 2 * field))
                    if len(members) == 1:
                        ref, to = dst, yb + at
                    else:
                        ref = rows_ref
                    ref[pl.ds(to, HALO), :] = xl_ref[pl.ds(xb + XBASE[level] + row, HALO, rows), :]
                    ref[pl.ds(to + HALO, n), :] = own_ref[pl.ds(ob + OBASE[level] + row, n, rows), :]
                    ref[pl.ds(to + HALO + n, HALO), :] = xr_ref[pl.ds(xb + XBASE[level] + row, HALO, rows), :]
                    if len(members) > 1:
                        vectors.append(ref[pl.ds(to, size), :])
                if vectors:
                    dst[pl.ds(yb + at, size), :] = share(vectors, how)


def widen(field, own_ref, xl_ref, xr_ref, yl_ref, yr_ref, wide_ref):
    ob, xb, yb, count = field * OROWS, field * XROWS, YROWS[field], LAYERS[field]
    for level in range(3):
        n, ring, rows = N[level], RING[level], OWN[level]
        for i in range(X[level]):
            if i < HALO:
                ref, at = xl_ref, xb + XBASE[level] + i * rows
            elif i < HALO + n:
                ref, at = own_ref, ob + OBASE[level] + (i - HALO) * rows
            else:
                ref, at = xr_ref, xb + XBASE[level] + (i - HALO - n) * rows
            for h in range(2):
                to = WBASE[level] + i * WIDE[level] + h * ring
                wide_ref[pl.ds(to, n), :] = ref[pl.ds(at + h * n, n), :]
    for at, level, members, how in y_parts(count):
        n, ring, size = N[level], RING[level], X[level]
        for ref, start in ((yr_ref, n), (yl_ref, ring - count)):
            shared = ref[pl.ds(yb + at, size), :]
            for (h, j), vector in zip(members, unshare(shared, len(members), how)):
                wide_ref[pl.ds(WBASE[level] + h * ring + start + j, size, WIDE[level]), :] = vector


def slab(ref, base, i, rows):
    return ref[pl.ds(pl.multiple_of(base + i * rows, 8), rows), :]


def put(ref, base, i, rows, value):
    ref[pl.ds(pl.multiple_of(base + i * rows, 8), rows), :] = value


def loop(low, high, value, store):
    groups = -(-(high - low) // UNROLL)
    size = -(-(high - low) // groups)
    lead = (high - low) - (groups - 1) * size

    def group(first, count):
        values = [value(first + u) for u in range(count)]
        for u in range(count):
            store(first + u, values[u])

    def step(g, carry):
        group(low + lead + g * size, size)
        return carry

    group(low, lead)
    if groups > 1:
        lax.fori_loop(0, groups - 1, step, 0)


def ring_sum(ref, base, i, ring, step):
    rows = 2 * ring
    mid = slab(ref, base, i, rows)
    total = slab(ref, base, i - 1, rows) + slab(ref, base, i + 1, rows) + (mid + mid)
    halves = []
    for h in range(2):
        t = total[h * ring : (h + 1) * ring]
        halves.append(pltpu.roll(t, 1, 0) + pltpu.roll(t, ring - 1, 0) + (t + t))
    lane = lanes_of(ring)
    a, b = halves
    ra, rb = pltpu.roll(a, step, 1), pltpu.roll(b, step, 1)
    sa, sb = pltpu.roll(a, LANES - step, 1), pltpu.roll(b, LANES - step, 1)
    low, high = lane < step, lane >= LANES - step
    new_a = a + a + jnp.where(low, rb, ra) + jnp.where(high, sb, sa)
    new_b = b + b + jnp.where(low, ra, rb) + jnp.where(high, sa, sb)
    return mid, new_a, new_b


def join(a, b):
    return jnp.concatenate([a, b], axis=0)


def sweeps(wide_b, wide_u, first, second):
    def sweep(edge, groups, src, dst):
        def value(level, i):
            rows, base = WIDE[level], WBASE[level]
            mid, a, b = ring_sum(src, base, i, RING[level], STEP[level])
            around = slab(wide_u, base, i, rows) * (join(a, b) - 8.0 * mid)
            return 0.2 * mid + slab(wide_b, base, i, rows) + around

        def group(g):
            done = []
            for level in range(3):
                high = X[level] - edge
                size = -(-(high - edge) // groups)
                start = jnp.minimum(edge + g * size, high - size)
                done += [(level, start + u, value(level, start + u)) for u in range(size)]
            for level, i, new in done:
                put(dst, WBASE[level], i, WIDE[level], new)

        pl.loop(0, groups)(group)

    sweep(1, GROUPS[0], wide_b, first)
    sweep(2, GROUPS[1], first, second)


def prolong(err, up3, up2):
    for q in range(6):
        for h in range(2):
            e3 = err[pl.ds(WBASE[2] + (q + 2) * 32 + h * 16, 16), :]
            to = q * 32 + h * 16
            up3[pl.ds(to, 5, 2), :] = e3[0:5]
            up3[pl.ds(to + 1, 5, 2), :] = e3[0:5]
            up3[pl.ds(to + 10, 4), :] = jnp.zeros((4, LANES), F32)
            up3[pl.ds(to + 14, 2), :] = jnp.broadcast_to(e3[15:16], (2, LANES))
    for a in range(10):
        for h in range(2):
            e2 = err[pl.ds(WBASE[1] + (a + 2) * 32 + h * 16, 16), :]
            e2 = e2 + up3[pl.ds(((a - 1) // 2 + 1) * 32 + h * 16, 16), :]
            to = a * 48 + h * 24
            up2[pl.ds(to, 9, 2), :] = e2[0:9]
            up2[pl.ds(to + 1, 9, 2), :] = e2[0:9]
            up2[pl.ds(to + 18, 4), :] = jnp.zeros((4, LANES), F32)
            up2[pl.ds(to + 22, 2), :] = jnp.broadcast_to(e2[15:16], (2, LANES))


def correct(err, up2, old_ref, sol_ref):
    for i in range(18):
        value = err[pl.ds((i + 2) * 48, 48), :] + up2[pl.ds(((i - 1) // 2 + 1) * 48, 48), :]
        if old_ref is not None:
            value = value + old_ref[pl.ds(i * 48, 48), :]
        sol_ref[pl.ds(i * 48, 48), :] = value


def first_round(
    raw_ref, own_ref, w_ref, xl_ref, xr_ref, yl_ref, yr_ref,
    next_ref, up_ref, down_ref, sol_ref, wide_u,
    wide_b, first, second, up3, up2, r_ref, tmp,
):
    widen(0, own_ref, xl_ref, xr_ref, yl_ref, yr_ref, wide_b)
    widen(1, own_ref, xl_ref, xr_ref, yl_ref, yr_ref, wide_u)
    sweeps(wide_b, wide_u, first, second)
    prolong(second, up3, up2)
    correct(second, up2, None, sol_ref)

    def resid(i):
        mid, a, b = ring_sum(sol_ref, 0, i + 1, 24, 1)
        halves = []
        for h, t in enumerate((a, b)):
            s = mid[h * 24 : h * 24 + 16]
            f = raw_ref[pl.ds(pl.multiple_of(i * 32 + h * 16, 16), 16), :]
            k = raw_ref[pl.ds(pl.multiple_of(OROWS + i * 32 + h * 16, 16), 16), :]
            halves.append(f - (k * (16.0 * s - 0.25 * t[:16]) + s))
        return join(*halves)

    loop(0, 16, resid, lambda i, new: put(r_ref, 0, i, 32, new))
    coarsen(r_ref, 0, 0, tmp, 0.125)
    coarsen(r_ref, 1, 0, tmp, 0.125)
    for at in range(0, OROWS, 32):
        next_ref[pl.ds(at, 32), :] = w_ref[pl.ds(at, 32), :] * r_ref[pl.ds(at, 32), :]
    x_faces(next_ref, 0, up_ref, down_ref, 0, LAYERS[0])


def second_round(
    fk_ref, own_ref, xl_ref, xr_ref, yl_ref, yr_ref, old_ref, wide_u,
    out_hbm, resid_hbm,
    wide_b, first, second, sol_ref, up3, up2, out_ref, resid_ref, sems,
):
    widen(0, own_ref, xl_ref, xr_ref, yl_ref, yr_ref, wide_b)
    sweeps(wide_b, wide_u, first, second)
    prolong(second, up3, up2)
    correct(second, up2, old_ref, sol_ref)
    for i in range(16):
        out_ref[pl.ds(16 * i, 16), :] = sol_ref[pl.ds(48 * (i + 1), 16), :]
    copies = [pltpu.make_async_copy(out_ref, out_hbm, sems.at[0])]
    copies[0].start()

    def resid(i):
        mid, a, _ = ring_sum(sol_ref, 0, i + 1, 24, 1)
        s = mid[:16]
        return slab(fk_ref, 0, i, 16) - (slab(fk_ref, 256, i, 16) * (16.0 * s - 0.25 * a[:16]) + s)

    for half in range(2):
        loop(8 * half, 8 * half + 8, resid, lambda i, new: put(resid_ref, 0, i, 16, new))
        at = pl.ds(128 * half, 128)
        copies.append(pltpu.make_async_copy(resid_ref.at[at, :], resid_hbm.at[at, :], sems.at[1 + half]))
        copies[-1].start()
    for copy in copies:
        copy.wait()


def exchange(up, down, axis):
    size = lax.axis_size(axis)
    odd = lax.axis_index(axis) % 2 == 1
    outer = [(i, i + 1) for i in range(1, size - 1, 2)]
    outer = outer + [(j, i) for i, j in outer]
    inner = [[i, i + 1] for i in range(0, size, 2)]
    two = lax.ppermute(jnp.where(odd, up, down), axis, outer)
    one = lax.all_gather(jnp.where(odd, down, up), axis, axis_index_groups=inner)
    return jnp.where(odd, one[0], two), jnp.where(odd, two, one[1])


def shards(forcing, kappa):
    shape = forcing.shape
    f = forcing.reshape(256, LANES)
    k = kappa.reshape(256, LANES)
    fk = lax.optimization_barrier(jnp.concatenate([f, k]))
    up, down = call(z_faces, [128, 128], [], fk)
    zl, zr = exchange(up, down, "grp")
    raw, own, w, up, down = call(
        begin, [2 * OROWS, 2 * OROWS, OROWS, PACKED[2], PACKED[2]], [256], fk, zl, zr
    )
    xl, xr = exchange(up, down, "gx")

    def faces(fields, own, xl, xr):
        def kernel(*refs):
            y_faces(fields, *refs)

        return call(kernel, [YROWS[fields]] * 2 + [fields * XROWS] * 2, [24 * 16], own, xl, xr)

    up, down, xl, xr = faces(2, own, xl, xr)
    yl, yr = exchange(up, down, "gy")
    own, up, down, sol, wide_u = call(
        first_round,
        [OROWS, PACKED[1], PACKED[1], SOLROWS, WROWS],
        [WROWS, WROWS, WROWS, 192, 480, OROWS, 256],
        raw, own, w, xl, xr, yl, yr,
    )
    xl, xr = exchange(up, down, "gx")
    up, down, xl, xr = faces(1, own, xl, xr)
    yl, yr = exchange(up, down, "gy")
    out, resid = call(
        second_round,
        [256, 256],
        [WROWS, WROWS, WROWS, SOLROWS, 192, 480, 256, 256],
        fk, own, xl, xr, yl, yr, sol, wide_u,
        out_specs=[HBM, HBM], copies=3,
    )
    return out.reshape(shape), resid.reshape(shape)


def solution(mesh):
    placed = (P("gx", "gy", "grp"), P("gx", "gy", "grp"))
    return jax.shard_map(shards, mesh=mesh, in_specs=placed, out_specs=placed, check_vma=False)
```

```python
import jax
import jax.numpy as jnp
from jax import lax
from jax.experimental import pallas as pl
from jax.experimental.pallas import tpu as pltpu
from jax.sharding import PartitionSpec as P

F32 = jnp.float32
LANES = 128
HALO = 3
N = (16, 8, 4)
X = tuple(n + 2 * HALO for n in N)
RING = (24, 16, 16)
STEP = (1, 2, 4)
OWN = tuple(2 * n for n in N)
WIDE = tuple(2 * r for r in RING)
OBASE = (0, 512, 640)
CELLS = 672
OROWS = 704
XBASE = (0, 96, 144)
XROWS = 256
YROWS = (0, 152, 264)
PACKED = (0, 96, 168)
LAYERS = (3, 2)
UNROLL = 8
GROUPS = (3, 3)
WBASE = (0, 1056, 1504)
WROWS = 2048
SOLROWS = 18 * 48
VMEM_LIMIT = 48 * 1024 * 1024


def lanes_of(rows):
    return lax.broadcasted_iota(jnp.int32, (rows, LANES), 1)


VM = pl.BlockSpec(memory_space=pltpu.VMEM)
HBM = pl.BlockSpec(memory_space=pl.ANY)


def call(kernel, outs, scratch, *args, out_specs=None, copies=0):
    return pl.pallas_call(
        kernel,
        out_shape=[jax.ShapeDtypeStruct((rows, LANES), F32) for rows in outs],
        in_specs=[VM] * len(args),
        out_specs=out_specs or [VM] * len(outs),
        scratch_shapes=[pltpu.VMEM((rows, LANES), F32) for rows in scratch]
        + ([pltpu.SemaphoreType.DMA((copies,))] if copies else []),
        compiler_params=pltpu.CompilerParams(vmem_limit_bytes=VMEM_LIMIT),
    )(*args)


def z_faces(fk_ref, up_ref, down_ref):
    quarter = lanes_of(16) // 32
    for field, ref in enumerate((fk_ref.at[pl.ds(0, 256), :], fk_ref.at[pl.ds(256, 256), :])):
        for g in range(4):
            slabs = [ref[pl.ds(16 * (4 * g + m), 16), :] for m in range(4)]
            up = pltpu.roll(slabs[0], 32, 1)
            down = slabs[0]
            for m in range(1, 4):
                shift = 32 * (m + 1) % LANES
                moved = pltpu.roll(slabs[m], shift, 1) if shift else slabs[m]
                up = jnp.where(quarter == m, moved, up)
                down = jnp.where(quarter == m, pltpu.roll(slabs[m], 32 * m, 1), down)
            at = pl.ds(64 * field + 16 * g, 16)
            up_ref[at, :] = up
            down_ref[at, :] = down


def coarsen(ref, level, base, tmp, scale):
    rows = OWN[level]
    half = rows // 2
    bit = STEP[level]
    even = (lanes_of(half) // bit) % 2 == 0
    for a in range(N[level] // 2):
        at = base + OBASE[level] + 2 * a * rows
        tmp[pl.ds(a * rows, rows), :] = ref[pl.ds(at, rows), :] + ref[pl.ds(at + rows, rows), :]
    for a in range(N[level] // 2):
        pair = tmp[pl.ds(a * rows, half, 2), :] + tmp[pl.ds(a * rows + 1, half, 2), :]
        other = jnp.where(even, pltpu.roll(pair, LANES - bit, 1), pltpu.roll(pair, bit, 1))
        ref[pl.ds(base + OBASE[level + 1] + a * half, half), :] = (pair + other) * scale


def x_faces(own_ref, base, up_ref, down_ref, xbase, count):
    lane = lanes_of(16)
    odd = lane % 2 == 1
    turn = lanes_of(8) % 4
    for dst, end in ((up_ref, 1), (down_ref, 0)):
        at = [base + OBASE[level] + end * (N[level] - count) * OWN[level] for level in range(3)]
        to = xbase
        for i in range(count):
            dst[pl.ds(to, 16), :] = own_ref[pl.ds(at[0] + 32 * i, 16), :]
            to += 16
        shared = own_ref[pl.ds(at[0] + 16, 16), :]
        for i in range(1, count):
            moved = pltpu.roll(own_ref[pl.ds(at[0] + 32 * i + 16, 16), :], 32 * i, 1)
            shared = jnp.where((lane + 16) // 32 == i, moved, shared)
        dst[pl.ds(to, 16), :] = shared
        c = [own_ref[pl.ds(at[1] + 16 * i, 16), :] for i in range(count)]
        dst[pl.ds(to + 16, 16), :] = jnp.where(odd, c[1], c[0])
        to += 32
        if count == 3:
            dst[pl.ds(to, 8), :] = jnp.where(odd[:8], c[2][8:], c[2][:8])
            to += 8
        c = [own_ref[pl.ds(at[2] + 8 * i, 8), :] for i in range(count)]
        shared = c[0]
        for i in range(1, count):
            shared = jnp.where(turn == i, c[i], shared)
        dst[pl.ds(to, 8), :] = shared


def unpack(src, at, dst, to, count, skip):
    odd = lanes_of(16) % 2 == 1
    turn = lanes_of(8) % 4
    for level in range(3):
        rows = OWN[level]
        for i in range(HALO):
            if not skip <= i < skip + count:
                dst[pl.ds(to + XBASE[level] + rows * i, rows), :] = jnp.zeros((rows, LANES), F32)
    to1, to2, to3 = (to + XBASE[level] + skip * OWN[level] for level in range(3))
    for i in range(count):
        dst[pl.ds(to1 + 32 * i, 16), :] = src[pl.ds(at, 16), :]
        at += 16
    shared = src[pl.ds(at, 16), :]
    for i in range(count):
        dst[pl.ds(to1 + 32 * i + 16, 16), :] = pltpu.roll(shared, LANES - 32 * i, 1) if i else shared

    def two(value):
        mask = odd[: value.shape[0]]
        return jnp.where(mask, pltpu.roll(value, 1, 1), value), jnp.where(mask, value, pltpu.roll(value, LANES - 1, 1))

    first = two(src[pl.ds(at + 16, 16), :])
    dst[pl.ds(to2, 16), :] = first[0]
    dst[pl.ds(to2 + 16, 16), :] = first[1]
    at += 32
    if count == 3:
        last = two(src[pl.ds(at, 8), :])
        dst[pl.ds(to2 + 32, 8), :] = last[0]
        dst[pl.ds(to2 + 40, 8), :] = last[1]
        at += 8
    c = src[pl.ds(at, 8), :]
    moved = {d: pltpu.roll(c, d % LANES, 1) if d else c for d in range(1 - count, 4)}
    for i in range(count):
        value = moved[-i]
        for lane in range(1, 4):
            value = jnp.where(turn == lane, moved[lane - i], value)
        dst[pl.ds(to3 + 8 * i, 8), :] = value


def begin(fk_ref, zl_ref, zr_ref, raw_ref, own_ref, w_ref, up_ref, down_ref, tmp):
    low = lanes_of(16) < 64
    for field, ref in enumerate((fk_ref.at[pl.ds(0, 256), :], fk_ref.at[pl.ds(256, 256), :])):
        base = field * OROWS
        for g in range(4):
            at = pl.ds(64 * field + 16 * g, 16)
            left, right = zl_ref[at, :], zr_ref[at, :]
            for m in range(4):
                slab = 4 * g + m
                shift_l, shift_r = (96 - 32 * m) % LANES, (-32 * m) % LANES
                from_l = pltpu.roll(left, shift_l, 1) if shift_l else left
                from_r = pltpu.roll(right, shift_r, 1) if shift_r else right
                raw_ref[pl.ds(base + 32 * slab, 16), :] = ref[pl.ds(16 * slab, 16), :]
                raw_ref[pl.ds(base + 32 * slab + 16, 16), :] = jnp.where(low, from_r, from_l)
        scale = 0.125 if field == 0 else 0.125 * 0.25
        coarsen(raw_ref, 0, base, tmp, scale)
        coarsen(raw_ref, 1, base, tmp, scale)
    for at in range(0, CELLS, 32):
        c = raw_ref[pl.ds(OROWS + at, 32), :]
        w = 0.8 / (14.0 * c + 1.0)
        w_ref[pl.ds(at, 32), :] = w
        own_ref[pl.ds(at, 32), :] = w * raw_ref[pl.ds(at, 32), :]
        own_ref[pl.ds(OROWS + at, 32), :] = 0.25 * (w * c)
    for field in range(2):
        x_faces(own_ref, field * OROWS, up_ref, down_ref, PACKED[field], LAYERS[field])


def y_parts(count):
    parts, at = [], 0
    for j in range(count):
        parts.append((at, 0, ((0, j),), None))
        at += X[0]
    for j in range(0, count, 2):
        members = tuple((h, k) for k in range(j, min(j + 2, count)) for h in range(2))
        parts.append((at, 2, members, "turns"))
        at += X[2]
    for j in range(count):
        parts.append((at, 1, ((0, j), (1, j)), "turns"))
        at += X[1]
    parts.append((at, 0, tuple((1, j) for j in range(count)), "lanes"))
    return parts


def share(vectors, how):
    shared = vectors[0]
    lane = lanes_of(shared.shape[0])
    for i in range(1, len(vectors)):
        if how == "lanes":
            shared = jnp.where((lane + 16) // 32 == i, pltpu.roll(vectors[i], 32 * i, 1), shared)
        else:
            shared = jnp.where(lane % len(vectors) == i, vectors[i], shared)
    return shared


def unshare(shared, number, how):
    if how != "turns":
        return [pltpu.roll(shared, LANES - 32 * i, 1) if i else shared for i in range(number)]
    turn = lanes_of(shared.shape[0]) % number
    moved = {d: pltpu.roll(shared, d % LANES, 1) if d else shared for d in range(1 - number, number)}
    vectors = []
    for i in range(number):
        value = moved[-i]
        for lane in range(1, number):
            value = jnp.where(turn == lane, moved[lane - i], value)
        vectors.append(value)
    return vectors


def y_faces(fields, own_ref, xl_packed, xr_packed, up_ref, down_ref, xl_ref, xr_ref, rows_ref):
    for field in range(fields):
        ob, xb, yb, count = field * OROWS, field * XROWS, YROWS[field], LAYERS[field]
        unpack(xl_packed, PACKED[field], xl_ref, xb, count, HALO - count)
        unpack(xr_packed, PACKED[field], xr_ref, xb, count, 0)
        for side, (dst, first) in enumerate(((up_ref, False), (down_ref, True))):
            for at, level, members, how in y_parts(count):
                n, rows, size = N[level], OWN[level], X[level]
                vectors = []
                for m, (h, j) in enumerate(members):
                    row = h * n + (j if first else n - count + j)
                    to = 24 * (m + 4 * (side + 2 * field))
                    if len(members) == 1:
                        ref, to = dst, yb + at
                    else:
                        ref = rows_ref
                    ref[pl.ds(to, HALO), :] = xl_ref[pl.ds(xb + XBASE[level] + row, HALO, rows), :]
                    ref[pl.ds(to + HALO, n), :] = own_ref[pl.ds(ob + OBASE[level] + row, n, rows), :]
                    ref[pl.ds(to + HALO + n, HALO), :] = xr_ref[pl.ds(xb + XBASE[level] + row, HALO, rows), :]
                    if len(members) > 1:
                        vectors.append(ref[pl.ds(to, size), :])
                if vectors:
                    dst[pl.ds(yb + at, size), :] = share(vectors, how)


def widen(field, own_ref, xl_ref, xr_ref, yl_ref, yr_ref, wide_ref):
    ob, xb, yb, count = field * OROWS, field * XROWS, YROWS[field], LAYERS[field]
    for level in range(3):
        n, ring, rows = N[level], RING[level], OWN[level]
        for i in range(X[level]):
            if i < HALO:
                ref, at = xl_ref, xb + XBASE[level] + i * rows
            elif i < HALO + n:
                ref, at = own_ref, ob + OBASE[level] + (i - HALO) * rows
            else:
                ref, at = xr_ref, xb + XBASE[level] + (i - HALO - n) * rows
            for h in range(2):
                to = WBASE[level] + i * WIDE[level] + h * ring
                wide_ref[pl.ds(to, n), :] = ref[pl.ds(at + h * n, n), :]
    for at, level, members, how in y_parts(count):
        n, ring, size = N[level], RING[level], X[level]
        for ref, start in ((yr_ref, n), (yl_ref, ring - count)):
            shared = ref[pl.ds(yb + at, size), :]
            for (h, j), vector in zip(members, unshare(shared, len(members), how)):
                wide_ref[pl.ds(WBASE[level] + h * ring + start + j, size, WIDE[level]), :] = vector


def slab(ref, base, i, rows):
    return ref[pl.ds(pl.multiple_of(base + i * rows, 8), rows), :]


def put(ref, base, i, rows, value):
    ref[pl.ds(pl.multiple_of(base + i * rows, 8), rows), :] = value


def loop(low, high, value, store):
    groups = -(-(high - low) // UNROLL)
    size = -(-(high - low) // groups)
    lead = (high - low) - (groups - 1) * size

    def group(first, count):
        values = [value(first + u) for u in range(count)]
        for u in range(count):
            store(first + u, values[u])

    def step(g, carry):
        group(low + lead + g * size, size)
        return carry

    group(low, lead)
    if groups > 1:
        lax.fori_loop(0, groups - 1, step, 0)


def ring_sum(ref, base, i, ring, step):
    rows = 2 * ring
    mid = slab(ref, base, i, rows)
    total = slab(ref, base, i - 1, rows) + slab(ref, base, i + 1, rows) + (mid + mid)
    halves = []
    for h in range(2):
        t = total[h * ring : (h + 1) * ring]
        halves.append(pltpu.roll(t, 1, 0) + pltpu.roll(t, ring - 1, 0) + (t + t))
    lane = lanes_of(ring)
    a, b = halves
    ra, rb = pltpu.roll(a, step, 1), pltpu.roll(b, step, 1)
    sa, sb = pltpu.roll(a, LANES - step, 1), pltpu.roll(b, LANES - step, 1)
    low, high = lane < step, lane >= LANES - step
    new_a = a + a + jnp.where(low, rb, ra) + jnp.where(high, sb, sa)
    new_b = b + b + jnp.where(low, ra, rb) + jnp.where(high, sa, sb)
    return mid, new_a, new_b


def join(a, b):
    return jnp.concatenate([a, b], axis=0)


def sweeps(wide_b, wide_u, first, second):
    def sweep(edge, groups, src, dst):
        def value(level, i):
            rows, base = WIDE[level], WBASE[level]
            mid, a, b = ring_sum(src, base, i, RING[level], STEP[level])
            around = slab(wide_u, base, i, rows) * (join(a, b) - 8.0 * mid)
            return 0.2 * mid + slab(wide_b, base, i, rows) + around

        def group(g):
            done = []
            for level in range(3):
                high = X[level] - edge
                size = -(-(high - edge) // groups)
                start = jnp.minimum(edge + g * size, high - size)
                done += [(level, start + u, value(level, start + u)) for u in range(size)]
            for level, i, new in done:
                put(dst, WBASE[level], i, WIDE[level], new)

        pl.loop(0, groups)(group)

    sweep(1, GROUPS[0], wide_b, first)
    sweep(2, GROUPS[1], first, second)


def prolong(err, up3, up2):
    for q in range(6):
        for h in range(2):
            e3 = err[pl.ds(WBASE[2] + (q + 2) * 32 + h * 16, 16), :]
            to = q * 32 + h * 16
            up3[pl.ds(to, 5, 2), :] = e3[0:5]
            up3[pl.ds(to + 1, 5, 2), :] = e3[0:5]
            up3[pl.ds(to + 10, 4), :] = jnp.zeros((4, LANES), F32)
            up3[pl.ds(to + 14, 2), :] = jnp.broadcast_to(e3[15:16], (2, LANES))
    for a in range(10):
        for h in range(2):
            e2 = err[pl.ds(WBASE[1] + (a + 2) * 32 + h * 16, 16), :]
            e2 = e2 + up3[pl.ds(((a - 1) // 2 + 1) * 32 + h * 16, 16), :]
            to = a * 48 + h * 24
            up2[pl.ds(to, 9, 2), :] = e2[0:9]
            up2[pl.ds(to + 1, 9, 2), :] = e2[0:9]
            up2[pl.ds(to + 18, 4), :] = jnp.zeros((4, LANES), F32)
            up2[pl.ds(to + 22, 2), :] = jnp.broadcast_to(e2[15:16], (2, LANES))


def correct(err, up2, old_ref, sol_ref):
    for i in range(18):
        value = err[pl.ds((i + 2) * 48, 48), :] + up2[pl.ds(((i - 1) // 2 + 1) * 48, 48), :]
        if old_ref is not None:
            value = value + old_ref[pl.ds(i * 48, 48), :]
        sol_ref[pl.ds(i * 48, 48), :] = value


def first_round(
    raw_ref, own_ref, w_ref, xl_ref, xr_ref, yl_ref, yr_ref,
    next_ref, up_ref, down_ref, sol_ref, wide_u,
    wide_b, first, second, up3, up2, r_ref, tmp,
):
    widen(0, own_ref, xl_ref, xr_ref, yl_ref, yr_ref, wide_b)
    widen(1, own_ref, xl_ref, xr_ref, yl_ref, yr_ref, wide_u)
    sweeps(wide_b, wide_u, first, second)
    prolong(second, up3, up2)
    correct(second, up2, None, sol_ref)

    def resid(i):
        mid, a, b = ring_sum(sol_ref, 0, i + 1, 24, 1)
        halves = []
        for h, t in enumerate((a, b)):
            s = mid[h * 24 : h * 24 + 16]
            f = raw_ref[pl.ds(pl.multiple_of(i * 32 + h * 16, 16), 16), :]
            k = raw_ref[pl.ds(pl.multiple_of(OROWS + i * 32 + h * 16, 16), 16), :]
            halves.append(f - (k * (16.0 * s - 0.25 * t[:16]) + s))
        return join(*halves)

    loop(0, 16, resid, lambda i, new: put(r_ref, 0, i, 32, new))
    coarsen(r_ref, 0, 0, tmp, 0.125)
    coarsen(r_ref, 1, 0, tmp, 0.125)
    for at in range(0, CELLS, 32):
        next_ref[pl.ds(at, 32), :] = w_ref[pl.ds(at, 32), :] * r_ref[pl.ds(at, 32), :]
    x_faces(next_ref, 0, up_ref, down_ref, 0, LAYERS[0])


def second_round(
    fk_ref, own_ref, xl_ref, xr_ref, yl_ref, yr_ref, old_ref, wide_u,
    out_hbm, resid_hbm,
    wide_b, first, second, sol_ref, up3, up2, out_ref, resid_ref, sems,
):
    widen(0, own_ref, xl_ref, xr_ref, yl_ref, yr_ref, wide_b)
    sweeps(wide_b, wide_u, first, second)
    prolong(second, up3, up2)
    correct(second, up2, old_ref, sol_ref)
    for i in range(16):
        out_ref[pl.ds(16 * i, 16), :] = sol_ref[pl.ds(48 * (i + 1), 16), :]
    copies = [pltpu.make_async_copy(out_ref, out_hbm, sems.at[0])]
    copies[0].start()

    def resid(i):
        mid, a, _ = ring_sum(sol_ref, 0, i + 1, 24, 1)
        s = mid[:16]
        return slab(fk_ref, 0, i, 16) - (slab(fk_ref, 256, i, 16) * (16.0 * s - 0.25 * a[:16]) + s)

    for half in range(2):
        loop(8 * half, 8 * half + 8, resid, lambda i, new: put(resid_ref, 0, i, 16, new))
        at = pl.ds(128 * half, 128)
        copies.append(pltpu.make_async_copy(resid_ref.at[at, :], resid_hbm.at[at, :], sems.at[1 + half]))
        copies[-1].start()
    for copy in copies:
        copy.wait()


def exchange(up, down, axis):
    size = lax.axis_size(axis)
    odd = lax.axis_index(axis) % 2 == 1
    outer = [(i, i + 1) for i in range(1, size - 1, 2)]
    outer = outer + [(j, i) for i, j in outer]
    inner = [[i, i + 1] for i in range(0, size, 2)]
    two = lax.ppermute(jnp.where(odd, up, down), axis, outer)
    one = lax.all_gather(jnp.where(odd, down, up), axis, axis_index_groups=inner)
    return jnp.where(odd, one[0], two), jnp.where(odd, two, one[1])


def shards(forcing, kappa):
    shape = forcing.shape
    f = forcing.reshape(256, LANES)
    k = kappa.reshape(256, LANES)
    fk = lax.optimization_barrier(jnp.concatenate([f, k]))
    up, down = call(z_faces, [128, 128], [], fk)
    zl, zr = exchange(up, down, "grp")
    raw, own, w, up, down = call(
        begin, [2 * OROWS, 2 * OROWS, OROWS, PACKED[2], PACKED[2]], [264], fk, zl, zr
    )
    xl, xr = exchange(up, down, "gx")

    def faces(fields, own, xl, xr):
        def kernel(*refs):
            y_faces(fields, *refs)

        return call(kernel, [YROWS[fields]] * 2 + [fields * XROWS] * 2, [400], own, xl, xr)

    up, down, xl, xr = faces(2, own, xl, xr)
    yl, yr = exchange(up, down, "gy")
    own, up, down, sol, wide_u = call(
        first_round,
        [OROWS, PACKED[1], PACKED[1], SOLROWS, WROWS],
        [WROWS, WROWS, WROWS, 208, 496, OROWS, 264],
        raw, own, w, xl, xr, yl, yr,
    )
    xl, xr = exchange(up, down, "gx")
    up, down, xl, xr = faces(1, own, xl, xr)
    yl, yr = exchange(up, down, "gy")
    out, resid = call(
        second_round,
        [256, 256],
        [WROWS, WROWS, WROWS, SOLROWS, 208, 496, 256, 256],
        fk, own, xl, xr, yl, yr, sol, wide_u,
        out_specs=[HBM, HBM], copies=3,
    )
    return out.reshape(shape), resid.reshape(shape)


def solution(mesh):
    placed = (P("gx", "gy", "grp"), P("gx", "gy", "grp"))
    return jax.shard_map(shards, mesh=mesh, in_specs=placed, out_specs=placed, check_vma=False)
```

```python
import jax
import jax.numpy as jnp
from jax import lax
from jax.experimental import pallas as pl
from jax.experimental.pallas import tpu as pltpu
from jax.sharding import PartitionSpec as P

F32 = jnp.float32
LANES = 128
HALO = 3
N = (16, 8, 4)
X = tuple(n + 2 * HALO for n in N)
RING = (24, 16, 16)
STEP = (1, 2, 4)
OWN = tuple(2 * n for n in N)
WIDE = tuple(2 * r for r in RING)
OBASE = (0, 512, 640)
ZWIDTH = 24
ZROWS = 48
CELLS = 672
OROWS = 704
XBASE = (0, 96, 144)
XROWS = 256
YROWS = (0, 152, 264)
PACKED = (0, 96, 168)
LAYERS = (3, 2)
UNROLL = 8
GROUPS = (3, 2)
WBASE = (0, 1056, 1504)
WROWS = 2048
SOLROWS = 18 * 48
VMEM_LIMIT = 48 * 1024 * 1024


def lanes_of(rows):
    return lax.broadcasted_iota(jnp.int32, (rows, LANES), 1)


VM = pl.BlockSpec(memory_space=pltpu.VMEM)
HBM = pl.BlockSpec(memory_space=pl.ANY)


def call(kernel, outs, scratch, *args, out_specs=None, copies=0):
    return pl.pallas_call(
        kernel,
        out_shape=[jax.ShapeDtypeStruct((rows, LANES), F32) for rows in outs],
        in_specs=[VM] * len(args),
        out_specs=out_specs or [VM] * len(outs),
        scratch_shapes=[pltpu.VMEM((rows, LANES), F32) for rows in scratch]
        + ([pltpu.SemaphoreType.DMA((copies,))] if copies else []),
        compiler_params=pltpu.CompilerParams(vmem_limit_bytes=VMEM_LIMIT),
    )(*args)


def z_faces(fk_ref, up_ref, down_ref):
    lane = lanes_of(16)
    for field in range(2):
        for tile in range(3):
            slot = (lane + LANES * tile) // ZWIDTH
            members = range(LANES * tile // ZWIDTH, (LANES * (tile + 1) - 1) // ZWIDTH + 1)
            for dst, begin_at in ((up_ref, LANES - ZWIDTH), (down_ref, 0)):
                shared = None
                for i in members:
                    value = fk_ref[pl.ds(256 * field + 16 * i, 16), :]
                    move = (ZWIDTH * i - begin_at) % LANES
                    value = pltpu.roll(value, move, 1) if move else value
                    shared = value if shared is None else jnp.where(slot == i, value, shared)
                dst[pl.ds(ZROWS * field + 16 * tile, 16), :] = shared


def z_slab(ref, field, i, begin_at):
    tile, at = divmod(ZWIDTH * i, LANES)
    value = ref[pl.ds(ZROWS * field + 16 * tile, 16), :]
    if at + ZWIDTH > LANES:
        value = jnp.where(lanes_of(16) >= at, value, ref[pl.ds(ZROWS * field + 16 * (tile + 1), 16), :])
    move = (begin_at - at) % LANES
    return pltpu.roll(value, move, 1) if move else value


def coarsen(ref, level, base, tmp, scale):
    rows = OWN[level]
    half = rows // 2
    bit = STEP[level]
    even = (lanes_of(half) // bit) % 2 == 0
    for a in range(N[level] // 2):
        at = base + OBASE[level] + 2 * a * rows
        tmp[pl.ds(a * rows, rows), :] = ref[pl.ds(at, rows), :] + ref[pl.ds(at + rows, rows), :]
    for a in range(N[level] // 2):
        pair = tmp[pl.ds(a * rows, half, 2), :] + tmp[pl.ds(a * rows + 1, half, 2), :]
        other = jnp.where(even, pltpu.roll(pair, LANES - bit, 1), pltpu.roll(pair, bit, 1))
        ref[pl.ds(base + OBASE[level + 1] + a * half, half), :] = (pair + other) * scale


def x_faces(own_ref, base, up_ref, down_ref, xbase, count):
    lane = lanes_of(16)
    odd = lane % 2 == 1
    turn = lanes_of(8) % 4
    for dst, end in ((up_ref, 1), (down_ref, 0)):
        at = [base + OBASE[level] + end * (N[level] - count) * OWN[level] for level in range(3)]
        to = xbase
        for i in range(count):
            dst[pl.ds(to, 16), :] = own_ref[pl.ds(at[0] + 32 * i, 16), :]
            to += 16
        shared = own_ref[pl.ds(at[0] + 16, 16), :]
        for i in range(1, count):
            moved = pltpu.roll(own_ref[pl.ds(at[0] + 32 * i + 16, 16), :], 32 * i, 1)
            shared = jnp.where((lane + 16) // 32 == i, moved, shared)
        dst[pl.ds(to, 16), :] = shared
        c = [own_ref[pl.ds(at[1] + 16 * i, 16), :] for i in range(count)]
        dst[pl.ds(to + 16, 16), :] = jnp.where(odd, c[1], c[0])
        to += 32
        if count == 3:
            dst[pl.ds(to, 8), :] = jnp.where(odd[:8], c[2][8:], c[2][:8])
            to += 8
        c = [own_ref[pl.ds(at[2] + 8 * i, 8), :] for i in range(count)]
        shared = c[0]
        for i in range(1, count):
            shared = jnp.where(turn == i, c[i], shared)
        dst[pl.ds(to, 8), :] = shared


def unpack(src, at, dst, to, count, skip):
    odd = lanes_of(16) % 2 == 1
    turn = lanes_of(8) % 4
    for level in range(3):
        rows = OWN[level]
        for i in range(HALO):
            if not skip <= i < skip + count:
                dst[pl.ds(to + XBASE[level] + rows * i, rows), :] = jnp.zeros((rows, LANES), F32)
    to1, to2, to3 = (to + XBASE[level] + skip * OWN[level] for level in range(3))
    for i in range(count):
        dst[pl.ds(to1 + 32 * i, 16), :] = src[pl.ds(at, 16), :]
        at += 16
    shared = src[pl.ds(at, 16), :]
    for i in range(count):
        dst[pl.ds(to1 + 32 * i + 16, 16), :] = pltpu.roll(shared, LANES - 32 * i, 1) if i else shared

    def two(value):
        mask = odd[: value.shape[0]]
        return jnp.where(mask, pltpu.roll(value, 1, 1), value), jnp.where(mask, value, pltpu.roll(value, LANES - 1, 1))

    first = two(src[pl.ds(at + 16, 16), :])
    dst[pl.ds(to2, 16), :] = first[0]
    dst[pl.ds(to2 + 16, 16), :] = first[1]
    at += 32
    if count == 3:
        last = two(src[pl.ds(at, 8), :])
        dst[pl.ds(to2 + 32, 8), :] = last[0]
        dst[pl.ds(to2 + 40, 8), :] = last[1]
        at += 8
    c = src[pl.ds(at, 8), :]
    moved = {d: pltpu.roll(c, d % LANES, 1) if d else c for d in range(1 - count, 4)}
    for i in range(count):
        value = moved[-i]
        for lane in range(1, 4):
            value = jnp.where(turn == lane, moved[lane - i], value)
        dst[pl.ds(to3 + 8 * i, 8), :] = value


def begin(fk_ref, zl_ref, zr_ref, raw_ref, own_ref, w_ref, up_ref, down_ref, tmp):
    low = lanes_of(16) < 64
    for field, ref in enumerate((fk_ref.at[pl.ds(0, 256), :], fk_ref.at[pl.ds(256, 256), :])):
        base = field * OROWS
        for i in range(16):
            from_l = z_slab(zl_ref, field, i, LANES - ZWIDTH)
            from_r = z_slab(zr_ref, field, i, 0)
            raw_ref[pl.ds(base + 32 * i, 16), :] = ref[pl.ds(16 * i, 16), :]
            raw_ref[pl.ds(base + 32 * i + 16, 16), :] = jnp.where(low, from_r, from_l)
        scale = 0.125 if field == 0 else 0.125 * 0.25
        coarsen(raw_ref, 0, base, tmp, scale)
        coarsen(raw_ref, 1, base, tmp, scale)
    for at in range(0, CELLS, 32):
        c = raw_ref[pl.ds(OROWS + at, 32), :]
        w = 0.8 / (14.0 * c + 1.0)
        w_ref[pl.ds(at, 32), :] = w
        own_ref[pl.ds(at, 32), :] = w * raw_ref[pl.ds(at, 32), :]
        own_ref[pl.ds(OROWS + at, 32), :] = 0.25 * (w * c)
    for field in range(2):
        x_faces(own_ref, field * OROWS, up_ref, down_ref, PACKED[field], LAYERS[field])


def y_parts(count):
    parts, at = [], 0
    for j in range(count):
        parts.append((at, 0, ((0, j),), None))
        at += X[0]
    for j in range(0, count, 2):
        members = tuple((h, k) for k in range(j, min(j + 2, count)) for h in range(2))
        parts.append((at, 2, members, "turns"))
        at += X[2]
    for j in range(count):
        parts.append((at, 1, ((0, j), (1, j)), "turns"))
        at += X[1]
    parts.append((at, 0, tuple((1, j) for j in range(count)), "lanes"))
    return parts


def share(vectors, how):
    shared = vectors[0]
    lane = lanes_of(shared.shape[0])
    for i in range(1, len(vectors)):
        if how == "lanes":
            shared = jnp.where((lane + 16) // 32 == i, pltpu.roll(vectors[i], 32 * i, 1), shared)
        else:
            shared = jnp.where(lane % len(vectors) == i, vectors[i], shared)
    return shared


def unshare(shared, number, how):
    if how != "turns":
        return [pltpu.roll(shared, LANES - 32 * i, 1) if i else shared for i in range(number)]
    turn = lanes_of(shared.shape[0]) % number
    moved = {d: pltpu.roll(shared, d % LANES, 1) if d else shared for d in range(1 - number, number)}
    vectors = []
    for i in range(number):
        value = moved[-i]
        for lane in range(1, number):
            value = jnp.where(turn == lane, moved[lane - i], value)
        vectors.append(value)
    return vectors


def y_faces(fields, own_ref, xl_packed, xr_packed, up_ref, down_ref, xl_ref, xr_ref, rows_ref):
    for field in range(fields):
        ob, xb, yb, count = field * OROWS, field * XROWS, YROWS[field], LAYERS[field]
        unpack(xl_packed, PACKED[field], xl_ref, xb, count, HALO - count)
        unpack(xr_packed, PACKED[field], xr_ref, xb, count, 0)
        for side, (dst, first) in enumerate(((up_ref, False), (down_ref, True))):
            for at, level, members, how in y_parts(count):
                n, rows, size = N[level], OWN[level], X[level]
                vectors = []
                for m, (h, j) in enumerate(members):
                    row = h * n + (j if first else n - count + j)
                    to = 24 * (m + 4 * (side + 2 * field))
                    if len(members) == 1:
                        ref, to = dst, yb + at
                    else:
                        ref = rows_ref
                    ref[pl.ds(to, HALO), :] = xl_ref[pl.ds(xb + XBASE[level] + row, HALO, rows), :]
                    ref[pl.ds(to + HALO, n), :] = own_ref[pl.ds(ob + OBASE[level] + row, n, rows), :]
                    ref[pl.ds(to + HALO + n, HALO), :] = xr_ref[pl.ds(xb + XBASE[level] + row, HALO, rows), :]
                    if len(members) > 1:
                        vectors.append(ref[pl.ds(to, size), :])
                if vectors:
                    dst[pl.ds(yb + at, size), :] = share(vectors, how)


def widen(field, own_ref, xl_ref, xr_ref, yl_ref, yr_ref, wide_ref):
    ob, xb, yb, count = field * OROWS, field * XROWS, YROWS[field], LAYERS[field]
    for level in range(3):
        n, ring, rows = N[level], RING[level], OWN[level]
        for i in range(X[level]):
            if i < HALO:
                ref, at = xl_ref, xb + XBASE[level] + i * rows
            elif i < HALO + n:
                ref, at = own_ref, ob + OBASE[level] + (i - HALO) * rows
            else:
                ref, at = xr_ref, xb + XBASE[level] + (i - HALO - n) * rows
            for h in range(2):
                to = WBASE[level] + i * WIDE[level] + h * ring
                wide_ref[pl.ds(to, n), :] = ref[pl.ds(at + h * n, n), :]
    for at, level, members, how in y_parts(count):
        n, ring, size = N[level], RING[level], X[level]
        for ref, start in ((yr_ref, n), (yl_ref, ring - count)):
            shared = ref[pl.ds(yb + at, size), :]
            for (h, j), vector in zip(members, unshare(shared, len(members), how)):
                wide_ref[pl.ds(WBASE[level] + h * ring + start + j, size, WIDE[level]), :] = vector


def slab(ref, base, i, rows):
    return ref[pl.ds(pl.multiple_of(base + i * rows, 8), rows), :]


def put(ref, base, i, rows, value):
    ref[pl.ds(pl.multiple_of(base + i * rows, 8), rows), :] = value


def loop(low, high, value, store):
    groups = -(-(high - low) // UNROLL)
    size = -(-(high - low) // groups)
    lead = (high - low) - (groups - 1) * size

    def group(first, count):
        values = [value(first + u) for u in range(count)]
        for u in range(count):
            store(first + u, values[u])

    def step(g, carry):
        group(low + lead + g * size, size)
        return carry

    group(low, lead)
    if groups > 1:
        lax.fori_loop(0, groups - 1, step, 0)


def ring_sum(ref, base, i, ring, step):
    rows = 2 * ring
    mid = slab(ref, base, i, rows)
    total = slab(ref, base, i - 1, rows) + slab(ref, base, i + 1, rows) + (mid + mid)
    halves = []
    for h in range(2):
        t = total[h * ring : (h + 1) * ring]
        halves.append((pltpu.roll(t, 1, 0) + pltpu.roll(t, ring - 1, 0)) + (t + t))
    lane = lanes_of(ring)
    a, b = halves
    ra, rb = pltpu.roll(a, step, 1), pltpu.roll(b, step, 1)
    sa, sb = pltpu.roll(a, LANES - step, 1), pltpu.roll(b, LANES - step, 1)
    low, high = lane < step, lane >= LANES - step
    new_a = (a + a) + (jnp.where(low, rb, ra) + jnp.where(high, sb, sa))
    new_b = (b + b) + (jnp.where(low, ra, rb) + jnp.where(high, sa, sb))
    return mid, new_a, new_b


def join(a, b):
    return jnp.concatenate([a, b], axis=0)


def sweeps(wide_b, wide_u, first, second):
    def sweep(edge, groups, src, dst):
        def value(level, i):
            rows, base = WIDE[level], WBASE[level]
            mid, a, b = ring_sum(src, base, i, RING[level], STEP[level])
            around = slab(wide_u, base, i, rows) * (join(a, b) - 8.0 * mid)
            return 0.2 * mid + slab(wide_b, base, i, rows) + around

        def group(g):
            done = []
            for level in range(3):
                high = X[level] - edge
                size = -(-(high - edge) // groups)
                start = jnp.minimum(edge + g * size, high - size)
                done += [(level, start + u, value(level, start + u)) for u in range(size)]
            for level, i, new in done:
                put(dst, WBASE[level], i, WIDE[level], new)

        pl.loop(0, groups)(group)

    sweep(1, GROUPS[0], wide_b, first)
    sweep(2, GROUPS[1], first, second)


def prolong(err, up3, up2):
    for q in range(6):
        for h in range(2):
            e3 = err[pl.ds(WBASE[2] + (q + 2) * 32 + h * 16, 16), :]
            to = q * 32 + h * 16
            up3[pl.ds(to, 5, 2), :] = e3[0:5]
            up3[pl.ds(to + 1, 5, 2), :] = e3[0:5]
            up3[pl.ds(to + 10, 4), :] = jnp.zeros((4, LANES), F32)
            up3[pl.ds(to + 14, 2), :] = jnp.broadcast_to(e3[15:16], (2, LANES))
    for a in range(10):
        for h in range(2):
            e2 = err[pl.ds(WBASE[1] + (a + 2) * 32 + h * 16, 16), :]
            e2 = e2 + up3[pl.ds(((a - 1) // 2 + 1) * 32 + h * 16, 16), :]
            to = a * 48 + h * 24
            up2[pl.ds(to, 9, 2), :] = e2[0:9]
            up2[pl.ds(to + 1, 9, 2), :] = e2[0:9]
            up2[pl.ds(to + 18, 4), :] = jnp.zeros((4, LANES), F32)
            up2[pl.ds(to + 22, 2), :] = jnp.broadcast_to(e2[15:16], (2, LANES))


def correct(err, up2, old_ref, sol_ref):
    for i in range(18):
        value = err[pl.ds((i + 2) * 48, 48), :] + up2[pl.ds(((i - 1) // 2 + 1) * 48, 48), :]
        if old_ref is not None:
            value = value + old_ref[pl.ds(i * 48, 48), :]
        sol_ref[pl.ds(i * 48, 48), :] = value


def first_round(
    raw_ref, own_ref, w_ref, xl_ref, xr_ref, yl_ref, yr_ref,
    next_ref, up_ref, down_ref, sol_ref, wide_u,
    wide_b, first, second, up3, up2, r_ref, tmp,
):
    widen(0, own_ref, xl_ref, xr_ref, yl_ref, yr_ref, wide_b)
    widen(1, own_ref, xl_ref, xr_ref, yl_ref, yr_ref, wide_u)
    sweeps(wide_b, wide_u, first, second)
    prolong(second, up3, up2)
    correct(second, up2, None, sol_ref)

    def resid(i):
        mid, a, b = ring_sum(sol_ref, 0, i + 1, 24, 1)
        halves = []
        for h, t in enumerate((a, b)):
            s = mid[h * 24 : h * 24 + 16]
            f = raw_ref[pl.ds(pl.multiple_of(i * 32 + h * 16, 16), 16), :]
            k = raw_ref[pl.ds(pl.multiple_of(OROWS + i * 32 + h * 16, 16), 16), :]
            halves.append(f - (k * (16.0 * s - 0.25 * t[:16]) + s))
        return join(*halves)

    loop(0, 16, resid, lambda i, new: put(r_ref, 0, i, 32, new))
    coarsen(r_ref, 0, 0, tmp, 0.125)
    coarsen(r_ref, 1, 0, tmp, 0.125)
    for at in range(0, CELLS, 32):
        next_ref[pl.ds(at, 32), :] = w_ref[pl.ds(at, 32), :] * r_ref[pl.ds(at, 32), :]
    x_faces(next_ref, 0, up_ref, down_ref, 0, LAYERS[0])


def second_round(
    fk_ref, own_ref, xl_ref, xr_ref, yl_ref, yr_ref, old_ref, wide_u,
    out_hbm, resid_hbm,
    wide_b, first, second, sol_ref, up3, up2, out_ref, resid_ref, sems,
):
    widen(0, own_ref, xl_ref, xr_ref, yl_ref, yr_ref, wide_b)
    sweeps(wide_b, wide_u, first, second)
    prolong(second, up3, up2)
    correct(second, up2, old_ref, sol_ref)
    for i in range(16):
        out_ref[pl.ds(16 * i, 16), :] = sol_ref[pl.ds(48 * (i + 1), 16), :]
    copies = [pltpu.make_async_copy(out_ref, out_hbm, sems.at[0])]
    copies[0].start()

    def resid(i):
        mid, a, _ = ring_sum(sol_ref, 0, i + 1, 24, 1)
        s = mid[:16]
        return slab(fk_ref, 0, i, 16) - (slab(fk_ref, 256, i, 16) * (16.0 * s - 0.25 * a[:16]) + s)

    for half in range(2):
        loop(8 * half, 8 * half + 8, resid, lambda i, new: put(resid_ref, 0, i, 16, new))
        at = pl.ds(128 * half, 128)
        copies.append(pltpu.make_async_copy(resid_ref.at[at, :], resid_hbm.at[at, :], sems.at[1 + half]))
        copies[-1].start()
    for copy in copies:
        copy.wait()


def exchange(up, down, axis):
    size = lax.axis_size(axis)
    odd = lax.axis_index(axis) % 2 == 1
    outer = [(i, i + 1) for i in range(1, size - 1, 2)]
    outer = outer + [(j, i) for i, j in outer]
    inner = [[i, i + 1] for i in range(0, size, 2)]
    two = lax.ppermute(jnp.where(odd, up, down), axis, outer)
    one = lax.all_gather(jnp.where(odd, down, up), axis, axis_index_groups=inner)
    return jnp.where(odd, one[0], two), jnp.where(odd, two, one[1])


def shards(forcing, kappa):
    shape = forcing.shape
    f = forcing.reshape(256, LANES)
    k = kappa.reshape(256, LANES)
    fk = lax.optimization_barrier(jnp.concatenate([f, k]))
    up, down = call(z_faces, [2 * ZROWS, 2 * ZROWS], [], fk)
    zl, zr = exchange(up, down, "grp")
    raw, own, w, up, down = call(
        begin, [2 * OROWS, 2 * OROWS, OROWS, PACKED[2], PACKED[2]], [264], fk, zl, zr
    )
    xl, xr = exchange(up, down, "gx")

    def faces(fields, own, xl, xr):
        def kernel(*refs):
            y_faces(fields, *refs)

        return call(kernel, [YROWS[fields]] * 2 + [fields * XROWS] * 2, [400], own, xl, xr)

    up, down, xl, xr = faces(2, own, xl, xr)
    yl, yr = exchange(up, down, "gy")
    own, up, down, sol, wide_u = call(
        first_round,
        [OROWS, PACKED[1], PACKED[1], SOLROWS, WROWS],
        [WROWS, WROWS, WROWS, 208, 496, OROWS, 264],
        raw, own, w, xl, xr, yl, yr,
    )
    xl, xr = exchange(up, down, "gx")
    up, down, xl, xr = faces(1, own, xl, xr)
    yl, yr = exchange(up, down, "gy")
    out, resid = call(
        second_round,
        [256, 256],
        [WROWS, WROWS, WROWS, SOLROWS, 208, 496, 256, 256],
        fk, own, xl, xr, yl, yr, sol, wide_u,
        out_specs=[HBM, HBM], copies=3,
    )
    return out.reshape(shape), resid.reshape(shape)


def solution(mesh):
    placed = (P("gx", "gy", "grp"), P("gx", "gy", "grp"))
    return jax.shard_map(shards, mesh=mesh, in_specs=placed, out_specs=placed, check_vma=False)
```

```python
import jax
import jax.numpy as jnp
from jax import lax
from jax.experimental import pallas as pl
from jax.experimental.pallas import tpu as pltpu
from jax.sharding import PartitionSpec as P

F32 = jnp.float32
LANES = 128
HALO = 3
N = (16, 8, 4)
X = tuple(n + 2 * HALO for n in N)
RING = (24, 16, 16)
STEP = (1, 2, 4)
OWN = tuple(2 * n for n in N)
WIDE = tuple(2 * r for r in RING)
OBASE = (0, 512, 640)
ZWIDTH = 24
ZROWS = 48
CELLS = 672
OROWS = 704
XBASE = (0, 96, 144)
XROWS = 256
YROWS = (0, 144, 256)
PACKED = (0, 88, 160)
LAYERS = (3, 2)
UNROLL = 8
GROUPS = (3, 2)
WBASE = (0, 1056, 1504)
WROWS = 2048
SOLROWS = 18 * 48
VMEM_LIMIT = 48 * 1024 * 1024


def lanes_of(rows):
    return lax.broadcasted_iota(jnp.int32, (rows, LANES), 1)


VM = pl.BlockSpec(memory_space=pltpu.VMEM)
HBM = pl.BlockSpec(memory_space=pl.ANY)


def call(kernel, outs, scratch, *args, out_specs=None, copies=0):
    return pl.pallas_call(
        kernel,
        out_shape=[jax.ShapeDtypeStruct((rows, LANES), F32) for rows in outs],
        in_specs=[VM] * len(args),
        out_specs=out_specs or [VM] * len(outs),
        scratch_shapes=[pltpu.VMEM((rows, LANES), F32) for rows in scratch]
        + ([pltpu.SemaphoreType.DMA((copies,))] if copies else []),
        compiler_params=pltpu.CompilerParams(vmem_limit_bytes=VMEM_LIMIT),
    )(*args)


def z_faces(fk_ref, up_ref, down_ref):
    lane = lanes_of(16)
    for field in range(2):
        for tile in range(3):
            slot = (lane + LANES * tile) // ZWIDTH
            members = range(LANES * tile // ZWIDTH, (LANES * (tile + 1) - 1) // ZWIDTH + 1)
            for dst, begin_at in ((up_ref, LANES - ZWIDTH), (down_ref, 0)):
                shared = None
                for i in members:
                    value = fk_ref[pl.ds(256 * field + 16 * i, 16), :]
                    move = (ZWIDTH * i - begin_at) % LANES
                    value = pltpu.roll(value, move, 1) if move else value
                    shared = value if shared is None else jnp.where(slot == i, value, shared)
                dst[pl.ds(ZROWS * field + 16 * tile, 16), :] = shared


def z_slab(ref, field, i, begin_at):
    tile, at = divmod(ZWIDTH * i, LANES)
    value = ref[pl.ds(ZROWS * field + 16 * tile, 16), :]
    if at + ZWIDTH > LANES:
        value = jnp.where(lanes_of(16) >= at, value, ref[pl.ds(ZROWS * field + 16 * (tile + 1), 16), :])
    move = (begin_at - at) % LANES
    return pltpu.roll(value, move, 1) if move else value


def coarsen(ref, level, base, tmp, scale):
    rows = OWN[level]
    half = rows // 2
    bit = STEP[level]
    even = (lanes_of(half) // bit) % 2 == 0
    for a in range(N[level] // 2):
        at = base + OBASE[level] + 2 * a * rows
        tmp[pl.ds(a * rows, rows), :] = ref[pl.ds(at, rows), :] + ref[pl.ds(at + rows, rows), :]
    for a in range(N[level] // 2):
        pair = tmp[pl.ds(a * rows, half, 2), :] + tmp[pl.ds(a * rows + 1, half, 2), :]
        other = jnp.where(even, pltpu.roll(pair, LANES - bit, 1), pltpu.roll(pair, bit, 1))
        ref[pl.ds(base + OBASE[level + 1] + a * half, half), :] = (pair + other) * scale


def slots(vectors):
    shared = vectors[0]
    slot = (lanes_of(shared.shape[0]) + 21) // 42
    for i in (1, 2):
        shared = jnp.where(slot == i, pltpu.roll(vectors[i], 42 * i, 1), shared)
    return shared


def unslots(shared):
    return [shared] + [pltpu.roll(shared, LANES - 42 * i, 1) for i in (1, 2)]


def x_faces(own_ref, base, up_ref, down_ref, xbase, count):
    lane = lanes_of(16)
    odd = lane % 2 == 1
    turn = lanes_of(8) % 4
    for dst, end in ((up_ref, 1), (down_ref, 0)):
        at = [base + OBASE[level] + end * (N[level] - count) * OWN[level] for level in range(3)]
        to = xbase
        for i in range(count):
            dst[pl.ds(to, 16), :] = own_ref[pl.ds(at[0] + 32 * i, 16), :]
            to += 16
        shared = own_ref[pl.ds(at[0] + 16, 16), :]
        for i in range(1, count):
            moved = pltpu.roll(own_ref[pl.ds(at[0] + 32 * i + 16, 16), :], 32 * i, 1)
            shared = jnp.where((lane + 16) // 32 == i, moved, shared)
        dst[pl.ds(to, 16), :] = shared
        c = [own_ref[pl.ds(at[1] + 16 * i, 16), :] for i in range(count)]
        if count == 3:
            dst[pl.ds(to + 16, 8), :] = jnp.where(odd[:8], c[1][:8], c[0][:8])
            dst[pl.ds(to + 24, 8), :] = jnp.where(odd[:8], slots([v[8:] for v in c]), c[2][:8])
        else:
            dst[pl.ds(to + 16, 16), :] = jnp.where(odd, c[1], c[0])
        to += 32
        c = [own_ref[pl.ds(at[2] + 8 * i, 8), :] for i in range(count)]
        shared = c[0]
        for i in range(1, count):
            shared = jnp.where(turn == i, c[i], shared)
        dst[pl.ds(to, 8), :] = shared


def unpack(src, at, dst, to, count, skip):
    odd = lanes_of(16) % 2 == 1
    turn = lanes_of(8) % 4
    for level in range(3):
        rows = OWN[level]
        for i in range(HALO):
            if not skip <= i < skip + count:
                dst[pl.ds(to + XBASE[level] + rows * i, rows), :] = jnp.zeros((rows, LANES), F32)
    to1, to2, to3 = (to + XBASE[level] + skip * OWN[level] for level in range(3))
    for i in range(count):
        dst[pl.ds(to1 + 32 * i, 16), :] = src[pl.ds(at, 16), :]
        at += 16
    shared = src[pl.ds(at, 16), :]
    for i in range(count):
        dst[pl.ds(to1 + 32 * i + 16, 16), :] = pltpu.roll(shared, LANES - 32 * i, 1) if i else shared

    def two(value):
        mask = odd[: value.shape[0]]
        return jnp.where(mask, pltpu.roll(value, 1, 1), value), jnp.where(mask, value, pltpu.roll(value, LANES - 1, 1))

    first = two(src[pl.ds(at + 16, 16), :])
    if count == 3:
        for i, value in enumerate((first[0][:8], first[1][:8], first[0][8:])):
            dst[pl.ds(to2 + 16 * i, 8), :] = value
        for i, value in enumerate(unslots(first[1][8:])):
            dst[pl.ds(to2 + 16 * i + 8, 8), :] = value
    else:
        dst[pl.ds(to2, 16), :] = first[0]
        dst[pl.ds(to2 + 16, 16), :] = first[1]
    at += 32
    c = src[pl.ds(at, 8), :]
    moved = {d: pltpu.roll(c, d % LANES, 1) if d else c for d in range(1 - count, 4)}
    for i in range(count):
        value = moved[-i]
        for lane in range(1, 4):
            value = jnp.where(turn == lane, moved[lane - i], value)
        dst[pl.ds(to3 + 8 * i, 8), :] = value


def begin(fk_ref, zl_ref, zr_ref, raw_ref, own_ref, w_ref, up_ref, down_ref, tmp):
    low = lanes_of(16) < 64
    for field, ref in enumerate((fk_ref.at[pl.ds(0, 256), :], fk_ref.at[pl.ds(256, 256), :])):
        base = field * OROWS
        for i in range(16):
            from_l = z_slab(zl_ref, field, i, LANES - ZWIDTH)
            from_r = z_slab(zr_ref, field, i, 0)
            raw_ref[pl.ds(base + 32 * i, 16), :] = ref[pl.ds(16 * i, 16), :]
            raw_ref[pl.ds(base + 32 * i + 16, 16), :] = jnp.where(low, from_r, from_l)
        scale = 0.125 if field == 0 else 0.125 * 0.25
        coarsen(raw_ref, 0, base, tmp, scale)
        coarsen(raw_ref, 1, base, tmp, scale)
    for at in range(0, CELLS, 32):
        c = raw_ref[pl.ds(OROWS + at, 32), :]
        w = 0.8 / (14.0 * c + 1.0)
        w_ref[pl.ds(at, 32), :] = w
        own_ref[pl.ds(at, 32), :] = w * raw_ref[pl.ds(at, 32), :]
        own_ref[pl.ds(OROWS + at, 32), :] = 0.25 * (w * c)
    for field in range(2):
        x_faces(own_ref, field * OROWS, up_ref, down_ref, PACKED[field], LAYERS[field])


def y_parts(count):
    parts, at = [], 0
    for j in range(count):
        parts.append((at, 0, ((0, j),), None))
        at += X[0]
    for j in range(0, count, 2):
        members = tuple((h, k) for k in range(j, min(j + 2, count)) for h in range(2))
        parts.append((at, 2, members, "turns"))
        at += X[2]
    if count == 3:
        second = ((((0, 0), (0, 1)), "turns"), (((0, 2), (1, 0), (1, 1), (1, 2)), "slots"))
    else:
        second = tuple((((0, j), (1, j)), "turns") for j in range(count))
    for members, how in second:
        parts.append((at, 1, members, how))
        at += X[1]
    parts.append((at, 0, tuple((1, j) for j in range(count)), "lanes"))
    return parts


def share(vectors, how):
    if how == "slots":
        vectors, how = [vectors[0], slots(vectors[1:])], "turns"
    shared = vectors[0]
    lane = lanes_of(shared.shape[0])
    for i in range(1, len(vectors)):
        if how == "lanes":
            shared = jnp.where((lane + 16) // 32 == i, pltpu.roll(vectors[i], 32 * i, 1), shared)
        else:
            shared = jnp.where(lane % len(vectors) == i, vectors[i], shared)
    return shared


def unshare(shared, number, how):
    if how == "slots":
        first, rest = unshare(shared, 2, "turns")
        return [first] + unslots(rest)
    if how != "turns":
        return [pltpu.roll(shared, LANES - 32 * i, 1) if i else shared for i in range(number)]
    turn = lanes_of(shared.shape[0]) % number
    moved = {d: pltpu.roll(shared, d % LANES, 1) if d else shared for d in range(1 - number, number)}
    vectors = []
    for i in range(number):
        value = moved[-i]
        for lane in range(1, number):
            value = jnp.where(turn == lane, moved[lane - i], value)
        vectors.append(value)
    return vectors


def y_faces(fields, own_ref, xl_packed, xr_packed, up_ref, down_ref, xl_ref, xr_ref, rows_ref):
    for field in range(fields):
        ob, xb, yb, count = field * OROWS, field * XROWS, YROWS[field], LAYERS[field]
        unpack(xl_packed, PACKED[field], xl_ref, xb, count, HALO - count)
        unpack(xr_packed, PACKED[field], xr_ref, xb, count, 0)
        for side, (dst, first) in enumerate(((up_ref, False), (down_ref, True))):
            for at, level, members, how in y_parts(count):
                n, rows, size = N[level], OWN[level], X[level]
                vectors = []
                for m, (h, j) in enumerate(members):
                    row = h * n + (j if first else n - count + j)
                    to = 24 * (m + 4 * (side + 2 * field))
                    if len(members) == 1:
                        ref, to = dst, yb + at
                    else:
                        ref = rows_ref
                    ref[pl.ds(to, HALO), :] = xl_ref[pl.ds(xb + XBASE[level] + row, HALO, rows), :]
                    ref[pl.ds(to + HALO, n), :] = own_ref[pl.ds(ob + OBASE[level] + row, n, rows), :]
                    ref[pl.ds(to + HALO + n, HALO), :] = xr_ref[pl.ds(xb + XBASE[level] + row, HALO, rows), :]
                    if len(members) > 1:
                        vectors.append(ref[pl.ds(to, size), :])
                if vectors:
                    dst[pl.ds(yb + at, size), :] = share(vectors, how)


def widen(field, own_ref, xl_ref, xr_ref, yl_ref, yr_ref, wide_ref):
    ob, xb, yb, count = field * OROWS, field * XROWS, YROWS[field], LAYERS[field]
    for level in range(3):
        n, ring, rows = N[level], RING[level], OWN[level]
        for i in range(X[level]):
            if i < HALO:
                ref, at = xl_ref, xb + XBASE[level] + i * rows
            elif i < HALO + n:
                ref, at = own_ref, ob + OBASE[level] + (i - HALO) * rows
            else:
                ref, at = xr_ref, xb + XBASE[level] + (i - HALO - n) * rows
            for h in range(2):
                to = WBASE[level] + i * WIDE[level] + h * ring
                wide_ref[pl.ds(to, n), :] = ref[pl.ds(at + h * n, n), :]
    for at, level, members, how in y_parts(count):
        n, ring, size = N[level], RING[level], X[level]
        for ref, start in ((yr_ref, n), (yl_ref, ring - count)):
            shared = ref[pl.ds(yb + at, size), :]
            for (h, j), vector in zip(members, unshare(shared, len(members), how)):
                wide_ref[pl.ds(WBASE[level] + h * ring + start + j, size, WIDE[level]), :] = vector


def slab(ref, base, i, rows):
    return ref[pl.ds(pl.multiple_of(base + i * rows, 8), rows), :]


def put(ref, base, i, rows, value):
    ref[pl.ds(pl.multiple_of(base + i * rows, 8), rows), :] = value


def loop(low, high, value, store):
    groups = -(-(high - low) // UNROLL)
    size = -(-(high - low) // groups)
    lead = (high - low) - (groups - 1) * size

    def group(first, count):
        values = [value(first + u) for u in range(count)]
        for u in range(count):
            store(first + u, values[u])

    def step(g, carry):
        group(low + lead + g * size, size)
        return carry

    group(low, lead)
    if groups > 1:
        lax.fori_loop(0, groups - 1, step, 0)


def ring_sum(ref, base, i, ring, step):
    rows = 2 * ring
    mid = slab(ref, base, i, rows)
    total = slab(ref, base, i - 1, rows) + slab(ref, base, i + 1, rows) + (mid + mid)
    halves = []
    for h in range(2):
        t = total[h * ring : (h + 1) * ring]
        halves.append((pltpu.roll(t, 1, 0) + pltpu.roll(t, ring - 1, 0)) + (t + t))
    lane = lanes_of(ring)
    a, b = halves
    ra, rb = pltpu.roll(a, step, 1), pltpu.roll(b, step, 1)
    sa, sb = pltpu.roll(a, LANES - step, 1), pltpu.roll(b, LANES - step, 1)
    low, high = lane < step, lane >= LANES - step
    new_a = (a + a) + (jnp.where(low, rb, ra) + jnp.where(high, sb, sa))
    new_b = (b + b) + (jnp.where(low, ra, rb) + jnp.where(high, sa, sb))
    return mid, new_a, new_b


def join(a, b):
    return jnp.concatenate([a, b], axis=0)


def sweeps(wide_b, wide_u, first, second):
    def sweep(edge, groups, src, dst):
        def value(level, i):
            rows, base = WIDE[level], WBASE[level]
            mid, a, b = ring_sum(src, base, i, RING[level], STEP[level])
            around = slab(wide_u, base, i, rows) * (join(a, b) - 8.0 * mid)
            return 0.2 * mid + slab(wide_b, base, i, rows) + around

        def group(g):
            done = []
            for level in range(3):
                high = X[level] - edge
                size = -(-(high - edge) // groups)
                start = jnp.minimum(edge + g * size, high - size)
                done += [(level, start + u, value(level, start + u)) for u in range(size)]
            for level, i, new in done:
                put(dst, WBASE[level], i, WIDE[level], new)

        pl.loop(0, groups)(group)

    sweep(1, GROUPS[0], wide_b, first)
    sweep(2, GROUPS[1], first, second)


def prolong(err, up3, up2):
    for q in range(6):
        for h in range(2):
            e3 = err[pl.ds(WBASE[2] + (q + 2) * 32 + h * 16, 16), :]
            to = q * 32 + h * 16
            up3[pl.ds(to, 5, 2), :] = e3[0:5]
            up3[pl.ds(to + 1, 5, 2), :] = e3[0:5]
            up3[pl.ds(to + 10, 4), :] = jnp.zeros((4, LANES), F32)
            up3[pl.ds(to + 14, 2), :] = jnp.broadcast_to(e3[15:16], (2, LANES))
    for a in range(10):
        for h in range(2):
            e2 = err[pl.ds(WBASE[1] + (a + 2) * 32 + h * 16, 16), :]
            e2 = e2 + up3[pl.ds(((a - 1) // 2 + 1) * 32 + h * 16, 16), :]
            to = a * 48 + h * 24
            up2[pl.ds(to, 9, 2), :] = e2[0:9]
            up2[pl.ds(to + 1, 9, 2), :] = e2[0:9]
            up2[pl.ds(to + 18, 4), :] = jnp.zeros((4, LANES), F32)
            up2[pl.ds(to + 22, 2), :] = jnp.broadcast_to(e2[15:16], (2, LANES))


def correct(err, up2, old_ref, sol_ref):
    for i in range(18):
        value = err[pl.ds((i + 2) * 48, 48), :] + up2[pl.ds(((i - 1) // 2 + 1) * 48, 48), :]
        if old_ref is not None:
            value = value + old_ref[pl.ds(i * 48, 48), :]
        sol_ref[pl.ds(i * 48, 48), :] = value


def first_round(
    raw_ref, own_ref, w_ref, xl_ref, xr_ref, yl_ref, yr_ref,
    next_ref, up_ref, down_ref, sol_ref, wide_u,
    wide_b, first, second, up3, up2, r_ref, tmp,
):
    widen(0, own_ref, xl_ref, xr_ref, yl_ref, yr_ref, wide_b)
    widen(1, own_ref, xl_ref, xr_ref, yl_ref, yr_ref, wide_u)
    sweeps(wide_b, wide_u, first, second)
    prolong(second, up3, up2)
    correct(second, up2, None, sol_ref)

    def resid(i):
        mid, a, b = ring_sum(sol_ref, 0, i + 1, 24, 1)
        halves = []
        for h, t in enumerate((a, b)):
            s = mid[h * 24 : h * 24 + 16]
            f = raw_ref[pl.ds(pl.multiple_of(i * 32 + h * 16, 16), 16), :]
            k = raw_ref[pl.ds(pl.multiple_of(OROWS + i * 32 + h * 16, 16), 16), :]
            halves.append(f - (k * (16.0 * s - 0.25 * t[:16]) + s))
        return join(*halves)

    loop(0, 16, resid, lambda i, new: put(r_ref, 0, i, 32, new))
    coarsen(r_ref, 0, 0, tmp, 0.125)
    coarsen(r_ref, 1, 0, tmp, 0.125)
    for at in range(0, CELLS, 32):
        next_ref[pl.ds(at, 32), :] = w_ref[pl.ds(at, 32), :] * r_ref[pl.ds(at, 32), :]
    x_faces(next_ref, 0, up_ref, down_ref, 0, LAYERS[0])


def second_round(
    fk_ref, own_ref, xl_ref, xr_ref, yl_ref, yr_ref, old_ref, wide_u,
    out_hbm, resid_hbm,
    wide_b, first, second, sol_ref, up3, up2, out_ref, resid_ref, sems,
):
    widen(0, own_ref, xl_ref, xr_ref, yl_ref, yr_ref, wide_b)
    sweeps(wide_b, wide_u, first, second)
    prolong(second, up3, up2)
    correct(second, up2, old_ref, sol_ref)
    for i in range(16):
        out_ref[pl.ds(16 * i, 16), :] = sol_ref[pl.ds(48 * (i + 1), 16), :]
    copies = [pltpu.make_async_copy(out_ref, out_hbm, sems.at[0])]
    copies[0].start()

    def resid(i):
        mid, a, _ = ring_sum(sol_ref, 0, i + 1, 24, 1)
        s = mid[:16]
        return slab(fk_ref, 0, i, 16) - (slab(fk_ref, 256, i, 16) * (16.0 * s - 0.25 * a[:16]) + s)

    for half in range(2):
        loop(8 * half, 8 * half + 8, resid, lambda i, new: put(resid_ref, 0, i, 16, new))
        at = pl.ds(128 * half, 128)
        copies.append(pltpu.make_async_copy(resid_ref.at[at, :], resid_hbm.at[at, :], sems.at[1 + half]))
        copies[-1].start()
    for copy in copies:
        copy.wait()


def exchange(up, down, axis):
    size = lax.axis_size(axis)
    odd = lax.axis_index(axis) % 2 == 1
    outer = [(i, i + 1) for i in range(1, size - 1, 2)]
    outer = outer + [(j, i) for i, j in outer]
    inner = [[i, i + 1] for i in range(0, size, 2)]
    two = lax.ppermute(jnp.where(odd, up, down), axis, outer)
    one = lax.all_gather(jnp.where(odd, down, up), axis, axis_index_groups=inner)
    return jnp.where(odd, one[0], two), jnp.where(odd, two, one[1])


def shards(forcing, kappa):
    shape = forcing.shape
    f = forcing.reshape(256, LANES)
    k = kappa.reshape(256, LANES)
    fk = lax.optimization_barrier(jnp.concatenate([f, k]))
    up, down = call(z_faces, [2 * ZROWS, 2 * ZROWS], [], fk)
    zl, zr = exchange(up, down, "grp")
    raw, own, w, up, down = call(
        begin, [2 * OROWS, 2 * OROWS, OROWS, PACKED[2], PACKED[2]], [264], fk, zl, zr
    )
    xl, xr = exchange(up, down, "gx")

    def faces(fields, own, xl, xr):
        def kernel(*refs):
            y_faces(fields, *refs)

        return call(kernel, [YROWS[fields]] * 2 + [fields * XROWS] * 2, [400], own, xl, xr)

    up, down, xl, xr = faces(2, own, xl, xr)
    yl, yr = exchange(up, down, "gy")
    own, up, down, sol, wide_u = call(
        first_round,
        [OROWS, PACKED[1], PACKED[1], SOLROWS, WROWS],
        [WROWS, WROWS, WROWS, 208, 496, OROWS, 264],
        raw, own, w, xl, xr, yl, yr,
    )
    xl, xr = exchange(up, down, "gx")
    up, down, xl, xr = faces(1, own, xl, xr)
    yl, yr = exchange(up, down, "gy")
    out, resid = call(
        second_round,
        [256, 256],
        [WROWS, WROWS, WROWS, SOLROWS, 208, 496, 256, 256],
        fk, own, xl, xr, yl, yr, sol, wide_u,
        out_specs=[HBM, HBM], copies=3,
    )
    return out.reshape(shape), resid.reshape(shape)


def solution(mesh):
    placed = (P("gx", "gy", "grp"), P("gx", "gy", "grp"))
    return jax.shard_map(shards, mesh=mesh, in_specs=placed, out_specs=placed, check_vma=False)
```

```python
import jax
import jax.numpy as jnp
from jax import lax
from jax.experimental import pallas as pl
from jax.experimental.pallas import tpu as pltpu
from jax.sharding import PartitionSpec as P

F32 = jnp.float32
LANES = 128
HALO = 3
N = (16, 8, 4)
X = tuple(n + 2 * HALO for n in N)
RING = (24, 16, 16)
STEP = (1, 2, 4)
OWN = tuple(2 * n for n in N)
WIDE = tuple(2 * r for r in RING)
OBASE = (0, 512, 640)
ZWIDTH = 24
ZROWS = 48
CELLS = 672
OROWS = 704
XBASE = (0, 96, 144)
XROWS = 256
YROWS = (0, 144, 256)
PACKED = (0, 88, 160)
LAYERS = (3, 2)
UNROLL = 8
GROUPS = (3, 2)
WBASE = (0, 1056, 1504)
WROWS = 2048
SOLROWS = 18 * 48
VMEM_LIMIT = 48 * 1024 * 1024


def lanes_of(rows):
    return lax.broadcasted_iota(jnp.int32, (rows, LANES), 1)


VM = pl.BlockSpec(memory_space=pltpu.VMEM)
HBM = pl.BlockSpec(memory_space=pl.ANY)


def call(kernel, outs, scratch, *args, out_specs=None, copies=0):
    return pl.pallas_call(
        kernel,
        out_shape=[jax.ShapeDtypeStruct((rows, LANES), F32) for rows in outs],
        in_specs=[VM] * len(args),
        out_specs=out_specs or [VM] * len(outs),
        scratch_shapes=[pltpu.VMEM((rows, LANES), F32) for rows in scratch]
        + ([pltpu.SemaphoreType.DMA((copies,))] if copies else []),
        compiler_params=pltpu.CompilerParams(vmem_limit_bytes=VMEM_LIMIT),
    )(*args)


def z_faces(fk_ref, up_ref, down_ref):
    lane = lanes_of(16)
    for field in range(2):
        for tile in range(3):
            slot = (lane + LANES * tile) // ZWIDTH
            members = range(LANES * tile // ZWIDTH, (LANES * (tile + 1) - 1) // ZWIDTH + 1)
            for dst, begin_at in ((up_ref, LANES - ZWIDTH), (down_ref, 0)):
                shared = None
                for i in members:
                    value = fk_ref[pl.ds(256 * field + 16 * i, 16), :]
                    move = (ZWIDTH * i - begin_at) % LANES
                    value = pltpu.roll(value, move, 1) if move else value
                    shared = value if shared is None else jnp.where(slot == i, value, shared)
                dst[pl.ds(ZROWS * field + 16 * tile, 16), :] = shared


def z_slab(ref, field, i, begin_at):
    tile, at = divmod(ZWIDTH * i, LANES)
    value = ref[pl.ds(ZROWS * field + 16 * tile, 16), :]
    if at + ZWIDTH > LANES:
        value = jnp.where(lanes_of(16) >= at, value, ref[pl.ds(ZROWS * field + 16 * (tile + 1), 16), :])
    move = (begin_at - at) % LANES
    return pltpu.roll(value, move, 1) if move else value


def coarsen(ref, level, base, tmp, scale):
    rows = OWN[level]
    half = rows // 2
    bit = STEP[level]
    even = (lanes_of(half) // bit) % 2 == 0
    for a in range(N[level] // 2):
        at = base + OBASE[level] + 2 * a * rows
        tmp[pl.ds(a * rows, rows), :] = ref[pl.ds(at, rows), :] + ref[pl.ds(at + rows, rows), :]
    for a in range(N[level] // 2):
        pair = tmp[pl.ds(a * rows, half, 2), :] + tmp[pl.ds(a * rows + 1, half, 2), :]
        other = jnp.where(even, pltpu.roll(pair, LANES - bit, 1), pltpu.roll(pair, bit, 1))
        ref[pl.ds(base + OBASE[level + 1] + a * half, half), :] = (pair + other) * scale


def slots(vectors):
    shared = vectors[0]
    slot = (lanes_of(shared.shape[0]) + 21) // 42
    for i in (1, 2):
        shared = jnp.where(slot == i, pltpu.roll(vectors[i], 42 * i, 1), shared)
    return shared


def unslots(shared):
    return [shared] + [pltpu.roll(shared, LANES - 42 * i, 1) for i in (1, 2)]


def x_faces(own_ref, base, up_ref, down_ref, xbase, count):
    lane = lanes_of(16)
    odd = lane % 2 == 1
    turn = lanes_of(8) % 4
    for dst, end in ((up_ref, 1), (down_ref, 0)):
        at = [base + OBASE[level] + end * (N[level] - count) * OWN[level] for level in range(3)]
        to = xbase
        for i in range(count):
            dst[pl.ds(to, 16), :] = own_ref[pl.ds(at[0] + 32 * i, 16), :]
            to += 16
        shared = own_ref[pl.ds(at[0] + 16, 16), :]
        for i in range(1, count):
            moved = pltpu.roll(own_ref[pl.ds(at[0] + 32 * i + 16, 16), :], 32 * i, 1)
            shared = jnp.where((lane + 16) // 32 == i, moved, shared)
        dst[pl.ds(to, 16), :] = shared
        c = [own_ref[pl.ds(at[1] + 16 * i, 16), :] for i in range(count)]
        if count == 3:
            dst[pl.ds(to + 16, 8), :] = jnp.where(odd[:8], c[1][:8], c[0][:8])
            dst[pl.ds(to + 24, 8), :] = jnp.where(odd[:8], slots([v[8:] for v in c]), c[2][:8])
        else:
            dst[pl.ds(to + 16, 16), :] = jnp.where(odd, c[1], c[0])
        to += 32
        c = [own_ref[pl.ds(at[2] + 8 * i, 8), :] for i in range(count)]
        shared = c[0]
        for i in range(1, count):
            shared = jnp.where(turn == i, c[i], shared)
        dst[pl.ds(to, 8), :] = shared


def unpack(src, at, dst, to, count, skip):
    odd = lanes_of(16) % 2 == 1
    turn = lanes_of(8) % 4
    for level in range(3):
        rows = OWN[level]
        for i in range(HALO):
            if not skip <= i < skip + count:
                dst[pl.ds(to + XBASE[level] + rows * i, rows), :] = jnp.zeros((rows, LANES), F32)
    to1, to2, to3 = (to + XBASE[level] + skip * OWN[level] for level in range(3))
    for i in range(count):
        dst[pl.ds(to1 + 32 * i, 16), :] = src[pl.ds(at, 16), :]
        at += 16
    shared = src[pl.ds(at, 16), :]
    for i in range(count):
        dst[pl.ds(to1 + 32 * i + 16, 16), :] = pltpu.roll(shared, LANES - 32 * i, 1) if i else shared

    def two(value):
        mask = odd[: value.shape[0]]
        return jnp.where(mask, pltpu.roll(value, 1, 1), value), jnp.where(mask, value, pltpu.roll(value, LANES - 1, 1))

    first = two(src[pl.ds(at + 16, 16), :])
    if count == 3:
        for i, value in enumerate((first[0][:8], first[1][:8], first[0][8:])):
            dst[pl.ds(to2 + 16 * i, 8), :] = value
        for i, value in enumerate(unslots(first[1][8:])):
            dst[pl.ds(to2 + 16 * i + 8, 8), :] = value
    else:
        dst[pl.ds(to2, 16), :] = first[0]
        dst[pl.ds(to2 + 16, 16), :] = first[1]
    at += 32
    c = src[pl.ds(at, 8), :]
    moved = {d: pltpu.roll(c, d % LANES, 1) if d else c for d in range(1 - count, 4)}
    for i in range(count):
        value = moved[-i]
        for lane in range(1, 4):
            value = jnp.where(turn == lane, moved[lane - i], value)
        dst[pl.ds(to3 + 8 * i, 8), :] = value


def begin(fk_ref, zl_ref, zr_ref, raw_ref, own_ref, w_ref, up_ref, down_ref, tmp):
    low = lanes_of(16) < 64
    for field, ref in enumerate((fk_ref.at[pl.ds(0, 256), :], fk_ref.at[pl.ds(256, 256), :])):
        base = field * OROWS
        for i in range(16):
            from_l = z_slab(zl_ref, field, i, LANES - ZWIDTH)
            from_r = z_slab(zr_ref, field, i, 0)
            raw_ref[pl.ds(base + 32 * i, 16), :] = ref[pl.ds(16 * i, 16), :]
            raw_ref[pl.ds(base + 32 * i + 16, 16), :] = jnp.where(low, from_r, from_l)
        scale = 0.125 if field == 0 else 0.125 * 0.25
        coarsen(raw_ref, 0, base, tmp, scale)
        coarsen(raw_ref, 1, base, tmp, scale)
    for at in range(0, CELLS, 32):
        c = raw_ref[pl.ds(OROWS + at, 32), :]
        w = 0.8 / (14.0 * c + 1.0)
        w_ref[pl.ds(at, 32), :] = w
        own_ref[pl.ds(at, 32), :] = w * raw_ref[pl.ds(at, 32), :]
        own_ref[pl.ds(OROWS + at, 32), :] = 0.25 * (w * c)
    for field in range(2):
        x_faces(own_ref, field * OROWS, up_ref, down_ref, PACKED[field], LAYERS[field])


def y_parts(count):
    parts, at = [], 0
    for j in range(count):
        parts.append((at, 0, ((0, j),), None))
        at += X[0]
    for j in range(0, count, 2):
        members = tuple((h, k) for k in range(j, min(j + 2, count)) for h in range(2))
        parts.append((at, 2, members, "turns"))
        at += X[2]
    if count == 3:
        second = ((((0, 0), (0, 1)), "turns"), (((0, 2), (1, 0), (1, 1), (1, 2)), "slots"))
    else:
        second = tuple((((0, j), (1, j)), "turns") for j in range(count))
    for members, how in second:
        parts.append((at, 1, members, how))
        at += X[1]
    parts.append((at, 0, tuple((1, j) for j in range(count)), "lanes"))
    return parts


def share(vectors, how):
    if how == "slots":
        vectors, how = [vectors[0], slots(vectors[1:])], "turns"
    shared = vectors[0]
    lane = lanes_of(shared.shape[0])
    for i in range(1, len(vectors)):
        if how == "lanes":
            shared = jnp.where((lane + 16) // 32 == i, pltpu.roll(vectors[i], 32 * i, 1), shared)
        else:
            shared = jnp.where(lane % len(vectors) == i, vectors[i], shared)
    return shared


def unshare(shared, number, how):
    if how == "slots":
        first, rest = unshare(shared, 2, "turns")
        return [first] + unslots(rest)
    if how != "turns":
        return [pltpu.roll(shared, LANES - 32 * i, 1) if i else shared for i in range(number)]
    turn = lanes_of(shared.shape[0]) % number
    moved = {d: pltpu.roll(shared, d % LANES, 1) if d else shared for d in range(1 - number, number)}
    vectors = []
    for i in range(number):
        value = moved[-i]
        for lane in range(1, number):
            value = jnp.where(turn == lane, moved[lane - i], value)
        vectors.append(value)
    return vectors


def y_faces(fields, own_ref, xl_packed, xr_packed, up_ref, down_ref, xl_ref, xr_ref, rows_ref):
    for field in range(fields):
        ob, xb, yb, count = field * OROWS, field * XROWS, YROWS[field], LAYERS[field]
        unpack(xl_packed, PACKED[field], xl_ref, xb, count, HALO - count)
        unpack(xr_packed, PACKED[field], xr_ref, xb, count, 0)
        for side, (dst, first) in enumerate(((up_ref, False), (down_ref, True))):
            for at, level, members, how in y_parts(count):
                n, rows, size = N[level], OWN[level], X[level]
                vectors = []
                for m, (h, j) in enumerate(members):
                    row = h * n + (j if first else n - count + j)
                    to = 24 * (m + 4 * (side + 2 * field))
                    if len(members) == 1:
                        ref, to = dst, yb + at
                    else:
                        ref = rows_ref
                    ref[pl.ds(to, HALO), :] = xl_ref[pl.ds(xb + XBASE[level] + row, HALO, rows), :]
                    ref[pl.ds(to + HALO, n), :] = own_ref[pl.ds(ob + OBASE[level] + row, n, rows), :]
                    ref[pl.ds(to + HALO + n, HALO), :] = xr_ref[pl.ds(xb + XBASE[level] + row, HALO, rows), :]
                    if len(members) > 1:
                        vectors.append(ref[pl.ds(to, size), :])
                if vectors:
                    dst[pl.ds(yb + at, size), :] = share(vectors, how)


def widen(field, own_ref, xl_ref, xr_ref, yl_ref, yr_ref, wide_ref):
    ob, xb, yb, count = field * OROWS, field * XROWS, YROWS[field], LAYERS[field]
    for level in range(3):
        n, ring, rows = N[level], RING[level], OWN[level]
        for i in range(HALO - count, X[level] - HALO + count):
            if i < HALO:
                ref, at = xl_ref, xb + XBASE[level] + i * rows
            elif i < HALO + n:
                ref, at = own_ref, ob + OBASE[level] + (i - HALO) * rows
            else:
                ref, at = xr_ref, xb + XBASE[level] + (i - HALO - n) * rows
            for h in range(2):
                to = WBASE[level] + i * WIDE[level] + h * ring
                wide_ref[pl.ds(to, n), :] = ref[pl.ds(at + h * n, n), :]
    for at, level, members, how in y_parts(count):
        n, ring, size = N[level], RING[level], X[level]
        for ref, start in ((yr_ref, n), (yl_ref, ring - count)):
            shared = ref[pl.ds(yb + at, size), :]
            for (h, j), vector in zip(members, unshare(shared, len(members), how)):
                wide_ref[pl.ds(WBASE[level] + h * ring + start + j, size, WIDE[level]), :] = vector


def slab(ref, base, i, rows):
    return ref[pl.ds(pl.multiple_of(base + i * rows, 8), rows), :]


def put(ref, base, i, rows, value):
    ref[pl.ds(pl.multiple_of(base + i * rows, 8), rows), :] = value


def loop(low, high, value, store):
    groups = -(-(high - low) // UNROLL)
    size = -(-(high - low) // groups)
    lead = (high - low) - (groups - 1) * size

    def group(first, count):
        values = [value(first + u) for u in range(count)]
        for u in range(count):
            store(first + u, values[u])

    def step(g, carry):
        group(low + lead + g * size, size)
        return carry

    group(low, lead)
    if groups > 1:
        lax.fori_loop(0, groups - 1, step, 0)


def ring_sum(ref, base, i, ring, step):
    rows = 2 * ring
    mid = slab(ref, base, i, rows)
    total = slab(ref, base, i - 1, rows) + slab(ref, base, i + 1, rows) + (mid + mid)
    halves = []
    for h in range(2):
        t = total[h * ring : (h + 1) * ring]
        halves.append((pltpu.roll(t, 1, 0) + pltpu.roll(t, ring - 1, 0)) + (t + t))
    lane = lanes_of(ring)
    a, b = halves
    ra, rb = pltpu.roll(a, step, 1), pltpu.roll(b, step, 1)
    sa, sb = pltpu.roll(a, LANES - step, 1), pltpu.roll(b, LANES - step, 1)
    low, high = lane < step, lane >= LANES - step
    new_a = (a + a) + (jnp.where(low, rb, ra) + jnp.where(high, sb, sa))
    new_b = (b + b) + (jnp.where(low, ra, rb) + jnp.where(high, sa, sb))
    return mid, new_a, new_b


def join(a, b):
    return jnp.concatenate([a, b], axis=0)


def sweeps(wide_b, wide_u, first, second):
    def sweep(edge, groups, src, dst):
        def value(level, i):
            rows, base = WIDE[level], WBASE[level]
            mid, a, b = ring_sum(src, base, i, RING[level], STEP[level])
            around = slab(wide_u, base, i, rows) * (join(a, b) - 8.0 * mid)
            return 0.2 * mid + slab(wide_b, base, i, rows) + around

        def group(g):
            done = []
            for level in range(3):
                high = X[level] - edge
                size = -(-(high - edge) // groups)
                start = jnp.minimum(edge + g * size, high - size)
                done += [(level, start + u, value(level, start + u)) for u in range(size)]
            for level, i, new in done:
                put(dst, WBASE[level], i, WIDE[level], new)

        pl.loop(0, groups)(group)

    sweep(1, GROUPS[0], wide_b, first)
    sweep(2, GROUPS[1], first, second)


def prolong(err, up3, up2):
    for q in range(6):
        for h in range(2):
            e3 = err[pl.ds(WBASE[2] + (q + 2) * 32 + h * 16, 16), :]
            to = q * 32 + h * 16
            up3[pl.ds(to, 5, 2), :] = e3[0:5]
            up3[pl.ds(to + 1, 5, 2), :] = e3[0:5]
            up3[pl.ds(to + 10, 4), :] = jnp.zeros((4, LANES), F32)
            up3[pl.ds(to + 14, 2), :] = jnp.broadcast_to(e3[15:16], (2, LANES))
    for a in range(10):
        for h in range(2):
            e2 = err[pl.ds(WBASE[1] + (a + 2) * 32 + h * 16, 16), :]
            e2 = e2 + up3[pl.ds(((a - 1) // 2 + 1) * 32 + h * 16, 16), :]
            to = a * 48 + h * 24
            up2[pl.ds(to, 9, 2), :] = e2[0:9]
            up2[pl.ds(to + 1, 9, 2), :] = e2[0:9]
            up2[pl.ds(to + 18, 4), :] = jnp.zeros((4, LANES), F32)
            up2[pl.ds(to + 22, 2), :] = jnp.broadcast_to(e2[15:16], (2, LANES))


def correct(err, up2, old_ref, sol_ref):
    for i in range(18):
        value = err[pl.ds((i + 2) * 48, 48), :] + up2[pl.ds(((i - 1) // 2 + 1) * 48, 48), :]
        if old_ref is not None:
            value = value + old_ref[pl.ds(i * 48, 48), :]
        sol_ref[pl.ds(i * 48, 48), :] = value


def first_round(
    raw_ref, own_ref, w_ref, xl_ref, xr_ref, yl_ref, yr_ref,
    next_ref, up_ref, down_ref, sol_ref, wide_u,
    wide_b, first, second, up3, up2, r_ref, tmp,
):
    widen(0, own_ref, xl_ref, xr_ref, yl_ref, yr_ref, wide_b)
    widen(1, own_ref, xl_ref, xr_ref, yl_ref, yr_ref, wide_u)
    sweeps(wide_b, wide_u, first, second)
    prolong(second, up3, up2)
    correct(second, up2, None, sol_ref)

    def resid(i):
        mid, a, b = ring_sum(sol_ref, 0, i + 1, 24, 1)
        halves = []
        for h, t in enumerate((a, b)):
            s = mid[h * 24 : h * 24 + 16]
            f = raw_ref[pl.ds(pl.multiple_of(i * 32 + h * 16, 16), 16), :]
            k = raw_ref[pl.ds(pl.multiple_of(OROWS + i * 32 + h * 16, 16), 16), :]
            halves.append(f - (k * (16.0 * s - 0.25 * t[:16]) + s))
        return join(*halves)

    loop(0, 16, resid, lambda i, new: put(r_ref, 0, i, 32, new))
    coarsen(r_ref, 0, 0, tmp, 0.125)
    coarsen(r_ref, 1, 0, tmp, 0.125)
    for at in range(0, CELLS, 32):
        next_ref[pl.ds(at, 32), :] = w_ref[pl.ds(at, 32), :] * r_ref[pl.ds(at, 32), :]
    x_faces(next_ref, 0, up_ref, down_ref, 0, LAYERS[0])


def second_round(
    fk_ref, own_ref, xl_ref, xr_ref, yl_ref, yr_ref, old_ref, wide_u,
    out_hbm, resid_hbm,
    wide_b, first, second, sol_ref, up3, up2, out_ref, resid_ref, sems,
):
    widen(0, own_ref, xl_ref, xr_ref, yl_ref, yr_ref, wide_b)
    sweeps(wide_b, wide_u, first, second)
    prolong(second, up3, up2)
    correct(second, up2, old_ref, sol_ref)
    for i in range(16):
        out_ref[pl.ds(16 * i, 16), :] = sol_ref[pl.ds(48 * (i + 1), 16), :]
    copies = [pltpu.make_async_copy(out_ref, out_hbm, sems.at[0])]
    copies[0].start()

    def resid(i):
        mid, a, _ = ring_sum(sol_ref, 0, i + 1, 24, 1)
        s = mid[:16]
        return slab(fk_ref, 0, i, 16) - (slab(fk_ref, 256, i, 16) * (16.0 * s - 0.25 * a[:16]) + s)

    for half in range(2):
        loop(8 * half, 8 * half + 8, resid, lambda i, new: put(resid_ref, 0, i, 16, new))
        at = pl.ds(128 * half, 128)
        copies.append(pltpu.make_async_copy(resid_ref.at[at, :], resid_hbm.at[at, :], sems.at[1 + half]))
        copies[-1].start()
    for copy in copies:
        copy.wait()


def exchange(up, down, axis):
    size = lax.axis_size(axis)
    odd = lax.axis_index(axis) % 2 == 1
    outer = [(i, i + 1) for i in range(1, size - 1, 2)]
    outer = outer + [(j, i) for i, j in outer]
    inner = [[i, i + 1] for i in range(0, size, 2)]
    two = lax.ppermute(jnp.where(odd, up, down), axis, outer)
    one = lax.all_gather(jnp.where(odd, down, up), axis, axis_index_groups=inner)
    return jnp.where(odd, one[0], two), jnp.where(odd, two, one[1])


def shards(forcing, kappa):
    shape = forcing.shape
    f = forcing.reshape(256, LANES)
    k = kappa.reshape(256, LANES)
    fk = lax.optimization_barrier(jnp.concatenate([f, k]))
    up, down = call(z_faces, [2 * ZROWS, 2 * ZROWS], [], fk)
    zl, zr = exchange(up, down, "grp")
    raw, own, w, up, down = call(
        begin, [2 * OROWS, 2 * OROWS, OROWS, PACKED[2], PACKED[2]], [264], fk, zl, zr
    )
    xl, xr = exchange(up, down, "gx")

    def faces(fields, own, xl, xr):
        def kernel(*refs):
            y_faces(fields, *refs)

        return call(kernel, [YROWS[fields]] * 2 + [fields * XROWS] * 2, [400], own, xl, xr)

    up, down, xl, xr = faces(2, own, xl, xr)
    yl, yr = exchange(up, down, "gy")
    own, up, down, sol, wide_u = call(
        first_round,
        [OROWS, PACKED[1], PACKED[1], SOLROWS, WROWS],
        [WROWS, WROWS, WROWS, 208, 496, OROWS, 264],
        raw, own, w, xl, xr, yl, yr,
    )
    xl, xr = exchange(up, down, "gx")
    up, down, xl, xr = faces(1, own, xl, xr)
    yl, yr = exchange(up, down, "gy")
    out, resid = call(
        second_round,
        [256, 256],
        [WROWS, WROWS, WROWS, SOLROWS, 208, 496, 256, 256],
        fk, own, xl, xr, yl, yr, sol, wide_u,
        out_specs=[HBM, HBM], copies=3,
    )
    return out.reshape(shape), resid.reshape(shape)


def solution(mesh):
    placed = (P("gx", "gy", "grp"), P("gx", "gy", "grp"))
    return jax.shard_map(shards, mesh=mesh, in_specs=placed, out_specs=placed, check_vma=False)
```

```python
import jax
import jax.numpy as jnp
from jax import lax
from jax.experimental import pallas as pl
from jax.experimental.pallas import tpu as pltpu
from jax.sharding import PartitionSpec as P

F32 = jnp.float32
LANES = 128
HALO = 3
N = (16, 8, 4)
X = tuple(n + 2 * HALO for n in N)
RING = (24, 16, 16)
STEP = (1, 2, 4)
OWN = tuple(2 * n for n in N)
WIDE = tuple(2 * r for r in RING)
OBASE = (0, 512, 640)
ZWIDTH = 24
ZROWS = 48
CELLS = 672
OROWS = 704
XBASE = (0, 96, 144)
XROWS = 256
YROWS = (0, 144, 256)
PACKED = (0, 88, 160)
LAYERS = (3, 2)
UNROLL = 8
GROUPS = (3, 2)
WBASE = (0, 1056, 1504)
WROWS = 2048
SOLROWS = 18 * 48
VMEM_LIMIT = 48 * 1024 * 1024


def lanes_of(rows):
    return lax.broadcasted_iota(jnp.int32, (rows, LANES), 1)


VM = pl.BlockSpec(memory_space=pltpu.VMEM)
HBM = pl.BlockSpec(memory_space=pl.ANY)


def call(kernel, outs, scratch, *args, out_specs=None, copies=0):
    return pl.pallas_call(
        kernel,
        out_shape=[jax.ShapeDtypeStruct((rows, LANES), F32) for rows in outs],
        in_specs=[VM] * len(args),
        out_specs=out_specs or [VM] * len(outs),
        scratch_shapes=[pltpu.VMEM((rows, LANES), F32) for rows in scratch]
        + ([pltpu.SemaphoreType.DMA((copies,))] if copies else []),
        compiler_params=pltpu.CompilerParams(vmem_limit_bytes=VMEM_LIMIT),
    )(*args)


def z_faces(fk_ref, up_ref, down_ref):
    lane = lanes_of(16)
    for field in range(2):
        for tile in range(3):
            slot = (lane + LANES * tile) // ZWIDTH
            members = range(LANES * tile // ZWIDTH, (LANES * (tile + 1) - 1) // ZWIDTH + 1)
            for dst, begin_at in ((up_ref, LANES - ZWIDTH), (down_ref, 0)):
                shared = None
                for i in members:
                    value = fk_ref[pl.ds(256 * field + 16 * i, 16), :]
                    move = (ZWIDTH * i - begin_at) % LANES
                    value = pltpu.roll(value, move, 1) if move else value
                    shared = value if shared is None else jnp.where(slot == i, value, shared)
                dst[pl.ds(ZROWS * field + 16 * tile, 16), :] = shared


def z_slab(ref, field, i, begin_at):
    tile, at = divmod(ZWIDTH * i, LANES)
    value = ref[pl.ds(ZROWS * field + 16 * tile, 16), :]
    if at + ZWIDTH > LANES:
        value = jnp.where(lanes_of(16) >= at, value, ref[pl.ds(ZROWS * field + 16 * (tile + 1), 16), :])
    move = (begin_at - at) % LANES
    return pltpu.roll(value, move, 1) if move else value


def coarsen(ref, level, base, tmp, scale):
    rows = OWN[level]
    half = rows // 2
    bit = STEP[level]
    even = (lanes_of(half) // bit) % 2 == 0
    for a in range(N[level] // 2):
        at = base + OBASE[level] + 2 * a * rows
        tmp[pl.ds(a * rows, rows), :] = ref[pl.ds(at, rows), :] + ref[pl.ds(at + rows, rows), :]
    for a in range(N[level] // 2):
        pair = tmp[pl.ds(a * rows, half, 2), :] + tmp[pl.ds(a * rows + 1, half, 2), :]
        other = jnp.where(even, pltpu.roll(pair, LANES - bit, 1), pltpu.roll(pair, bit, 1))
        ref[pl.ds(base + OBASE[level + 1] + a * half, half), :] = (pair + other) * scale


def slots(vectors):
    shared = vectors[0]
    slot = (lanes_of(shared.shape[0]) + 21) // 42
    for i in (1, 2):
        shared = jnp.where(slot == i, pltpu.roll(vectors[i], 42 * i, 1), shared)
    return shared


def unslots(shared):
    return [shared] + [pltpu.roll(shared, LANES - 42 * i, 1) for i in (1, 2)]


def x_faces(own_ref, base, up_ref, down_ref, xbase, count):
    lane = lanes_of(16)
    odd = lane % 2 == 1
    turn = lanes_of(8) % 4
    for dst, end in ((up_ref, 1), (down_ref, 0)):
        at = [base + OBASE[level] + end * (N[level] - count) * OWN[level] for level in range(3)]
        to = xbase
        for i in range(count):
            dst[pl.ds(to, 16), :] = own_ref[pl.ds(at[0] + 32 * i, 16), :]
            to += 16
        shared = own_ref[pl.ds(at[0] + 16, 16), :]
        for i in range(1, count):
            moved = pltpu.roll(own_ref[pl.ds(at[0] + 32 * i + 16, 16), :], 32 * i, 1)
            shared = jnp.where((lane + 16) // 32 == i, moved, shared)
        dst[pl.ds(to, 16), :] = shared
        c = [own_ref[pl.ds(at[1] + 16 * i, 16), :] for i in range(count)]
        if count == 3:
            dst[pl.ds(to + 16, 8), :] = jnp.where(odd[:8], c[1][:8], c[0][:8])
            dst[pl.ds(to + 24, 8), :] = jnp.where(odd[:8], slots([v[8:] for v in c]), c[2][:8])
        else:
            dst[pl.ds(to + 16, 16), :] = jnp.where(odd, c[1], c[0])
        to += 32
        c = [own_ref[pl.ds(at[2] + 8 * i, 8), :] for i in range(count)]
        shared = c[0]
        for i in range(1, count):
            shared = jnp.where(turn == i, c[i], shared)
        dst[pl.ds(to, 8), :] = shared


def unpack(src, at, dst, to, count, skip):
    odd = lanes_of(16) % 2 == 1
    turn = lanes_of(8) % 4
    for level in range(3):
        rows = OWN[level]
        for i in range(HALO):
            if not skip <= i < skip + count:
                dst[pl.ds(to + XBASE[level] + rows * i, rows), :] = jnp.zeros((rows, LANES), F32)
    to1, to2, to3 = (to + XBASE[level] + skip * OWN[level] for level in range(3))
    for i in range(count):
        dst[pl.ds(to1 + 32 * i, 16), :] = src[pl.ds(at, 16), :]
        at += 16
    shared = src[pl.ds(at, 16), :]
    for i in range(count):
        dst[pl.ds(to1 + 32 * i + 16, 16), :] = pltpu.roll(shared, LANES - 32 * i, 1) if i else shared

    def two(value):
        mask = odd[: value.shape[0]]
        return jnp.where(mask, pltpu.roll(value, 1, 1), value), jnp.where(mask, value, pltpu.roll(value, LANES - 1, 1))

    first = two(src[pl.ds(at + 16, 16), :])
    if count == 3:
        for i, value in enumerate((first[0][:8], first[1][:8], first[0][8:])):
            dst[pl.ds(to2 + 16 * i, 8), :] = value
        for i, value in enumerate(unslots(first[1][8:])):
            dst[pl.ds(to2 + 16 * i + 8, 8), :] = value
    else:
        dst[pl.ds(to2, 16), :] = first[0]
        dst[pl.ds(to2 + 16, 16), :] = first[1]
    at += 32
    c = src[pl.ds(at, 8), :]
    moved = {d: pltpu.roll(c, d % LANES, 1) if d else c for d in range(1 - count, 4)}
    for i in range(count):
        value = moved[-i]
        for lane in range(1, 4):
            value = jnp.where(turn == lane, moved[lane - i], value)
        dst[pl.ds(to3 + 8 * i, 8), :] = value


def begin(fk_ref, zl_ref, zr_ref, raw_ref, own_ref, w_ref, up_ref, down_ref, tmp):
    low = lanes_of(16) < 64
    for field, ref in enumerate((fk_ref.at[pl.ds(0, 256), :], fk_ref.at[pl.ds(256, 256), :])):
        base = field * OROWS
        for i in range(16):
            from_l = z_slab(zl_ref, field, i, LANES - ZWIDTH)
            from_r = z_slab(zr_ref, field, i, 0)
            raw_ref[pl.ds(base + 32 * i, 16), :] = ref[pl.ds(16 * i, 16), :]
            raw_ref[pl.ds(base + 32 * i + 16, 16), :] = jnp.where(low, from_r, from_l)
        scale = 0.125 if field == 0 else 0.125 * 0.25
        coarsen(raw_ref, 0, base, tmp, scale)
        coarsen(raw_ref, 1, base, tmp, scale)
    for at in range(0, CELLS, 32):
        c = raw_ref[pl.ds(OROWS + at, 32), :]
        w = 0.8 / (14.0 * c + 1.0)
        w_ref[pl.ds(at, 32), :] = w
        own_ref[pl.ds(at, 32), :] = w * raw_ref[pl.ds(at, 32), :]
        own_ref[pl.ds(OROWS + at, 32), :] = 0.25 * (w * c)
    for field in range(2):
        x_faces(own_ref, field * OROWS, up_ref, down_ref, PACKED[field], LAYERS[field])


def y_parts(count):
    parts, at = [], 0
    for j in range(count):
        parts.append((at, 0, ((0, j),), None))
        at += X[0]
    for j in range(0, count, 2):
        members = tuple((h, k) for k in range(j, min(j + 2, count)) for h in range(2))
        parts.append((at, 2, members, "turns"))
        at += X[2]
    if count == 3:
        second = ((((0, 0), (0, 1)), "turns"), (((0, 2), (1, 0), (1, 1), (1, 2)), "slots"))
    else:
        second = tuple((((0, j), (1, j)), "turns") for j in range(count))
    for members, how in second:
        parts.append((at, 1, members, how))
        at += X[1]
    parts.append((at, 0, tuple((1, j) for j in range(count)), "lanes"))
    return parts


def share(vectors, how):
    if how == "slots":
        vectors, how = [vectors[0], slots(vectors[1:])], "turns"
    shared = vectors[0]
    lane = lanes_of(shared.shape[0])
    for i in range(1, len(vectors)):
        if how == "lanes":
            shared = jnp.where((lane + 16) // 32 == i, pltpu.roll(vectors[i], 32 * i, 1), shared)
        else:
            shared = jnp.where(lane % len(vectors) == i, vectors[i], shared)
    return shared


def unshare(shared, number, how):
    if how == "slots":
        first, rest = unshare(shared, 2, "turns")
        return [first] + unslots(rest)
    if how != "turns":
        return [pltpu.roll(shared, LANES - 32 * i, 1) if i else shared for i in range(number)]
    turn = lanes_of(shared.shape[0]) % number
    moved = {d: pltpu.roll(shared, d % LANES, 1) if d else shared for d in range(1 - number, number)}
    vectors = []
    for i in range(number):
        value = moved[-i]
        for lane in range(1, number):
            value = jnp.where(turn == lane, moved[lane - i], value)
        vectors.append(value)
    return vectors


def y_faces(fields, own_ref, xl_packed, xr_packed, up_ref, down_ref, xl_ref, xr_ref, rows_ref):
    spare = 0
    for field in range(fields):
        ob, xb, yb, count = field * OROWS, field * XROWS, YROWS[field], LAYERS[field]
        unpack(xl_packed, PACKED[field], xl_ref, xb, count, HALO - count)
        unpack(xr_packed, PACKED[field], xr_ref, xb, count, 0)
        for dst, first in ((up_ref, False), (down_ref, True)):
            for at, level, members, how in y_parts(count):
                n, rows, size = N[level], OWN[level], X[level]
                vectors = []
                for h, j in members:
                    row = h * n + (j if first else n - count + j)
                    to, spare = spare, spare + 24
                    if len(members) == 1:
                        ref, to = dst, yb + at
                    else:
                        ref = rows_ref
                    ref[pl.ds(to, HALO), :] = xl_ref[pl.ds(xb + XBASE[level] + row, HALO, rows), :]
                    ref[pl.ds(to + HALO, n), :] = own_ref[pl.ds(ob + OBASE[level] + row, n, rows), :]
                    ref[pl.ds(to + HALO + n, HALO), :] = xr_ref[pl.ds(xb + XBASE[level] + row, HALO, rows), :]
                    if len(members) > 1:
                        vectors.append(ref[pl.ds(to, size), :])
                if vectors:
                    dst[pl.ds(yb + at, size), :] = share(vectors, how)


def widen(field, own_ref, xl_ref, xr_ref, yl_ref, yr_ref, wide_ref):
    ob, xb, yb, count = field * OROWS, field * XROWS, YROWS[field], LAYERS[field]
    for level in range(3):
        n, ring, rows = N[level], RING[level], OWN[level]
        for i in range(X[level]):
            if i < HALO:
                ref, at = xl_ref, xb + XBASE[level] + i * rows
            elif i < HALO + n:
                ref, at = own_ref, ob + OBASE[level] + (i - HALO) * rows
            else:
                ref, at = xr_ref, xb + XBASE[level] + (i - HALO - n) * rows
            for h in range(2):
                to = WBASE[level] + i * WIDE[level] + h * ring
                wide_ref[pl.ds(to, n), :] = ref[pl.ds(at + h * n, n), :]
    for at, level, members, how in y_parts(count):
        n, ring, size = N[level], RING[level], X[level]
        for ref, start in ((yr_ref, n), (yl_ref, ring - count)):
            shared = ref[pl.ds(yb + at, size), :]
            for (h, j), vector in zip(members, unshare(shared, len(members), how)):
                wide_ref[pl.ds(WBASE[level] + h * ring + start + j, size, WIDE[level]), :] = vector


def slab(ref, base, i, rows):
    return ref[pl.ds(pl.multiple_of(base + i * rows, 8), rows), :]


def put(ref, base, i, rows, value):
    ref[pl.ds(pl.multiple_of(base + i * rows, 8), rows), :] = value


def loop(low, high, value, store):
    groups = -(-(high - low) // UNROLL)
    size = -(-(high - low) // groups)
    lead = (high - low) - (groups - 1) * size

    def group(first, count):
        values = [value(first + u) for u in range(count)]
        for u in range(count):
            store(first + u, values[u])

    def step(g, carry):
        group(low + lead + g * size, size)
        return carry

    group(low, lead)
    if groups > 1:
        lax.fori_loop(0, groups - 1, step, 0)


def ring_sum(ref, base, i, ring, step):
    rows = 2 * ring
    mid = slab(ref, base, i, rows)
    total = slab(ref, base, i - 1, rows) + slab(ref, base, i + 1, rows) + (mid + mid)
    halves = []
    for h in range(2):
        t = total[h * ring : (h + 1) * ring]
        halves.append((pltpu.roll(t, 1, 0) + pltpu.roll(t, ring - 1, 0)) + (t + t))
    lane = lanes_of(ring)
    a, b = halves
    ra, rb = pltpu.roll(a, step, 1), pltpu.roll(b, step, 1)
    sa, sb = pltpu.roll(a, LANES - step, 1), pltpu.roll(b, LANES - step, 1)
    low, high = lane < step, lane >= LANES - step
    new_a = (a + a) + (jnp.where(low, rb, ra) + jnp.where(high, sb, sa))
    new_b = (b + b) + (jnp.where(low, ra, rb) + jnp.where(high, sa, sb))
    return mid, new_a, new_b


def join(a, b):
    return jnp.concatenate([a, b], axis=0)


def sweeps(wide_b, wide_u, first, second):
    def sweep(edge, groups, src, dst):
        def value(level, i):
            rows, base = WIDE[level], WBASE[level]
            mid, a, b = ring_sum(src, base, i, RING[level], STEP[level])
            around = slab(wide_u, base, i, rows) * (join(a, b) - 8.0 * mid)
            return 0.2 * mid + slab(wide_b, base, i, rows) + around

        def group(g):
            done = []
            for level in range(3):
                high = X[level] - edge
                size = -(-(high - edge) // groups)
                start = jnp.minimum(edge + g * size, high - size)
                done += [(level, start + u, value(level, start + u)) for u in range(size)]
            for level, i, new in done:
                put(dst, WBASE[level], i, WIDE[level], new)

        pl.loop(0, groups)(group)

    sweep(1, GROUPS[0], wide_b, first)
    sweep(2, GROUPS[1], first, second)


def prolong(err, up3, up2):
    for q in range(6):
        for h in range(2):
            e3 = err[pl.ds(WBASE[2] + (q + 2) * 32 + h * 16, 16), :]
            to = q * 32 + h * 16
            up3[pl.ds(to, 5, 2), :] = e3[0:5]
            up3[pl.ds(to + 1, 5, 2), :] = e3[0:5]
            up3[pl.ds(to + 10, 4), :] = jnp.zeros((4, LANES), F32)
            up3[pl.ds(to + 14, 2), :] = jnp.broadcast_to(e3[15:16], (2, LANES))
    for a in range(10):
        for h in range(2):
            e2 = err[pl.ds(WBASE[1] + (a + 2) * 32 + h * 16, 16), :]
            e2 = e2 + up3[pl.ds(((a - 1) // 2 + 1) * 32 + h * 16, 16), :]
            to = a * 48 + h * 24
            up2[pl.ds(to, 9, 2), :] = e2[0:9]
            up2[pl.ds(to + 1, 9, 2), :] = e2[0:9]
            up2[pl.ds(to + 18, 4), :] = jnp.zeros((4, LANES), F32)
            up2[pl.ds(to + 22, 2), :] = jnp.broadcast_to(e2[15:16], (2, LANES))


def correct(err, up2, old_ref, sol_ref):
    for i in range(18):
        value = err[pl.ds((i + 2) * 48, 48), :] + up2[pl.ds(((i - 1) // 2 + 1) * 48, 48), :]
        if old_ref is not None:
            value = value + old_ref[pl.ds(i * 48, 48), :]
        sol_ref[pl.ds(i * 48, 48), :] = value


def first_round(
    raw_ref, own_ref, w_ref, xl_ref, xr_ref, yl_ref, yr_ref,
    next_ref, up_ref, down_ref, sol_ref, wide_u,
    wide_b, first, second, up3, up2, r_ref, tmp,
):
    widen(0, own_ref, xl_ref, xr_ref, yl_ref, yr_ref, wide_b)
    widen(1, own_ref, xl_ref, xr_ref, yl_ref, yr_ref, wide_u)
    sweeps(wide_b, wide_u, first, second)
    prolong(second, up3, up2)
    correct(second, up2, None, sol_ref)

    def resid(i):
        mid, a, b = ring_sum(sol_ref, 0, i + 1, 24, 1)
        halves = []
        for h, t in enumerate((a, b)):
            s = mid[h * 24 : h * 24 + 16]
            f = raw_ref[pl.ds(pl.multiple_of(i * 32 + h * 16, 16), 16), :]
            k = raw_ref[pl.ds(pl.multiple_of(OROWS + i * 32 + h * 16, 16), 16), :]
            halves.append(f - (k * (16.0 * s - 0.25 * t[:16]) + s))
        return join(*halves)

    loop(0, 16, resid, lambda i, new: put(r_ref, 0, i, 32, new))
    coarsen(r_ref, 0, 0, tmp, 0.125)
    coarsen(r_ref, 1, 0, tmp, 0.125)
    for at in range(0, CELLS, 32):
        next_ref[pl.ds(at, 32), :] = w_ref[pl.ds(at, 32), :] * r_ref[pl.ds(at, 32), :]
    x_faces(next_ref, 0, up_ref, down_ref, 0, LAYERS[0])


def second_round(
    fk_ref, own_ref, xl_ref, xr_ref, yl_ref, yr_ref, old_ref, wide_u,
    out_hbm, resid_hbm,
    wide_b, first, second, sol_ref, up3, up2, out_ref, resid_ref, sems,
):
    widen(0, own_ref, xl_ref, xr_ref, yl_ref, yr_ref, wide_b)
    sweeps(wide_b, wide_u, first, second)
    prolong(second, up3, up2)
    correct(second, up2, old_ref, sol_ref)
    for i in range(16):
        out_ref[pl.ds(16 * i, 16), :] = sol_ref[pl.ds(48 * (i + 1), 16), :]
    copies = [pltpu.make_async_copy(out_ref, out_hbm, sems.at[0])]
    copies[0].start()

    def resid(i):
        mid, a, _ = ring_sum(sol_ref, 0, i + 1, 24, 1)
        s = mid[:16]
        return slab(fk_ref, 0, i, 16) - (slab(fk_ref, 256, i, 16) * (16.0 * s - 0.25 * a[:16]) + s)

    for half in range(2):
        loop(8 * half, 8 * half + 8, resid, lambda i, new: put(resid_ref, 0, i, 16, new))
        at = pl.ds(128 * half, 128)
        copies.append(pltpu.make_async_copy(resid_ref.at[at, :], resid_hbm.at[at, :], sems.at[1 + half]))
        copies[-1].start()
    for copy in copies:
        copy.wait()


def exchange(up, down, axis):
    size = lax.axis_size(axis)
    odd = lax.axis_index(axis) % 2 == 1
    outer = [(i, i + 1) for i in range(1, size - 1, 2)]
    outer = outer + [(j, i) for i, j in outer]
    inner = [[i, i + 1] for i in range(0, size, 2)]
    two = lax.ppermute(jnp.where(odd, up, down), axis, outer)
    one = lax.all_gather(jnp.where(odd, down, up), axis, axis_index_groups=inner)
    return jnp.where(odd, one[0], two), jnp.where(odd, two, one[1])


def shards(forcing, kappa):
    shape = forcing.shape
    f = forcing.reshape(256, LANES)
    k = kappa.reshape(256, LANES)
    fk = lax.optimization_barrier(jnp.concatenate([f, k]))
    up, down = call(z_faces, [2 * ZROWS, 2 * ZROWS], [], fk)
    zl, zr = exchange(up, down, "grp")
    raw, own, w, up, down = call(
        begin, [2 * OROWS, 2 * OROWS, OROWS, PACKED[2], PACKED[2]], [264], fk, zl, zr
    )
    xl, xr = exchange(up, down, "gx")

    def faces(fields, own, xl, xr):
        def kernel(*refs):
            y_faces(fields, *refs)

        return call(kernel, [YROWS[fields]] * 2 + [fields * XROWS] * 2, [72 * 24], own, xl, xr)

    up, down, xl, xr = faces(2, own, xl, xr)
    yl, yr = exchange(up, down, "gy")
    own, up, down, sol, wide_u = call(
        first_round,
        [OROWS, PACKED[1], PACKED[1], SOLROWS, WROWS],
        [WROWS, WROWS, WROWS, 208, 496, OROWS, 264],
        raw, own, w, xl, xr, yl, yr,
    )
    xl, xr = exchange(up, down, "gx")
    up, down, xl, xr = faces(1, own, xl, xr)
    yl, yr = exchange(up, down, "gy")
    out, resid = call(
        second_round,
        [256, 256],
        [WROWS, WROWS, WROWS, SOLROWS, 208, 496, 256, 256],
        fk, own, xl, xr, yl, yr, sol, wide_u,
        out_specs=[HBM, HBM], copies=3,
    )
    return out.reshape(shape), resid.reshape(shape)


def solution(mesh):
    placed = (P("gx", "gy", "grp"), P("gx", "gy", "grp"))
    return jax.shard_map(shards, mesh=mesh, in_specs=placed, out_specs=placed, check_vma=False)
```
